32 devices in a mesh: grp: 4 (over y, core), rep: 8 (over z, x).
Axes of the slice: x: 2, y: 2, z: 4, core: 2. Of those that a mesh axis runs over, the one named last changes fastest.
Arguments:
- tokens: bfloat16 [32768, 768], P(('grp', 'rep')), may hold values from -6 to 6
- out_grad: bfloat16 [32768, 768], P(('grp', 'rep')), may hold values from -6 to 6
- destination: int32 [256], P(('grp', 'rep')), may hold values from 0 to 31, as said below
- seq_first: int32 [256], P(('grp', 'rep')), may hold values from 0 to 7, as said below
- valid_count: int32 [256], P(('grp', 'rep')), may hold values from 0 to 128, as said below
- first_gain: float32 [768], replicated, may hold values from 0.5 to 1.5
- first_bias: float32 [768], replicated, may hold values from -1.8 to 1.8
- attn_weight: bfloat16 [768, 2304], replicated, may hold values from -0.3125 to 0.3125
- attn_bias: float32 [1536], replicated, may hold values from -1.8 to 1.8
- mix_weight: bfloat16 [768, 768], replicated, may hold values from -0.875 to 0.875
- mix_bias: float32 [768], replicated, may hold values from -1.8 to 1.8
- second_gain: float32 [768], replicated, may hold values from 0.5 to 1.5
- second_bias: float32 [768], replicated, may hold values from -1.8 to 1.8
- up_weight: bfloat16 [768, 3072], replicated, may hold values from -0.21875 to 0.21875
- up_bias: float32 [3072], replicated, may hold values from -1.8 to 1.8
- down_weight: bfloat16 [3072, 768], replicated, may hold values from -0.15625 to 0.15625
- down_bias: float32 [768], replicated, may hold values from -1.8 to 1.8
Outputs:
- mixed: bfloat16 [32768, 768], P(('grp', 'rep'))
- tokens_grad: bfloat16 [32768, 768], P(('grp', 'rep'))
- first_gain_grad: float32 [768], P('rep')
- first_bias_grad: float32 [768], P('rep')
- attn_weight_grad: float32 [768, 2304], P('rep')
- attn_bias_grad: float32 [1536], P('rep')
- mix_weight_grad: float32 [768, 768], P('rep')
- mix_bias_grad: float32 [768], P('rep')
- second_gain_grad: float32 [768], P('rep')
- second_bias_grad: float32 [768], P('rep')
- up_weight_grad: float32 [768, 3072], P('rep')
- up_bias_grad: float32 [3072], P('rep')
- down_weight_grad: float32 [3072, 768], P('rep')
- down_bias_grad: float32 [768], P('rep')
The draws below stay inside these ranges and needn't reach their ends.
Inputs may be any that keep to these rules, and one draw needn't show every extreme that they name: `destination`: an entry g * 8 + c names device g along grp of the same group and block slot c there. Within a group every slot of every device is named exactly once, and one device names one device for at most 4 of its blocks, exactly 4 for some pair in every draw. `seq_first`: A sequence occupies consecutive blocks of one device, all full but its last; it has 80 to 1024 tokens, and some device holds one of 1024 tokens. A block with no live token is a sequence of its own. `valid_count`: blocks without live tokens come after all sequences of their device.
All inputs are finite; a program needn't handle non-finite values.
Results may differ from the reference program's by a relative error of at most 0.019.
Values may be sent and summed in bfloat16 or wider, within the bound.
No kernel may reach another device: no remote copies, remote signals or barrier semaphores. Data moves between devices by JAX's collectives and lax.ppermute only.
A program may use at most 256 MiB of HBM per device.

```python
import jax
import jax.numpy as jnp
from jax import lax

D = 768
HEADS = 12
HEAD_DIM = 64
FF = 3072
NB = 8
BL = 128
MIN_LEN = 80
TOKENS = 32768
N_GRP = 4
N_REP = 8


def block_layout(key):
    devices = N_GRP * N_REP
    index = jnp.arange(devices, dtype=jnp.int32)
    fewest = (3 * NB + 7) // 8
    used = fewest + (NB - fewest) * index // (devices - 1)
    cut_key, fill_key = jax.random.split(key)
    cuts = jax.random.randint(cut_key, (devices, NB), 0, 2)
    blocks = jnp.arange(NB, dtype=jnp.int32)
    final = (index == devices - 1)[:, None]
    unused = blocks[None, :] >= used[:, None]
    opens = (blocks[None, :] == 0) | (cuts == 1) & jnp.logical_not(final) | unused
    first = lax.cummax(jnp.where(opens, blocks[None, :], 0), axis=1)
    later = opens[:, None, :] & (blocks[None, None, :] > blocks[None, :, None])
    following = jnp.min(jnp.where(later, blocks[None, None, :], NB), axis=2)
    closing = following == blocks[None, :] + 1
    single = following - first == 1
    least = jnp.where(single, MIN_LEN, 1)
    drawn = jax.random.randint(fill_key, (devices, NB), least, BL + 1)
    tail = jnp.where(final, BL, drawn)
    counts = jnp.where(unused, 0, jnp.where(closing, tail, BL))
    return (first.reshape(-1).astype(jnp.int32), counts.reshape(-1).astype(jnp.int32))


def draw_seq_first(key, part):
    shared = block_layout(key)
    return shared[0]


def draw_valid_count(key, part):
    shared = block_layout(key)
    return shared[1]


def draw_destination(key, part):
    key = jax.random.fold_in(key, 5)
    share = NB // N_GRP
    keys = jax.random.split(key, 4)
    first_peer = jax.random.randint(keys[0], (N_REP,), 0, N_GRP)
    stride = jax.random.randint(keys[1], (N_REP,), 1, N_GRP)
    second_peer = (first_peer + stride) % N_GRP
    peers = jnp.arange(N_GRP, dtype=jnp.int32)
    counts = share + share * (peers[None, :] == first_peer[:, None]).astype(jnp.int32) - share * (peers[None, :] == second_peer[:, None]).astype(jnp.int32)
    ends = jnp.cumsum(counts, axis=1)
    send_keys = jax.random.split(keys[2], N_GRP * N_REP)
    order = jax.vmap(lambda k: jax.random.permutation(k, NB))(send_keys).reshape(N_GRP, N_REP, NB)
    slot_keys = jax.random.split(keys[3], N_GRP * N_REP)
    slot_perm = jax.vmap(lambda k: jax.random.permutation(k, NB))(slot_keys).reshape(N_GRP, N_REP, NB)
    offset = jnp.sum((ends[None, :, None, :] <= order[:, :, :, None]).astype(jnp.int32), axis=-1)
    target = (jnp.arange(N_GRP, dtype=jnp.int32)[:, None, None] + offset) % N_GRP
    reps = jnp.broadcast_to(jnp.arange(N_REP, dtype=jnp.int32)[None, :, None], target.shape)
    slot = slot_perm[target, reps, order]
    return (target * NB + slot).reshape(-1).astype(jnp.int32)


def shard_levels(own_key, shape, cuts, smallest, largest):
    def one(dim, shards_of):
        steps = jax.random.uniform(jax.random.fold_in(jax.random.fold_in(own_key, 6), dim), (shards_of,), jnp.float32, smallest / len(cuts), largest / len(cuts))
        return jnp.repeat(jnp.exp(steps), shape[dim] // shards_of).reshape((-1,) + (1,) * (len(shape) - dim - 1))

    level = one(*cuts[0])
    for cut in cuts[1:]:
        level = level * one(*cut)
    return level


def scatter_about(key, shape, scale, limit, cuts=(), kind=jnp.bfloat16):
    level = shard_levels(key, shape, cuts, -0.22, 0.18) if cuts else 1.0
    result = jax.random.normal(key, shape, jnp.float32) * scale * level
    return jnp.minimum(jnp.maximum(result, -limit), limit).astype(kind)


def setup_inputs(seed: int = 0) -> dict:
    splits = jax.random.split(jax.random.key(seed), 18)
    return {
        "tokens": scatter_about(splits[0], (TOKENS, D), 1.0, 6.0, ((0, 32),)),
        "out_grad": scatter_about(splits[1], (TOKENS, D), 1.0, 6.0, ((0, 32),)),
        "destination": draw_destination(jax.random.fold_in(splits[17], 71), 0),
        "seq_first": draw_seq_first(jax.random.fold_in(splits[17], 71), 0),
        "valid_count": draw_valid_count(jax.random.fold_in(splits[17], 71), 0),
        "first_gain": jnp.clip(1.0 + 0.1 * jax.random.normal(splits[5], (D,), jnp.float32), 0.5, 1.5),
        "first_bias": scatter_about(splits[6], (D,), 0.3, 1.8, (), jnp.float32),
        "attn_weight": scatter_about(splits[7], (D, 3 * D), (D // 2) ** -0.5, 0.3125),
        "attn_bias": scatter_about(splits[8], (2 * D,), 0.3, 1.8, (), jnp.float32),
        "mix_weight": scatter_about(splits[9], (D, D), (D // 16) ** -0.5, 0.875),
        "mix_bias": scatter_about(splits[10], (D,), 0.3, 1.8, (), jnp.float32),
        "second_gain": jnp.clip(1.0 + 0.1 * jax.random.normal(splits[11], (D,), jnp.float32), 0.5, 1.5),
        "second_bias": scatter_about(splits[12], (D,), 0.3, 1.8, (), jnp.float32),
        "up_weight": scatter_about(splits[13], (D, FF), D ** -0.5, 0.21875),
        "up_bias": scatter_about(splits[14], (FF,), 0.3, 1.8, (), jnp.float32),
        "down_weight": scatter_about(splits[15], (FF, D), (FF // 2) ** -0.5, 0.15625),
        "down_bias": scatter_about(splits[16], (D,), 0.3, 1.8, (), jnp.float32),
    }


HIGH = lax.Precision.HIGHEST
EPSILON = 1e-05
GELU_COEFF = 0.7978845608028654

@jax.custom_vjp
def low(v):
    return lax.optimization_barrier(v.astype(jnp.bfloat16)).astype(jnp.float32)

@jax.custom_vjp
def low_back(v):
    return v

def low_keep(v):
    return (low(v), None)

def low_pass(kept, grad):
    return (grad,)

def back_keep(v):
    return (v, None)

def back_low(kept, grad):
    return (low(grad),)
low.defvjp(low_keep, low_pass)
low_back.defvjp(back_keep, back_low)

def both_ways(value):
    return low_back(low(value))

def layer_norm(rows, gain, shift):
    center = lax.optimization_barrier(jnp.mean(rows, axis=-1, keepdims=True))
    centered = rows - center
    spread = lax.optimization_barrier(jnp.mean(centered * centered, axis=-1, keepdims=True))
    return centered * lax.rsqrt(spread + EPSILON) * gain + shift

def gelu_tanh(value):
    inner = GELU_COEFF * (value + 0.044715 * value * value * value)
    return 0.5 * value * (1.0 + jnp.tanh(inner))

def attend(pieces):
    query, key, value, seq_ids, live = pieces
    order = jnp.arange(query.shape[0], dtype=jnp.int32)
    allowed = (seq_ids[:, None] == seq_ids[None, :]) & live[None, :] & (order[None, :] <= order[:, None])
    scores = low_back(jnp.einsum('qhd,khd->hqk', query, key, precision=HIGH) * HEAD_DIM ** (-0.5))
    masked = jnp.where(allowed[None], scores, -1e+30)
    top = lax.optimization_barrier(jnp.max(masked, axis=-1, keepdims=True))
    weights = jnp.exp(masked - top)
    probs = low(weights / lax.optimization_barrier(jnp.sum(weights, axis=-1, keepdims=True)))
    return jnp.einsum('hqk,khd->qhd', probs, value, precision=HIGH)

def forward(tokens, first_gain, first_bias, attn_weight, attn_bias, mix_weight, mix_bias, second_gain, second_bias, up_weight, up_bias, down_weight, down_bias, inverse, forward_map, seq_ids, live):
    regrouped = low_back(tokens.reshape(-1, BL, D)[inverse].reshape(-1, D))
    normed = low(layer_norm(regrouped, first_gain, first_bias))
    packed = jnp.dot(normed, attn_weight, precision=HIGH)
    query = both_ways(packed[:, :D] + attn_bias[:D])
    key = both_ways(packed[:, D:2 * D])
    value = both_ways(packed[:, 2 * D:] + attn_bias[D:])
    shape_four = (-1, NB * BL, HEADS, HEAD_DIM)
    heads_out = lax.map(jax.checkpoint(attend), (query.reshape(shape_four), key.reshape(shape_four), value.reshape(shape_four), seq_ids, live))
    context = both_ways(heads_out.reshape(-1, D))
    live_rows = live.reshape(-1).astype(jnp.float32)[:, None]
    branch = both_ways((jnp.dot(context, mix_weight, precision=HIGH) + mix_bias) * live_rows)
    returned = branch.reshape(-1, BL, D)[forward_map].reshape(-1, D)
    hidden = tokens + returned
    second = low(layer_norm(hidden, second_gain, second_bias))
    upper = low_back(jnp.dot(second, up_weight, precision=HIGH) + up_bias)
    active = low(gelu_tanh(upper))
    return hidden + jnp.dot(active, down_weight, precision=HIGH) + down_bias

def reference(tokens, out_grad, destination, seq_first, valid_count, first_gain, first_bias, attn_weight, attn_bias, mix_weight, mix_bias, second_gain, second_bias, up_weight, up_bias, down_weight, down_bias):
    block_ids = jnp.arange(destination.shape[0], dtype=jnp.int32)
    rep_of = block_ids // NB % N_REP
    forward_map = ((destination // NB * N_REP + rep_of) * NB + destination % NB).astype(jnp.int32)
    inverse = jnp.zeros_like(destination).at[forward_map].set(block_ids).astype(jnp.int32)
    offsets = jnp.arange(BL, dtype=jnp.int32)
    seq_ids = jnp.repeat(seq_first, BL).reshape(-1, NB * BL)
    live = (offsets[None, :] < valid_count[:, None]).reshape(-1, NB * BL)

    def layer(tokens_f, g_one, b_one, w_attn, b_attn, w_mix, b_mix, g_two, b_two, w_up, b_up, w_down, b_down):
        return forward(tokens_f, g_one, b_one, w_attn, b_attn, w_mix, b_mix, g_two, b_two, w_up, b_up, w_down, b_down, inverse, forward_map, seq_ids, live)
    output, pull = jax.vjp(layer, tokens.astype(jnp.float32), first_gain.astype(jnp.float32), first_bias.astype(jnp.float32), attn_weight.astype(jnp.float32), attn_bias.astype(jnp.float32), mix_weight.astype(jnp.float32), mix_bias.astype(jnp.float32), second_gain.astype(jnp.float32), second_bias.astype(jnp.float32), up_weight.astype(jnp.float32), up_bias.astype(jnp.float32), down_weight.astype(jnp.float32), down_bias.astype(jnp.float32))
    grads = pull(out_grad.astype(jnp.float32))
    scale = 1.0 / jnp.sum(valid_count.astype(jnp.float32))
    return (output.astype(jnp.bfloat16), grads[0].astype(jnp.bfloat16), grads[1] * scale, grads[2] * scale, grads[3] * scale, grads[4] * scale, grads[5] * scale, grads[6] * scale, grads[7] * scale, grads[8] * scale, grads[9] * scale, grads[10] * scale, grads[11] * scale, grads[12] * scale)
```

```python
import functools

import jax
import jax.numpy as jnp
from jax import lax
from jax.experimental import pallas as pl
from jax.experimental.pallas import tpu as pltpu
from jax.sharding import PartitionSpec as P

F32 = jnp.float32
BF = jnp.bfloat16
HEAD_DIM = 64
NB = 8
BL = 128
LANES = 128
CW = 384
EXTRA = 16
EPSILON = 1e-05
C0 = 0.7978845608028654
C1 = 0.044715
NEG = -1e30
VMEM = 56 * 2**20
NT = (((1,), (1,)), ((), ()))
TN = (((0,), (0,)), ((), ()))


def dot(a, b):
    return jnp.dot(a, b, preferred_element_type=F32)


def dot_nt(a, b):
    return lax.dot_general(a, b, NT, preferred_element_type=F32)


def dot_tn(a, b):
    return lax.dot_general(a, b, TN, preferred_element_type=F32)


def normalise(rows):
    width = rows.shape[1]
    centered = rows - jnp.sum(rows, axis=1, keepdims=True) * (1.0 / width)
    rstd = lax.rsqrt(
        jnp.sum(centered * centered, axis=1, keepdims=True) * (1.0 / width) + EPSILON
    )
    return centered * rstd, rstd


def norm_back(grad, gain, xhat, rstd):
    width = grad.shape[1]
    dx = grad * gain
    mean_one = jnp.sum(dx, axis=1, keepdims=True) * (1.0 / width)
    mean_two = jnp.sum(dx * xhat, axis=1, keepdims=True) * (1.0 / width)
    return rstd * (dx - mean_one - xhat * mean_two)


def colsum(rows):
    return jnp.sum(rows, axis=0, keepdims=True)


def params(**more):
    return pltpu.CompilerParams(vmem_limit_bytes=VMEM, **more)


def swap(value, axis, size, bit):
    return lax.ppermute(value, axis, [(i, i ^ (1 << bit)) for i in range(size)])


def share(value, size):
    found = [value]
    order = [0]
    bits = size.bit_length() - 1
    for bit in reversed(range(bits)):
        found = found + [swap(v, "grp", size, bit) for v in found]
        order = order + [o | (1 << bit) for o in order]
    return [v for _, v in sorted(zip(order, found), key=lambda pair: pair[0])]


def start_gather(pick, place, sources, target, sems):
    for c in range(NB):
        for k, source in enumerate(sources):

            @pl.when(pick[c] == k)
            def _(c=c, source=source):
                begin = pl.multiple_of(place[c] * BL, BL)
                pltpu.make_async_copy(
                    source.at[pl.ds(begin, BL)], target.at[pl.ds(c * BL, BL)], sems.at[c]
                ).start()


def wait_gather(c, sources, target, sems):
    pltpu.make_async_copy(
        sources[0].at[pl.ds(0, BL)], target.at[pl.ds(c * BL, BL)], sems.at[c]
    ).wait()


def collect_kernel(pick, place, *refs, n):
    sources, target, sems = refs[:n], refs[n], refs[n + 1]
    start_gather(pick, place, sources, target, sems)
    for c in range(NB):
        wait_gather(c, sources, target, sems)


def collect(pick, place, sources):
    n = len(sources)
    return pl.pallas_call(
        functools.partial(collect_kernel, n=n),
        grid_spec=pltpu.PrefetchScalarGridSpec(
            num_scalar_prefetch=2,
            grid=(1,),
            in_specs=[pl.BlockSpec(memory_space=pl.ANY)] * n,
            out_specs=pl.BlockSpec(memory_space=pl.ANY),
            scratch_shapes=[pltpu.SemaphoreType.DMA((NB,))],
        ),
        out_shape=jax.ShapeDtypeStruct(sources[0].shape, sources[0].dtype),
        compiler_params=params(),
        name="collect",
    )(pick, place, *sources)


def project_kernel(pick, place, *refs, n, tile):
    sources = refs[:n]
    gain, shift, weight, bias, x_out, normed_out, qkv_out, x_buf, sems = refs[n:]
    step = pl.program_id(0)
    per = tile // BL

    @pl.when(step == 0)
    def _():
        start_gather(pick, place, sources, x_buf, sems)

    for c in range(NB):

        @pl.when(step == c // per)
        def _(c=c):
            wait_gather(c, sources, x_buf, sems)

    x = x_buf[pl.ds(pl.multiple_of(step * tile, tile), tile), :]
    x_out[...] = x
    xhat, _ = normalise(x.astype(F32))
    normed = (xhat * gain[...] + shift[...]).astype(BF)
    normed_out[...] = normed
    width = x.shape[1]
    for i in range(3):
        cols = slice(i * width, (i + 1) * width)
        qkv_out[:, cols] = (dot(normed, weight[:, cols]) + bias[:, cols]).astype(BF)


def project(pick, place, sources, gain, shift, weight, bias, tile=256):
    n = len(sources)
    rows, width = sources[0].shape
    row = lambda w: pl.BlockSpec((tile, w), lambda i, *_: (i, 0))
    full = lambda a: pl.BlockSpec(a.shape, lambda i, *_: (0, 0))
    small = (gain, shift, weight, bias)
    return pl.pallas_call(
        functools.partial(project_kernel, n=n, tile=tile),
        grid_spec=pltpu.PrefetchScalarGridSpec(
            num_scalar_prefetch=2,
            grid=(rows // tile,),
            in_specs=[pl.BlockSpec(memory_space=pl.ANY)] * n + [full(a) for a in small],
            out_specs=[row(width), row(width), row(3 * width)],
            scratch_shapes=[pltpu.VMEM((rows, width), BF), pltpu.SemaphoreType.DMA((NB,))],
        ),
        out_shape=[
            jax.ShapeDtypeStruct((rows, width), BF),
            jax.ShapeDtypeStruct((rows, width), BF),
            jax.ShapeDtypeStruct((rows, 3 * width), BF),
        ],
        compiler_params=params(),
        cost_estimate=pl.CostEstimate(
            flops=6 * rows * width * width, bytes_accessed=16 * 2**20, transcendentals=0
        ),
        name="project",
    )(pick, place, *sources, *small)


def head_masks(rows):
    lane = lax.broadcasted_iota(jnp.int32, (rows, LANES), 1)
    return [lane < HEAD_DIM, lane >= HEAD_DIM]


def attention_kernel(first, count, q_ref, k_ref, v_ref, ctx_ref, p_ref, *, rows, tile):
    q = q_ref[...]
    k = k_ref[...]
    v = v_ref[...]
    masks = head_masks(rows)
    zero = jnp.zeros((), BF)
    scale = jnp.asarray(HEAD_DIM**-0.5, BF)
    key_pos = lax.broadcasted_iota(jnp.int32, (BL, BL), 1)
    causal = key_pos <= lax.broadcasted_iota(jnp.int32, (BL, BL), 0)
    value_mean = colsum(v.astype(F32)) * (1.0 / rows)
    queries = [jnp.where(m, q, zero) * scale for m in masks]
    values = [jnp.where(m, v, zero) for m in masks]
    for i in range(rows // tile):
        keys = k[: (i + 1) * tile]
        scores = [dot_nt(query[i * tile : (i + 1) * tile], keys) for query in queries]
        for c in range(i * tile // BL, (i + 1) * tile // BL):
            begin = c * BL - i * tile
            allowed = causal & (key_pos < count[c])
            total = None
            for h in range(2):
                strip = scores[h][begin : begin + BL]
                parts = []
                for j in range(c):
                    other = jnp.where(j >= first[c], jnp.float32(0), jnp.float32(NEG))
                    parts.append(strip[:, j * BL : (j + 1) * BL] + other)
                parts.append(jnp.where(allowed, strip[:, c * BL : (c + 1) * BL], NEG))
                top = functools.reduce(jnp.maximum, parts)
                top = jnp.max(top, axis=1, keepdims=True)
                parts = [jnp.exp(part - top) for part in parts]
                inverse = 1.0 / jnp.sum(
                    functools.reduce(jnp.add, parts), axis=1, keepdims=True
                )
                parts = [(part * inverse).astype(BF) for part in parts]
                for j, part in enumerate(parts):
                    p_ref[h, c * BL : (c + 1) * BL, j * BL : (j + 1) * BL] = part
                probs = jnp.concatenate(parts, axis=1) if c else parts[0]
                out = dot(probs, values[h][: (c + 1) * BL])
                total = out if total is None else total + out
            total = jnp.where(count[c] == 0, jnp.broadcast_to(value_mean, total.shape), total)
            ctx_ref[c * BL : (c + 1) * BL, :] = total.astype(BF)


def attention(first, count, qkv, tile=512):
    rows = qkv.shape[0]
    width = qkv.shape[1] // 3
    pairs = width // LANES
    col = lambda off: pl.BlockSpec((rows, LANES), lambda i, *_: (0, i + off))
    return pl.pallas_call(
        functools.partial(attention_kernel, rows=rows, tile=tile),
        grid_spec=pltpu.PrefetchScalarGridSpec(
            num_scalar_prefetch=2,
            grid=(pairs,),
            in_specs=[col(0), col(pairs), col(2 * pairs)],
            out_specs=[col(0), pl.BlockSpec((2, rows, rows), lambda i, *_: (i, 0, 0))],
        ),
        out_shape=[
            jax.ShapeDtypeStruct((rows, width), BF),
            jax.ShapeDtypeStruct((2 * pairs, rows, rows), BF),
        ],
        compiler_params=params(),
        cost_estimate=pl.CostEstimate(
            flops=16 * rows * rows * width, bytes_accessed=32 * 2**20, transcendentals=0
        ),
        name="attention",
    )(first, count, qkv, qkv, qkv)


def attention_back_kernel(
    core, q_ref, k_ref, v_ref, o_ref, g_ref, p_ref, dq_ref, dk_ref, dv_ref, ds_ref, *, rows, tile
):
    q = q_ref[...]
    k = k_ref[...]
    v = v_ref[...]
    grad = g_ref[...]
    masks = head_masks(rows)
    zero = jnp.zeros((), BF)
    scale = jnp.asarray(HEAD_DIM**-0.5, BF)
    product = grad.astype(F32) * o_ref[...].astype(F32)
    grads = [jnp.where(m, grad, zero) for m in masks]
    keys = [jnp.where(m, k, zero) * scale for m in masks]
    queries = [jnp.where(m, q, zero) * scale for m in masks]
    inner = [jnp.sum(jnp.where(m, product, 0.0), axis=1, keepdims=True) for m in masks]
    for i in range(rows // tile):
        cut = slice(i * tile, (i + 1) * tile)
        dprobs = [dot_nt(g[cut], v[: (i + 1) * tile]) for g in grads]
        for c in range(i * tile // BL, (i + 1) * tile // BL):
            begin = c * BL - i * tile
            own = slice(c * BL, (c + 1) * BL)
            width = (c + 1) * BL
            total = None
            for h in range(2):
                probs = p_ref[h, own, :width].astype(F32)
                ds = (probs * (dprobs[h][begin : begin + BL, :width] - inner[h][own])).astype(BF)
                ds_ref[h, own, :width] = ds
                out = dot(ds, keys[h][:width])
                total = out if total is None else total + out
            dq_ref[own, :] = total.astype(BF)
    for c in range(rows // BL):
        own = slice(c * BL, (c + 1) * BL)
        dk = dv = None
        for h in range(2):
            one = dot_tn(ds_ref[h, c * BL :, own], queries[h][c * BL :])
            two = dot_tn(p_ref[h, c * BL :, own], grads[h][c * BL :])
            dk = one if dk is None else dk + one
            dv = two if dv is None else dv + two
        dk_ref[own, :] = dk.astype(BF)
        dv_ref[own, :] = dv.astype(BF)


def attention_back(core, qkv, ctx, grad, probs, tile=512):
    rows = qkv.shape[0]
    width = qkv.shape[1] // 3
    pairs = width // LANES
    half = pairs // 2

    def pair(i, core):
        return jnp.where(i < half, 2 * i + 1 - core[0], 2 * (i - half) + core[0])

    col = lambda off: pl.BlockSpec((rows, LANES), lambda i, core: (0, pair(i, core) + off))
    out = jax.ShapeDtypeStruct((rows, width), BF)
    return pl.pallas_call(
        functools.partial(attention_back_kernel, rows=rows, tile=tile),
        grid_spec=pltpu.PrefetchScalarGridSpec(
            num_scalar_prefetch=1,
            grid=(pairs,),
            in_specs=[
                col(0),
                col(pairs),
                col(2 * pairs),
                col(0),
                col(0),
                pl.BlockSpec((2, rows, rows), lambda i, core: (pair(i, core), 0, 0)),
            ],
            out_specs=[col(0)] * 3,
            scratch_shapes=[pltpu.VMEM((2, rows, rows), BF)],
        ),
        out_shape=[out] * 3,
        compiler_params=params(),
        cost_estimate=pl.CostEstimate(
            flops=20 * rows * rows * width, bytes_accessed=36 * 2**20, transcendentals=0
        ),
        name="attention_back",
    )(core, qkv, qkv, qkv, ctx, grad, probs)


def feed_kernel(pick, place, count, *refs, n, tile, ftile):
    sources = refs[:n]
    (x_ref, ctx_ref, mixw, mixb, gain, shift, upw, upb, downw, downb) = refs[n : n + 10]
    (
        mixed_ref,
        second_ref,
        act_ref,
        gu_ref,
        gh_ref,
        pre_ref,
        dctx_ref,
        og_ref,
        sums_ref,
        og_buf,
        sems,
    ) = refs[n + 10 :]
    step = pl.program_id(0)
    per = tile // BL
    width = x_ref.shape[1]
    ff = upw.shape[1]

    @pl.when(step == 0)
    def _():
        start_gather(pick, place, sources, og_buf, sems)
        sums_ref[...] = jnp.zeros_like(sums_ref)

    for c in range(NB):

        @pl.when(step == c // per)
        def _(c=c):
            wait_gather(c, sources, og_buf, sems)

    row = lax.broadcasted_iota(jnp.int32, (tile, 1), 0)
    live = jnp.zeros((tile, 1), F32)
    for b in range(per):
        filled = count[step * per + b]
        live = jnp.where((row >= b * BL) & (row < b * BL + filled), 1.0, live)
    branch = ((dot(ctx_ref[...], mixw[...]) + mixb[...]) * live).astype(BF).astype(F32)
    hidden = x_ref[...].astype(F32) + branch
    xhat, rstd = normalise(hidden)
    second = (xhat * gain[...] + shift[...]).astype(BF)
    second_ref[...] = second
    og = og_buf[pl.ds(pl.multiple_of(step * tile, tile), tile), :]
    og_ref[...] = og
    mixed = hidden + downb[...]
    gs = jnp.zeros((tile, width), F32)
    for f in range(ff // ftile):
        cols = slice(f * ftile, (f + 1) * ftile)
        v = dot(second, upw[:, cols]) + upb[:, cols]
        da = dot_nt(og, downw[cols, :])
        square = v * v
        half = 0.5 + 0.5 * jnp.tanh(v * (C0 + (C0 * C1) * square))
        act = (v * half).astype(BF)
        act_ref[:, cols] = act
        mixed = mixed + dot(act, downw[cols, :])
        slope = half + v * (half - half * half) * (2 * C0 + (6 * C0 * C1) * square)
        gu = (da * slope).astype(BF)
        gu_ref[:, cols] = gu
        sums_ref[0:1, cols] += colsum(gu.astype(F32))
        gs = gs + dot_nt(gu, upw[:, cols])
    mixed_ref[...] = mixed.astype(BF)
    og = og.astype(F32)
    gh = og + norm_back(gs, gain[...], xhat, rstd)
    gh_ref[...] = gh
    pre = gh.astype(BF).astype(F32) * live
    sums_ref[1:2, :width] += colsum(og)
    sums_ref[2:3, :width] += colsum(gs * xhat)
    sums_ref[3:4, :width] += colsum(gs)
    sums_ref[4:5, :width] += colsum(pre)
    pre = pre.astype(BF)
    pre_ref[...] = pre
    dctx_ref[...] = dot_nt(pre, mixw[...]).astype(BF)


def feed(pick, place, count, sources, x, ctx, weights, tile=256, ftile=512):
    n = len(sources)
    rows, width = x.shape
    ff = weights[4].shape[1]
    row = lambda w: pl.BlockSpec((tile, w), lambda i, *_: (i, 0))
    full = lambda a: pl.BlockSpec(a.shape, lambda i, *_: (0, 0))
    bf = lambda w: jax.ShapeDtypeStruct((rows, w), BF)
    return pl.pallas_call(
        functools.partial(feed_kernel, n=n, tile=tile, ftile=ftile),
        grid_spec=pltpu.PrefetchScalarGridSpec(
            num_scalar_prefetch=3,
            grid=(rows // tile,),
            in_specs=[pl.BlockSpec(memory_space=pl.ANY)] * n
            + [row(width), row(width)]
            + [full(a) for a in weights],
            out_specs=[row(width), row(width), row(ff), row(ff)]
            + [row(width)] * 4
            + [pl.BlockSpec((8, ff), lambda i, *_: (0, 0))],
            scratch_shapes=[pltpu.VMEM((rows, width), BF), pltpu.SemaphoreType.DMA((NB,))],
        ),
        out_shape=[
            bf(width),
            bf(width),
            bf(ff),
            bf(ff),
            jax.ShapeDtypeStruct((rows, width), F32),
            bf(width),
            bf(width),
            bf(width),
            jax.ShapeDtypeStruct((8, ff), F32),
        ],
        compiler_params=params(),
        cost_estimate=pl.CostEstimate(
            flops=8 * rows * width * ff, bytes_accessed=40 * 2**20, transcendentals=0
        ),
        name="feed",
    )(pick, place, count, *sources, x, ctx, *weights)


def project_back_kernel(
    x_ref, dq_ref, dk_ref, dv_ref, gh_ref, weight, gain, tg_ref, sums_ref
):
    step = pl.program_id(0)
    width = x_ref.shape[1]

    @pl.when(step == 0)
    def _():
        sums_ref[...] = jnp.zeros_like(sums_ref)

    xhat, rstd = normalise(x_ref[...].astype(F32))
    grad = None
    for i, ref in enumerate((dq_ref, dk_ref, dv_ref)):
        part = dot_nt(ref[...], weight[:, i * width : (i + 1) * width])
        grad = part if grad is None else grad + part
    back = norm_back(grad, gain[...], xhat, rstd).astype(BF).astype(F32)
    tg_ref[...] = (gh_ref[...] + back).astype(BF)
    sums_ref[0:1, :] += colsum(grad * xhat)
    sums_ref[1:2, :] += colsum(grad)
    sums_ref[2:3, :] += colsum(dq_ref[...].astype(F32))
    sums_ref[3:4, :] += colsum(dv_ref[...].astype(F32))


def project_back(x, dq, dk, dv, gh, weight, gain, tile=256):
    rows, width = x.shape
    row = pl.BlockSpec((tile, width), lambda i: (i, 0))
    full = lambda a: pl.BlockSpec(a.shape, lambda i: (0, 0))
    return pl.pallas_call(
        project_back_kernel,
        grid=(rows // tile,),
        in_specs=[row] * 5 + [full(weight), full(gain)],
        out_specs=[row, pl.BlockSpec((8, width), lambda i: (0, 0))],
        out_shape=[
            jax.ShapeDtypeStruct((rows, width), BF),
            jax.ShapeDtypeStruct((8, width), F32),
        ],
        compiler_params=params(),
        cost_estimate=pl.CostEstimate(
            flops=6 * rows * width * width, bytes_accessed=16 * 2**20, transcendentals=0
        ),
        name="project_back",
    )(x, dq, dk, dv, gh, weight, gain)


def split_by(bit, value, keep_ref, send_ref, where):
    for i in range(value.shape[0] // 2):
        even, odd = value[2 * i], value[2 * i + 1]
        keep_ref[(i,) + where] = jnp.where(bit == 0, even, odd).astype(BF)
        send_ref[(i,) + where] = jnp.where(bit == 0, odd, even).astype(BF)


def sums_kernel(sel, *refs, plan, parts, keeps):
    n_in = plan["inputs"]
    ins = refs[:n_in]
    rest = refs[n_in:]
    step = pl.program_id(0)
    if keeps:
        got, extra, keep_ref, send_ref = rest
    else:
        (out_ref,) = rest
    for s, (left, rights, at, size) in enumerate(plan["steps"]):

        @pl.when(step == s)
        def _(left=left, rights=rights, at=at, size=size):
            right = [ins[r][...] for r in rights]
            right = jnp.concatenate(right, axis=1) if len(right) > 1 else right[0]
            product = dot_tn(ins[left][...], right)
            for j in range(product.shape[1] // CW):
                piece = product[:, j * CW : (j + 1) * CW].reshape(parts, -1, CW)
                where = (slice(at + j * size, at + (j + 1) * size), slice(None))
                if keeps:
                    piece = piece + got[(slice(None),) + where].astype(F32)
                    split_by(sel[1], piece, keep_ref, send_ref, where)
                else:
                    out_ref[(slice(None),) + where] = piece.astype(BF)

    if keeps and plan["extra"] is not None:
        at = plan["extra"]

        @pl.when(step == 0)
        def _():
            split_by(
                sel[1], extra[...], keep_ref, send_ref, (slice(at, at + EXTRA), slice(None))
            )


def weight_sums(sel, plan, arrays, specs, parts, total, got=None, extra=None):
    keeps = got is not None
    whole = lambda a: pl.BlockSpec(a.shape, lambda i, sel: (0,) * a.ndim)
    in_specs = list(specs)
    args = list(arrays)
    if keeps:
        if extra is None:
            extra = jnp.zeros((1, 8, LANES), BF)
        in_specs += [whole(got), whole(extra)]
        args += [got, extra]
        out_shape = [jax.ShapeDtypeStruct((parts // 2, total, CW), BF)] * 2
    else:
        out_shape = jax.ShapeDtypeStruct((parts, total, CW), BF)
    out_specs = jax.tree.map(lambda a: pl.BlockSpec(a.shape, lambda i, sel: (0, 0, 0)), out_shape)
    return pl.pallas_call(
        functools.partial(sums_kernel, plan=plan, parts=parts, keeps=keeps),
        grid_spec=pltpu.PrefetchScalarGridSpec(
            num_scalar_prefetch=1,
            grid=(len(plan["steps"]),),
            in_specs=in_specs,
            out_specs=out_specs,
        ),
        out_shape=out_shape,
        compiler_params=params(),
        cost_estimate=pl.CostEstimate(
            flops=2 * 1024 * 768 * 384 * len(plan["steps"]),
            bytes_accessed=8 * 2**20,
            transcendentals=0,
        ),
        name="weight_sums",
    )(sel, *args)


def halve_kernel(bit, one_ref, two_ref, keep_ref, send_ref):
    value = one_ref[...].astype(F32) + two_ref[...].astype(F32)
    split_by(bit[0], value, keep_ref, send_ref, (slice(None), slice(None)))


def halve(bit, one, two):
    m, n, c = one.shape
    pair = pl.BlockSpec((2, n, c), lambda i, bit: (i, 0, 0))
    single = pl.BlockSpec((1, n, c), lambda i, bit: (i, 0, 0))
    return pl.pallas_call(
        halve_kernel,
        grid_spec=pltpu.PrefetchScalarGridSpec(
            num_scalar_prefetch=1,
            grid=(m // 2,),
            in_specs=[pair, pair],
            out_specs=[single, single],
        ),
        out_shape=[jax.ShapeDtypeStruct((m // 2, n, c), BF)] * 2,
        compiler_params=params(),
        cost_estimate=pl.CostEstimate(
            flops=m * n * c, bytes_accessed=6 * m * n * c, transcendentals=0
        ),
        name="halve",
    )(bit, one, two)


def add(one, two):
    return (one.astype(F32) + two.astype(F32)).astype(BF)


def reduce_rest(keep, send, reps, group, rep_bits):
    bits = reps.bit_length() - 1
    for b in range(bits):
        got = swap(send, "rep", reps, b)
        if b + 1 < bits:
            keep, send = halve(rep_bits[b + 1], keep, got)
        else:
            keep = add(keep, got)
    for b in range(1, group.bit_length() - 1):
        keep = add(keep, swap(keep, "grp", group, b))
    other = swap(keep, "grp", group, 0)
    return keep[0], other[0]


def per_device(
    tokens,
    out_grad,
    destination,
    seq_first,
    valid_count,
    first_gain,
    first_bias,
    attn_weight,
    attn_bias,
    mix_weight,
    mix_bias,
    second_gain,
    second_bias,
    up_weight,
    up_bias,
    down_weight,
    down_bias,
):
    rows, width = tokens.shape
    ff = up_weight.shape[1]
    group = lax.axis_size("grp")
    reps = lax.axis_size("rep")
    me = lax.axis_index("grp")
    rep = lax.axis_index("rep")
    core = (me & 1).astype(jnp.int32)
    rep_bits = [((rep >> b) & 1).astype(jnp.int32).reshape(1) for b in range(reps.bit_length() - 1)]
    sel = jnp.stack([core, rep_bits[0][0]])
    core_one = core.reshape(1)
    row2 = lambda a: a.reshape(1, -1)

    table = jnp.stack(share(destination, group))
    wanted = me * NB + jnp.arange(NB, dtype=jnp.int32)
    match = table[:, :, None] == wanted[None, None, :]
    peers = jnp.arange(group, dtype=jnp.int32)[:, None, None]
    blocks = jnp.arange(NB, dtype=jnp.int32)[None, :, None]
    from_peer = jnp.sum(jnp.where(match, peers, 0), axis=(0, 1))
    from_block = jnp.sum(jnp.where(match, blocks, 0), axis=(0, 1))
    home_peer = (destination // NB) ^ me
    home_block = destination % NB

    total = jnp.sum(valid_count.astype(F32)).reshape(1, 1)
    for b in range(group.bit_length() - 1):
        total = total + swap(total, "grp", group, b)
    for b in range(reps.bit_length() - 1):
        total = total + swap(total, "rep", reps, b)
    scale = 1.0 / total[0, 0]

    token_parts = share(tokens, group)
    grad_parts = share(out_grad, group)
    qkv_bias = jnp.concatenate([attn_bias[:width], jnp.zeros((width,), F32), attn_bias[width:]])
    x, normed, qkv = project(
        from_peer,
        from_block,
        token_parts,
        row2(first_gain),
        row2(first_bias),
        attn_weight,
        row2(qkv_bias),
    )
    ctx, probs = attention(seq_first, valid_count, qkv)
    weights = (
        mix_weight,
        row2(mix_bias),
        row2(second_gain),
        row2(second_bias),
        up_weight,
        row2(up_bias),
        down_weight,
        row2(down_bias),
    )
    mixed, second, act, gu, gh, pre, dctx, og, sums = feed(
        from_peer, from_block, valid_count, grad_parts, x, ctx, weights
    )
    mixed_parts = share(mixed, group)

    size = width // reps
    ffs = ff // reps
    col = lambda w, index: pl.BlockSpec((rows, w), index)
    down_sent = down_sums(sel, act, og, reps, None)
    down_send = swap(down_sent, "grp", group, 0)

    def up_plan(own):
        half = (lambda sel: sel[0]) if own else (lambda sel: 1 - sel[0])
        wide = 2 * CW
        n_up = ff // 2 // wide
        specs = [
            col(width, lambda i, sel: (0, 0)),
            col(wide, lambda i, sel: (0, half(sel) * n_up + jnp.minimum(i, n_up - 1))),
            col(width, lambda i, sel: (0, 0)),
            col(CW, lambda i, sel: (0, half(sel))),
        ]
        steps = [(0, (1,), 2 * s * size, size) for s in range(n_up)]
        steps.append((2, (3,), 2 * n_up * size, size))
        rows_used = (2 * n_up + 1) * size
        return dict(inputs=4, steps=steps, extra=rows_used), specs, rows_used

    plan, specs, used = up_plan(False)
    up_sent = weight_sums(sel, plan, (second, gu, ctx, pre), specs, reps, used)
    up_send = swap(up_sent, "grp", group, 0)

    down_keep, down_next = down_sums(sel, act, og, reps, down_send)
    small = small_rows(
        [
            [(sums[0], ffs)],
            [(sums[r, :width], size) for r in (1, 2, 3, 4)],
        ],
        reps,
    )
    plan, specs, used = up_plan(True)
    up_keep, up_next = weight_sums(
        sel, plan, (second, gu, ctx, pre), specs, reps, used + EXTRA, up_send, small
    )
    down_halves = reduce_rest(down_keep, down_next, reps, group, rep_bits)
    up_halves = reduce_rest(up_keep, up_next, reps, group, rep_bits)

    dq, dk, dv = attention_back(core_one, qkv, ctx, dctx, probs)

    def attn_plan(own):
        half = (lambda sel: sel[0]) if own else (lambda sel: 1 - sel[0])
        n = width // LANES // 2
        specs = [col(width, lambda i, sel: (0, 0))]
        specs += [col(LANES, lambda i, sel: (0, 2 * i + half(sel)))] * 3
        steps = [(0, (1, 2, 3), s * size, size) for s in range(n)]
        return dict(inputs=4, steps=steps, extra=n * size), specs, n * size

    plan, specs, used = attn_plan(False)
    attn_sent = weight_sums(sel, plan, (normed, dq, dk, dv), specs, reps, used)
    attn_send = swap(attn_sent, "grp", group, 0)
    tokens_grad, sums_one = project_back(
        x, dq, dk, dv, gh, attn_weight, row2(first_gain)
    )
    home_parts = share(tokens_grad, group)
    bias_sums = jnp.concatenate([sums_one[2], sums_one[3]])
    small = small_rows(
        [[(sums_one[0], size), (sums_one[1], size), (bias_sums, 2 * size)]], reps
    )
    plan, specs, used = attn_plan(True)
    attn_keep, attn_next = weight_sums(
        sel, plan, (normed, dq, dk, dv), specs, reps, used + EXTRA, attn_send, small
    )
    attn_halves = reduce_rest(attn_keep, attn_next, reps, group, rep_bits)

    mixed_home = collect(home_peer, home_block, mixed_parts)
    tokens_home = collect(home_peer, home_block, home_parts)

    def ordered(halves):
        own, other = (h.astype(F32) * scale for h in halves)
        return jnp.where(core == 0, own, other), jnp.where(core == 0, other, own)

    low, high = ordered(down_halves)
    g_down = jnp.concatenate([low, high], axis=1)
    low, high = ordered(up_halves)
    n_up = ff // 2 // CW
    cut = lambda h, j: h[j * size : (j + 1) * size]
    g_up = jnp.concatenate([cut(h, j) for h in (low, high) for j in range(n_up)], axis=1)
    g_mix = jnp.concatenate([cut(low, n_up), cut(high, n_up)], axis=1)
    tail = (low + high)[(n_up + 1) * size :]
    g_up_bias = tail[0, :ffs]
    g_down_bias, g_gain_two, g_bias_two, g_mix_bias = (
        tail[1, j * size : (j + 1) * size] for j in range(4)
    )
    low, high = ordered(attn_halves)
    n_pair = width // LANES // 2
    pieces = [cut(h, j) for j in range(n_pair) for h in (low, high)]
    g_attn = jnp.concatenate(
        [p[:, i * LANES : (i + 1) * LANES] for i in range(3) for p in pieces], axis=1
    )
    tail = (low + high)[n_pair * size]
    g_gain_one = tail[:size]
    g_bias_one = tail[size : 2 * size]
    g_attn_bias = tail[2 * size : 4 * size]
    return (
        mixed_home,
        tokens_home,
        g_gain_one,
        g_bias_one,
        g_attn,
        g_attn_bias,
        g_mix,
        g_mix_bias,
        g_gain_two,
        g_bias_two,
        g_up,
        g_up_bias,
        g_down,
        g_down_bias,
    )


def small_rows(lines, reps):
    made = []
    for line in lines:
        row = jnp.concatenate([v.reshape(reps, n) for v, n in line], axis=1)
        made.append(jnp.pad(row, ((0, 0), (0, CW - row.shape[1]))))
    out = jnp.stack(made, axis=1)
    return jnp.pad(out, ((0, 0), (0, EXTRA - out.shape[1]), (0, 0))).astype(BF)


def down_kernel(sel, act_ref, og_ref, *refs, keeps):
    product = dot_tn(act_ref[...], og_ref[...])
    if not keeps:
        (out_ref,) = refs
        out_ref[...] = product.reshape(out_ref.shape).astype(BF)
        return
    got, keep_ref, send_ref = refs
    value = product.reshape(got.shape) + got[...].astype(F32)
    split_by(sel[1], value, keep_ref, send_ref, (slice(None), slice(None)))


def down_sums(sel, act, og, reps, got):
    rows, ff = act.shape
    keeps = got is not None
    share_rows = ff // reps
    steps = 4
    per = reps // steps
    block = pl.BlockSpec((per, share_rows, CW), lambda i, sel: (i, 0, 0))
    half = pl.BlockSpec((per // 2, share_rows, CW), lambda i, sel: (i, 0, 0))
    side = (lambda sel: sel[0]) if keeps else (lambda sel: 1 - sel[0])
    in_specs = [
        pl.BlockSpec((rows, ff // steps), lambda i, sel: (0, i)),
        pl.BlockSpec((rows, CW), lambda i, sel: (0, side(sel))),
    ]
    if keeps:
        in_specs.append(block)
    return pl.pallas_call(
        functools.partial(down_kernel, keeps=keeps),
        grid_spec=pltpu.PrefetchScalarGridSpec(
            num_scalar_prefetch=1,
            grid=(steps,),
            in_specs=in_specs,
            out_specs=[half, half] if keeps else block,
        ),
        out_shape=[jax.ShapeDtypeStruct((reps // 2, share_rows, CW), BF)] * 2
        if keeps
        else jax.ShapeDtypeStruct((reps, share_rows, CW), BF),
        compiler_params=params(),
        cost_estimate=pl.CostEstimate(
            flops=2 * rows * ff * CW, bytes_accessed=10 * 2**20, transcendentals=0
        ),
        name="down_sums",
    )(sel, act, og, *([got] if keeps else []))


def solution(mesh):
    tokens = P(("grp", "rep"), None)
    blocks = P(("grp", "rep"))
    return jax.shard_map(
        per_device,
        mesh=mesh,
        in_specs=(tokens, tokens, blocks, blocks, blocks) + (P(),) * 12,
        out_specs=(
            tokens,
            tokens,
            P("rep"),
            P("rep"),
            P("rep", None),
            P("rep"),
            P("rep", None),
            P("rep"),
            P("rep"),
            P("rep"),
            P("rep", None),
            P("rep"),
            P("rep", None),
            P("rep"),
        ),
        check_vma=False,
    )
```

```python
import functools

import jax
import jax.numpy as jnp
from jax import lax
from jax.experimental import pallas as pl
from jax.experimental.pallas import tpu as pltpu
from jax.sharding import PartitionSpec as P

F32 = jnp.float32
BF = jnp.bfloat16
HEAD_DIM = 64
NB = 8
BL = 128
LANES = 128
CW = 384
EXTRA = 16
DOWN_STEPS = 4
EPSILON = 1e-05
C0 = 0.7978845608028654
C1 = 0.044715
NEG = -1e30
VMEM = 56 * 2**20
NT = (((1,), (1,)), ((), ()))
TN = (((0,), (0,)), ((), ()))


def dot(a, b):
    return jnp.dot(a, b, preferred_element_type=F32)


def dot_nt(a, b):
    return lax.dot_general(a, b, NT, preferred_element_type=F32)


def dot_tn(a, b):
    return lax.dot_general(a, b, TN, preferred_element_type=F32)


def normalise(rows):
    width = rows.shape[1]
    centered = rows - jnp.sum(rows, axis=1, keepdims=True) * (1.0 / width)
    rstd = lax.rsqrt(
        jnp.sum(centered * centered, axis=1, keepdims=True) * (1.0 / width) + EPSILON
    )
    return centered * rstd, rstd


def norm_back(grad, gain, xhat, rstd):
    width = grad.shape[1]
    dx = grad * gain
    mean_one = jnp.sum(dx, axis=1, keepdims=True) * (1.0 / width)
    mean_two = jnp.sum(dx * xhat, axis=1, keepdims=True) * (1.0 / width)
    return rstd * (dx - mean_one - xhat * mean_two)


def colsum(rows):
    return jnp.sum(rows, axis=0, keepdims=True)


def params(**more):
    return pltpu.CompilerParams(vmem_limit_bytes=VMEM, **more)


def cost(us):
    return pl.CostEstimate(flops=int(us * 2e10), bytes_accessed=int(us * 1e6), transcendentals=0)


def whole(array):
    return pl.BlockSpec(array.shape, lambda *_: (0,) * array.ndim)


def swap(value, axis, size, bit):
    return lax.ppermute(value, axis, [(i, i ^ (1 << bit)) for i in range(size)])


def top_bit(size):
    return size.bit_length() - 2


def spread(value, size):
    found = [value]
    for bit in range(top_bit(size)):
        found = found + [swap(v, "grp", size, bit) for v in found]
    return found


def far(value, size):
    return swap(value, "grp", size, top_bit(size))


def share(value, size):
    return spread(value, size) + spread(far(value, size), size)


def after(value, *earlier):
    return lax.optimization_barrier((value,) + earlier)[0]


def start_gather(me, tables, sources, target, sems):
    for table, source in zip(tables, sources):
        for b in range(NB):
            slot = table[b] - me[0] * NB

            @pl.when((slot >= 0) & (slot < NB))
            def _(b=b, source=source, slot=slot):
                begin = pl.multiple_of(slot * BL, BL)
                pltpu.make_async_copy(
                    source.at[pl.ds(b * BL, BL)], target.at[pl.ds(begin, BL)], sems.at[slot]
                ).start()


def wait_gather(c, sources, target, sems):
    pltpu.make_async_copy(
        sources[0].at[pl.ds(0, BL)], target.at[pl.ds(c * BL, BL)], sems.at[c]
    ).wait()


def collect_kernel(me, destination, *refs, n):
    sources, out, sems = refs[:n], refs[n], refs[n + 1]
    for b in range(NB):
        peer = lax.div(destination[b], NB) ^ me[0]
        begin = pl.multiple_of(lax.rem(destination[b], NB) * BL, BL)
        for k, source in enumerate(sources):

            @pl.when(peer == k)
            def _(b=b, source=source, begin=begin):
                pltpu.make_async_copy(
                    source.at[pl.ds(begin, BL)], out.at[pl.ds(b * BL, BL)], sems.at[b]
                ).start()

    for b in range(NB):
        wait_gather(b, sources, out, sems)


def collect(me, destination, sources):
    n = len(sources)
    rows, width = sources[0].shape
    return pl.pallas_call(
        functools.partial(collect_kernel, n=n),
        grid_spec=pltpu.PrefetchScalarGridSpec(
            num_scalar_prefetch=2,
            grid=(1,),
            in_specs=[pl.BlockSpec(memory_space=pl.ANY)] * n,
            out_specs=pl.BlockSpec((rows, width), lambda i, *_: (0, 0)),
            scratch_shapes=[pltpu.SemaphoreType.DMA((NB,))],
        ),
        out_shape=jax.ShapeDtypeStruct((rows, width), sources[0].dtype),
        compiler_params=params(),
        cost_estimate=cost(4),
        name="collect",
    )(me, destination, *sources)


def project_kernel(me, *refs, n, tile, at):
    tables, sources, refs = refs[:n], refs[n : 2 * n], refs[2 * n :]
    vec, weight, x_out, normed_out, qkv_out, x_buf, sems = refs
    step = pl.program_id(0)
    per = tile // BL

    @pl.when(step == 0)
    def _():
        start_gather(me, tables, sources, x_buf, sems)

    for c in range(NB):

        @pl.when(step == c // per)
        def _(c=c):
            wait_gather(c, sources, x_buf, sems)

    x = x_buf[pl.ds(pl.multiple_of(step * tile, tile), tile), :]
    x_out[...] = x
    xhat, _ = normalise(x.astype(F32))
    width = x.shape[1]
    line = lambda name: vec[at[name] : at[name] + 1, :width]
    normed = xhat * line("first_gain") + line("first_bias")
    normed_out[...] = normed.T.astype(BF)
    normed = normed.astype(BF)
    for i, name in enumerate(("query_bias", None, "value_bias")):
        cols = slice(i * width, (i + 1) * width)
        part = dot(normed, weight[:, cols])
        qkv_out[:, cols] = (part + line(name) if name else part).astype(BF)


def project(me, tables, sources, vec, at, weight, tile=256):
    n = len(sources)
    rows, width = sources[0].shape
    row = lambda w: pl.BlockSpec((tile, w), lambda i, *_: (i, 0))
    return pl.pallas_call(
        functools.partial(project_kernel, n=n, tile=tile, at=at),
        grid_spec=pltpu.PrefetchScalarGridSpec(
            num_scalar_prefetch=1 + n,
            grid=(rows // tile,),
            in_specs=[pl.BlockSpec(memory_space=pl.ANY)] * n + [whole(vec), whole(weight)],
            out_specs=[
                row(width),
                pl.BlockSpec((width, tile), lambda i, *_: (0, i)),
                row(3 * width),
            ],
            scratch_shapes=[pltpu.VMEM((rows, width), BF), pltpu.SemaphoreType.DMA((NB,))],
        ),
        out_shape=[
            jax.ShapeDtypeStruct((rows, width), BF),
            jax.ShapeDtypeStruct((width, rows), BF),
            jax.ShapeDtypeStruct((rows, 3 * width), BF),
        ],
        compiler_params=params(),
        cost_estimate=cost(9),
        name="project",
    )(me, *tables, *sources, vec, weight)


def head_masks(rows):
    lane = lax.broadcasted_iota(jnp.int32, (rows, LANES), 1)
    return [lane < HEAD_DIM, lane >= HEAD_DIM]


def attention_kernel(first, count, q_ref, k_ref, v_ref, ctx_ref, p_ref, *, rows, tile):
    q = q_ref[...]
    k = k_ref[...]
    v = v_ref[...]
    masks = head_masks(rows)
    zero = jnp.zeros((), BF)
    scale = jnp.asarray(HEAD_DIM**-0.5, BF)
    key_pos = lax.broadcasted_iota(jnp.int32, (BL, BL), 1)
    causal = key_pos <= lax.broadcasted_iota(jnp.int32, (BL, BL), 0)
    value_mean = colsum(v.astype(F32)) * (1.0 / rows)
    queries = [jnp.where(m, q, zero) * scale for m in masks]
    values = [jnp.where(m, v, zero) for m in masks]
    for i in range(rows // tile):
        keys = k[: (i + 1) * tile]
        scores = [dot_nt(query[i * tile : (i + 1) * tile], keys) for query in queries]
        for c in range(i * tile // BL, (i + 1) * tile // BL):
            begin = c * BL - i * tile
            allowed = causal & (key_pos < count[c])
            total = None
            for h in range(2):
                strip = scores[h][begin : begin + BL]
                parts = []
                for j in range(c):
                    other = jnp.where(j >= first[c], jnp.float32(0), jnp.float32(NEG))
                    parts.append(strip[:, j * BL : (j + 1) * BL] + other)
                parts.append(jnp.where(allowed, strip[:, c * BL : (c + 1) * BL], NEG))
                top = functools.reduce(jnp.maximum, parts)
                top = jnp.max(top, axis=1, keepdims=True)
                parts = [jnp.exp(part - top) for part in parts]
                inverse = 1.0 / jnp.sum(
                    functools.reduce(jnp.add, parts), axis=1, keepdims=True
                )
                parts = [(part * inverse).astype(BF) for part in parts]
                for j, part in enumerate(parts):
                    p_ref[h, c * BL : (c + 1) * BL, j * BL : (j + 1) * BL] = part
                probs = jnp.concatenate(parts, axis=1) if c else parts[0]
                out = dot(probs, values[h][: (c + 1) * BL])
                total = out if total is None else total + out
            total = jnp.where(count[c] == 0, jnp.broadcast_to(value_mean, total.shape), total)
            ctx_ref[c * BL : (c + 1) * BL, :] = total.astype(BF)


def attention(first, count, qkv, tile=512):
    rows = qkv.shape[0]
    width = qkv.shape[1] // 3
    pairs = width // LANES
    col = lambda off: pl.BlockSpec((rows, LANES), lambda i, *_: (0, i + off))
    return pl.pallas_call(
        functools.partial(attention_kernel, rows=rows, tile=tile),
        grid_spec=pltpu.PrefetchScalarGridSpec(
            num_scalar_prefetch=2,
            grid=(pairs,),
            in_specs=[col(0), col(pairs), col(2 * pairs)],
            out_specs=[col(0), pl.BlockSpec((2, rows, rows), lambda i, *_: (i, 0, 0))],
        ),
        out_shape=[
            jax.ShapeDtypeStruct((rows, width), BF),
            jax.ShapeDtypeStruct((2 * pairs, rows, rows), BF),
        ],
        compiler_params=params(),
        cost_estimate=cost(0.001),
        name="attention",
    )(first, count, qkv, qkv, qkv)


def split_by(bit, value, keep_ref, send_ref, where):
    for i in range(value.shape[0] // 2):
        even, odd = value[2 * i], value[2 * i + 1]
        keep_ref[(i,) + where] = jnp.where(bit == 0, even, odd).astype(BF)
        send_ref[(i,) + where] = jnp.where(bit == 0, odd, even).astype(BF)


def window(total, share_size, r):
    return min(r * share_size // LANES * LANES, max(total - 2 * LANES, 0))


def small_shares(vectors, parts):
    lines = []
    for v in vectors:
        w = v.shape[1]
        size = w // parts
        if size % LANES == 0:
            pieces = [v[:, r * size : (r + 1) * size] for r in range(parts)]
        else:
            pieces = [v[:, window(w, size, r) :][:, : 2 * LANES] for r in range(parts)]
        lines.append([jnp.pad(p, ((0, 0), (0, CW - p.shape[1]))) for p in pieces])
    blank = jnp.zeros((EXTRA - len(lines), CW), F32)
    return [jnp.concatenate([line[r] for line in lines] + [blank], axis=0) for r in range(parts)]


def take_small(line, total, parts, rep):
    size = total // parts
    if size % LANES == 0:
        return line[:size]
    begin = jnp.minimum(rep * size // LANES * LANES, max(total - 2 * LANES, 0))
    return lax.dynamic_slice(line, (rep * size - begin,), (size,))


def feed_kernel(me, count, core, *refs, n, tile, ftile, at, parts):
    tables, sources, refs = refs[:n], refs[n : 2 * n], refs[2 * n :]
    x_ref, ctx_ref, vec, mixw, upw, downw = refs[:6]
    mixed_ref, branch_ref, second_ref, slope_ref, sent_ref, keep_ref = refs[6:12]
    og_buf, act_buf, sems = refs[12:]
    step = pl.program_id(0)
    per = tile // BL
    rows, width = og_buf.shape
    ff = upw.shape[1]
    tiles = rows // tile
    line = lambda name, w: vec[at[name] : at[name] + 1, :w]

    @pl.when(step == 0)
    def _():
        start_gather(me, tables, sources, og_buf, sems)

    @pl.when(step < tiles)
    def _():
        row = lax.broadcasted_iota(jnp.int32, (tile, 1), 0)
        live = jnp.zeros((tile, 1), F32)
        for b in range(per):
            filled = count[step * per + b]
            live = jnp.where((row >= b * BL) & (row < b * BL + filled), 1.0, live)
        branch = ((dot(ctx_ref[...], mixw[...]) + line("mix_bias", width)) * live).astype(BF)
        branch_ref[...] = branch
        hidden = x_ref[...].astype(F32) + branch.astype(F32)
        xhat, _ = normalise(hidden)
        second = xhat * line("second_gain", width) + line("second_bias", width)
        second_ref[...] = second.T.astype(BF)
        second = second.astype(BF)
        mixed = hidden + line("down_bias", width)
        begin = pl.multiple_of(step * tile, tile)
        for f in range(ff // ftile):
            cols = slice(f * ftile, (f + 1) * ftile)
            v = dot(second, upw[:, cols]) + vec[at["up_bias"] : at["up_bias"] + 1, cols]
            square = v * v
            half = 0.5 + 0.5 * jnp.tanh(v * (C0 + (C0 * C1) * square))
            act = (v * half).astype(BF)
            act_buf[pl.ds(begin, tile), cols] = act
            slope_ref[:, cols] = half + v * (half - half * half) * (
                2 * C0 + (6 * C0 * C1) * square
            )
            mixed = mixed + dot(act, downw[cols, :])
        mixed_ref[...] = mixed.astype(BF)

    @pl.when(step == tiles)
    def _():
        for c in range(NB):
            wait_gather(c, sources, og_buf, sems)

    @pl.when(step >= tiles)
    def _():
        block = ff // DOWN_STEPS
        begin = pl.multiple_of((step - tiles) * block, block)
        product = dot_tn(act_buf[:, pl.ds(begin, block)], og_buf[...])
        low = product[:, :CW].reshape(keep_ref.shape)
        high = product[:, CW:].reshape(keep_ref.shape)
        keep_ref[...] = jnp.where(core[0] == 0, low, high).astype(BF)
        sent_ref[...] = jnp.where(core[0] == 0, high, low).astype(BF)


def feed(me, tables, count, core, sources, x, ctx, vec, at, mixw, upw, downw, parts):
    tile, ftile = 256, 512
    n = len(sources)
    rows, width = x.shape
    ff = upw.shape[1]
    tiles = rows // tile
    now = lambda i: jnp.minimum(i, tiles - 1)
    row = lambda w: pl.BlockSpec((tile, w), lambda i, *_: (now(i), 0))
    block = pl.BlockSpec(
        (parts // DOWN_STEPS, ff // parts, CW), lambda i, *_: (jnp.maximum(i - tiles, 0), 0, 0)
    )
    bf = lambda *shape: jax.ShapeDtypeStruct(shape, BF)
    return pl.pallas_call(
        functools.partial(feed_kernel, n=n, tile=tile, ftile=ftile, at=at, parts=parts),
        grid_spec=pltpu.PrefetchScalarGridSpec(
            num_scalar_prefetch=3 + n,
            grid=(tiles + DOWN_STEPS,),
            in_specs=[pl.BlockSpec(memory_space=pl.ANY)] * n
            + [row(width), row(width)]
            + [whole(a) for a in (vec, mixw, upw, downw)],
            out_specs=[
                row(width),
                row(width),
                pl.BlockSpec((width, tile), lambda i, *_: (0, now(i))),
                row(ff),
                block,
                block,
            ],
            scratch_shapes=[
                pltpu.VMEM((rows, width), BF),
                pltpu.VMEM((rows, ff), BF),
                pltpu.SemaphoreType.DMA((NB,)),
            ],
        ),
        out_shape=[
            bf(rows, width),
            bf(rows, width),
            bf(width, rows),
            jax.ShapeDtypeStruct((rows, ff), F32),
            bf(parts, ff // parts, CW),
            bf(parts, ff // parts, CW),
        ],
        compiler_params=params(),
        cost_estimate=cost(28),
        name="feed",
    )(me, count, core, *tables, *sources, x, ctx, vec, mixw, upw, downw)


def feed_back_kernel(me, count, core, *refs, n, tile, ftile, at, parts):
    tables, sources, refs = refs[:n], refs[n : 2 * n], refs[2 * n :]
    x_ref, branch_ref, slope_ref, second_ref, ctx_ref, vec, mixw, upw, downw = refs[:9]
    (
        gh_ref,
        dctx_ref,
        up_sent,
        up_keep,
        mix_sent,
        mix_keep,
        small_ref,
        og_buf,
        gu_buf,
        pre_buf,
        sums,
        sems,
    ) = refs[9:]
    step = pl.program_id(0)
    per = tile // BL
    rows, width = og_buf.shape
    ff = upw.shape[1]
    tiles = rows // tile
    size = width // parts
    up_steps = ff // (2 * CW)
    line = lambda name, w: vec[at[name] : at[name] + 1, :w]

    @pl.when(step == 0)
    def _():
        start_gather(me, tables, sources, og_buf, sems)
        sums[...] = jnp.zeros_like(sums)

    for c in range(NB):

        @pl.when(step == c // per)
        def _(c=c):
            wait_gather(c, sources, og_buf, sems)

    @pl.when(step < tiles)
    def _():
        begin = pl.multiple_of(step * tile, tile)
        row = lax.broadcasted_iota(jnp.int32, (tile, 1), 0)
        live = jnp.zeros((tile, 1), F32)
        for b in range(per):
            filled = count[step * per + b]
            live = jnp.where((row >= b * BL) & (row < b * BL + filled), 1.0, live)
        og = og_buf[pl.ds(begin, tile), :]
        gs = jnp.zeros((tile, width), F32)
        for f in range(ff // ftile):
            cols = slice(f * ftile, (f + 1) * ftile)
            gu = (dot_nt(og, downw[cols, :]) * slope_ref[:, cols]).astype(BF)
            gu_buf[pl.ds(begin, tile), cols] = gu
            sums[0:1, cols] += colsum(gu.astype(F32))
            gs = gs + dot_nt(gu, upw[:, cols])
        xhat, rstd = normalise(x_ref[...].astype(F32) + branch_ref[...].astype(F32))
        og = og.astype(F32)
        gh = og + norm_back(gs, line("second_gain", width), xhat, rstd)
        gh_ref[...] = gh
        pre = gh.astype(BF).astype(F32) * live
        sums[1:2, :width] += colsum(og)
        sums[2:3, :width] += colsum(gs * xhat)
        sums[3:4, :width] += colsum(gs)
        sums[4:5, :width] += colsum(pre)
        pre = pre.astype(BF)
        pre_buf[pl.ds(begin, tile), :] = pre
        dctx_ref[...] = dot_nt(pre, mixw[...]).astype(BF)

    @pl.when((step >= tiles) & (step < tiles + up_steps))
    def _():
        s = step - tiles
        half_steps = up_steps // 2
        turn = jnp.where(s < half_steps, 1 - core[0], core[0])
        block = turn * half_steps + lax.rem(s, half_steps)
        cols = pl.ds(pl.multiple_of(block * 2 * CW, 2 * CW), 2 * CW)
        product = dot(second_ref[...], gu_buf[:, cols])
        pieces = [product[:, j * CW : (j + 1) * CW].reshape(parts, size, CW) for j in range(2)]
        pieces = [p.astype(BF) for p in pieces]

        @pl.when(s < half_steps)
        def _():
            for j in range(2):
                up_sent[:, j * size : (j + 1) * size, :] = pieces[j]

        @pl.when(s >= half_steps)
        def _():
            for j in range(2):
                up_keep[:, j * size : (j + 1) * size, :] = pieces[j]

    @pl.when(step == tiles + up_steps)
    def _():
        product = dot_tn(ctx_ref[...], pre_buf[...])
        low = product[:, :CW].reshape(mix_keep.shape)
        high = product[:, CW:].reshape(mix_keep.shape)
        mix_keep[...] = jnp.where(core[0] == 0, low, high).astype(BF)
        mix_sent[...] = jnp.where(core[0] == 0, high, low).astype(BF)
        vectors = [sums[0:1, :]] + [sums[j : j + 1, :width] for j in range(1, 5)]
        for r, value in enumerate(small_shares(vectors, parts)):
            small_ref[r] = value.astype(BF)


def feed_back(
    me, tables, count, core, sources, x, branch, slope, second, ctx, vec, at, mixw, upw, downw, parts
):
    tile, ftile = 256, 512
    n = len(sources)
    rows, width = x.shape
    ff = upw.shape[1]
    tiles = rows // tile
    size = width // parts
    up_steps = ff // (2 * CW)
    half = up_steps // 2
    now = lambda i: jnp.minimum(i, tiles - 1)
    row = lambda w: pl.BlockSpec((tile, w), lambda i, *_: (now(i), 0))
    up_block = lambda begin: pl.BlockSpec(
        (parts, 2 * size, CW), lambda i, *_: (0, jnp.clip(i - tiles - begin, 0, half - 1), 0)
    )
    bf = lambda *shape: jax.ShapeDtypeStruct(shape, BF)
    once = lambda *shape: pl.BlockSpec(shape, lambda i, *_: (0,) * len(shape))
    up_rows = ff // 2 // CW * size
    return pl.pallas_call(
        functools.partial(feed_back_kernel, n=n, tile=tile, ftile=ftile, at=at, parts=parts),
        grid_spec=pltpu.PrefetchScalarGridSpec(
            num_scalar_prefetch=3 + n,
            grid=(tiles + up_steps + 1,),
            in_specs=[pl.BlockSpec(memory_space=pl.ANY)] * n
            + [row(width), row(width), row(ff)]
            + [whole(a) for a in (second, ctx, vec, mixw, upw, downw)],
            out_specs=[
                row(width),
                row(width),
                up_block(0),
                up_block(half),
                once(parts, size, CW),
                once(parts, size, CW),
                once(parts, EXTRA, CW),
            ],
            scratch_shapes=[
                pltpu.VMEM((rows, width), BF),
                pltpu.VMEM((rows, ff), BF),
                pltpu.VMEM((rows, width), BF),
                pltpu.VMEM((8, ff), F32),
                pltpu.SemaphoreType.DMA((NB,)),
            ],
        ),
        out_shape=[
            jax.ShapeDtypeStruct((rows, width), F32),
            bf(rows, width),
            bf(parts, up_rows, CW),
            bf(parts, up_rows, CW),
            bf(parts, size, CW),
            bf(parts, size, CW),
            bf(parts, EXTRA, CW),
        ],
        compiler_params=params(),
        cost_estimate=cost(28),
        name="feed_back",
    )(me, count, core, *tables, *sources, x, branch, slope, second, ctx, vec, mixw, upw, downw)


def pair_back(q_ref, k_ref, v_ref, o_ref, g_ref, p_ref, ds_ref, out_ref, rows, tile):
    q = q_ref[...]
    k = k_ref[...]
    v = v_ref[...]
    grad = g_ref[...]
    masks = head_masks(rows)
    zero = jnp.zeros((), BF)
    scale = jnp.asarray(HEAD_DIM**-0.5, BF)
    product = grad.astype(F32) * o_ref[...].astype(F32)
    grads = [jnp.where(m, grad, zero) for m in masks]
    keys = [jnp.where(m, k, zero) * scale for m in masks]
    queries = [jnp.where(m, q, zero) * scale for m in masks]
    inner = [jnp.sum(jnp.where(m, product, 0.0), axis=1, keepdims=True) for m in masks]
    for i in range(rows // tile):
        cut = slice(i * tile, (i + 1) * tile)
        dprobs = [dot_nt(g[cut], v[: (i + 1) * tile]) for g in grads]
        for c in range(i * tile // BL, (i + 1) * tile // BL):
            begin = c * BL - i * tile
            own = slice(c * BL, (c + 1) * BL)
            width = (c + 1) * BL
            total = None
            for h in range(2):
                probs = p_ref[h, own, :width].astype(F32)
                ds = (probs * (dprobs[h][begin : begin + BL, :width] - inner[h][own])).astype(BF)
                ds_ref[h, own, :width] = ds
                out = dot(ds, keys[h][:width])
                total = out if total is None else total + out
            out_ref[own, :LANES] = total.astype(BF)
    for c in range(rows // BL):
        own = slice(c * BL, (c + 1) * BL)
        dk = dv = None
        for h in range(2):
            one = dot_tn(ds_ref[h, c * BL :, own], queries[h][c * BL :])
            two = dot_tn(p_ref[h, c * BL :, own], grads[h][c * BL :])
            dk = one if dk is None else dk + one
            dv = two if dv is None else dv + two
        out_ref[own, LANES : 2 * LANES] = dk.astype(BF)
        out_ref[own, 2 * LANES :] = dv.astype(BF)


def pairs_kernel(core, *refs, rows, tile, parts, at):
    ins = refs[:6]
    (
        normed,
        wq,
        wk,
        wv,
        vec,
        x_in,
        gh_in,
        tg_ref,
        sent_ref,
        keep_ref,
        small_ref,
        ds_ref,
        out_ref,
        grad,
        x_buf,
        gh_buf,
        bias,
        sems,
    ) = refs[6:]
    step = pl.program_id(0)
    steps = pl.num_programs(0)
    half = steps // 2
    width = x_buf.shape[1]
    copies = [
        pltpu.make_async_copy(a, b, sems.at[i])
        for i, (a, b) in enumerate(((x_in, x_buf), (gh_in, gh_buf)))
    ]

    @pl.when(step == 0)
    def _():
        for copy in copies:
            copy.start()
        grad[...] = jnp.zeros_like(grad)

    pair_back(*ins, ds_ref, out_ref, rows, tile)
    out = out_ref[...]
    value = dot(normed[...], out).reshape(sent_ref.shape).astype(BF)

    @pl.when(step < half)
    def _():
        sent_ref[...] = value

    @pl.when(step >= half)
    def _():
        keep_ref[...] = value

    weight = jnp.concatenate([wq[...], wk[...], wv[...]], axis=1)
    grad[...] += dot_nt(out, weight)
    sums = colsum(out.astype(F32))
    lanes = pl.ds(pl.multiple_of(pair_of(step, core, half) * LANES, LANES), LANES)
    bias[0:1, lanes] = sums[:, :LANES]
    bias[1:2, lanes] = sums[:, 2 * LANES :]

    @pl.when(step == steps - 1)
    def _():
        for copy in copies:
            copy.wait()
        gain = vec[at["first_gain"] : at["first_gain"] + 1, :width]
        gain_sum = jnp.zeros((1, width), F32)
        bias_sum = jnp.zeros((1, width), F32)
        block = 256
        for i in range(rows // block):
            cut = slice(i * block, (i + 1) * block)
            xhat, rstd = normalise(x_buf[cut, :].astype(F32))
            g = grad[cut, :]
            back = norm_back(g, gain, xhat, rstd).astype(BF).astype(F32)
            tg_ref[cut, :] = (gh_buf[cut, :] + back).astype(BF)
            gain_sum += colsum(g * xhat)
            bias_sum += colsum(g)
        both = jnp.concatenate([bias[0:1, :], bias[1:2, :]], axis=1)
        for r, value in enumerate(small_shares([gain_sum, bias_sum, both], parts)):
            small_ref[r] = value.astype(BF)


def pair_of(step, core, half):
    return jnp.where(step < half, 2 * step + 1 - core[0], 2 * (step - half) + core[0])


def attention_back(core, qkv, ctx, grad, probs, normed, weight, vec, at, x, gh, parts, tile=512):
    rows = qkv.shape[0]
    width = qkv.shape[1] // 3
    pairs = width // LANES
    half = pairs // 2
    size = width // parts
    anywhere = pl.BlockSpec(memory_space=pl.ANY)
    col = lambda off, h=rows: pl.BlockSpec(
        (h, LANES), lambda i, core: (0, pair_of(i, core, half) + off)
    )
    share_block = lambda begin: pl.BlockSpec(
        (parts, size, CW), lambda i, core: (0, jnp.clip(i - begin, 0, half - 1), 0)
    )
    return pl.pallas_call(
        functools.partial(pairs_kernel, rows=rows, tile=tile, parts=parts, at=at),
        grid_spec=pltpu.PrefetchScalarGridSpec(
            num_scalar_prefetch=1,
            grid=(pairs,),
            in_specs=[
                col(0),
                col(pairs),
                col(2 * pairs),
                col(0),
                col(0),
                pl.BlockSpec((2, rows, rows), lambda i, core: (pair_of(i, core, half), 0, 0)),
                whole(normed),
                col(0, width),
                col(pairs, width),
                col(2 * pairs, width),
                whole(vec),
                anywhere,
                anywhere,
            ],
            out_specs=[
                pl.BlockSpec((rows, width), lambda i, core: (0, 0)),
                share_block(0),
                share_block(half),
                pl.BlockSpec((parts, EXTRA, CW), lambda i, core: (0, 0, 0)),
            ],
            scratch_shapes=[
                pltpu.VMEM((2, rows, rows), BF),
                pltpu.VMEM((rows, 3 * LANES), BF),
                pltpu.VMEM((rows, width), F32),
                pltpu.VMEM((rows, width), BF),
                pltpu.VMEM((rows, width), F32),
                pltpu.VMEM((8, width), F32),
                pltpu.SemaphoreType.DMA((2,)),
            ],
        ),
        out_shape=[
            jax.ShapeDtypeStruct((rows, width), BF),
            jax.ShapeDtypeStruct((parts, half * size, CW), BF),
            jax.ShapeDtypeStruct((parts, half * size, CW), BF),
            jax.ShapeDtypeStruct((parts, EXTRA, CW), BF),
        ],
        compiler_params=params(),
        cost_estimate=cost(40),
        name="attention_back",
    )(core, qkv, qkv, qkv, ctx, grad, probs, normed, weight, weight, weight, vec, x, gh)


def halve_kernel(bit, *refs, counts):
    keep_ref, send_ref = refs[-2:]
    at = 0
    given = iter(refs[:-2])
    for number in counts:
        arrays = [next(given)[...].astype(F32) for _ in range(number)]
        value = functools.reduce(jnp.add, arrays)
        split_by(
            bit[0], value, keep_ref, send_ref, (slice(at, at + value.shape[1]), slice(None))
        )
        at += value.shape[1]


def halve(bit, *groups):
    arrays = [a for group in groups for a in group]
    m, _, c = arrays[0].shape
    n = sum(group[0].shape[1] for group in groups)
    pair = lambda a: pl.BlockSpec((2,) + a.shape[1:], lambda i, bit: (i, 0, 0))
    single = pl.BlockSpec((1, n, c), lambda i, bit: (i, 0, 0))
    return pl.pallas_call(
        functools.partial(halve_kernel, counts=[len(group) for group in groups]),
        grid_spec=pltpu.PrefetchScalarGridSpec(
            num_scalar_prefetch=1,
            grid=(m // 2,),
            in_specs=[pair(a) for a in arrays],
            out_specs=[single, single],
        ),
        out_shape=[jax.ShapeDtypeStruct((m // 2, n, c), BF)] * 2,
        compiler_params=params(),
        cost_estimate=cost(2),
        name="halve",
    )(bit, *arrays)


def deal_kernel(place, one_ref, two_ref, *outs):
    step = pl.program_id(0)
    for k, out in enumerate(outs):

        @pl.when(step == k)
        def _(out=out):
            out[...] = (one_ref[0].astype(F32) + two_ref[0].astype(F32)).astype(BF)


def deal(place, one, two):
    m, n, c = one.shape
    entry = pl.BlockSpec((1, n, c), lambda i, place: (place[0] ^ i, 0, 0))
    return pl.pallas_call(
        deal_kernel,
        grid_spec=pltpu.PrefetchScalarGridSpec(
            num_scalar_prefetch=1,
            grid=(m,),
            in_specs=[entry, entry],
            out_specs=[pl.BlockSpec((n, c), lambda i, place: (0, 0))] * m,
        ),
        out_shape=[jax.ShapeDtypeStruct((n, c), BF)] * m,
        compiler_params=params(),
        cost_estimate=cost(2),
        name="deal",
    )(place, one, two)


def add(*arrays):
    return functools.reduce(jnp.add, [a.astype(F32) for a in arrays]).astype(BF)


def cross(value, axis, size, mask):
    return lax.ppermute(value, axis, [(i, i ^ mask) for i in range(size)])


class Reduction:
    def __init__(self, keep, send, reps, group, rep):
        self.reps, self.group, self.rep = reps, group, rep
        self.bits = reps.bit_length() - 1
        self.keep, self.send, self.bit = keep, send, 0

    def along_first(self):
        got = swap(self.send, "rep", self.reps, self.bit)
        self.bit += 1
        while self.reps >> self.bit > 4:
            bit = ((self.rep >> self.bit) & 1).astype(jnp.int32).reshape(1)
            self.keep, self.send = halve(bit, (self.keep, got))
            got = swap(self.send, "rep", self.reps, self.bit)
            self.bit += 1
        self.got = got

    def along_rest(self):
        place = (self.rep >> self.bit).astype(jnp.int32).reshape(1)
        parts = list(deal(place, self.keep, self.got))
        self.parts = [parts[0]] + [
            cross(part, "rep", self.reps, k << self.bit) for k, part in enumerate(parts) if k
        ]


def across(value, group):
    for b in range(1, group.bit_length() - 1):
        value = add(value, swap(value, "grp", group, b))
    return value


def both_cores(value, group):
    return value, swap(value, "grp", group, 0)


def per_device(
    tokens,
    out_grad,
    destination,
    seq_first,
    valid_count,
    first_gain,
    first_bias,
    attn_weight,
    attn_bias,
    mix_weight,
    mix_bias,
    second_gain,
    second_bias,
    up_weight,
    up_bias,
    down_weight,
    down_bias,
):
    rows, width = tokens.shape
    ff = up_weight.shape[1]
    group = lax.axis_size("grp")
    reps = lax.axis_size("rep")
    me = lax.axis_index("grp").astype(jnp.int32).reshape(1)
    rep = lax.axis_index("rep").astype(jnp.int32)
    core = me & 1
    rep_bit = (rep & 1).reshape(1)
    size = width // reps
    ffs = ff // reps

    names = {
        "first_gain": first_gain,
        "first_bias": first_bias,
        "query_bias": attn_bias[:width],
        "value_bias": attn_bias[width:],
        "mix_bias": mix_bias,
        "second_gain": second_gain,
        "second_bias": second_bias,
        "up_bias": up_bias,
        "down_bias": down_bias,
    }
    at = {name: i for i, name in enumerate(names)}
    vec = jnp.stack([jnp.pad(v, (0, ff - v.shape[0])) for v in names.values()])

    tables = share(destination, group)
    total = jnp.sum(valid_count).reshape(1)
    for b in range(group.bit_length() - 1):
        total = total + swap(total, "grp", group, b)
    total_grp = total
    for b in range(reps.bit_length() - 1):
        total = total + swap(total, "rep", reps, b)
    scale = 1.0 / total[0].astype(F32)
    tokens_far = far(after(tokens, tables[-1], total_grp), group)
    tokens_near = spread(tokens, group)
    grad_near = spread(after(out_grad, tables[-1]), group)
    grad_far = far(after(out_grad, tokens_far), group)
    token_parts = tokens_near + spread(
        after(tokens_far, vec, total, *tables, *tokens_near[1:], *grad_near[1:]), group
    )
    x, normed, qkv = project(me, tables, token_parts, vec, at, attn_weight)
    ctx, probs = attention(seq_first, valid_count, qkv)
    grad_parts = grad_near + spread(after(grad_far, ctx), group)
    mixed, branch, second, slope, down_sent, down_keep = feed(
        me,
        tables,
        valid_count,
        core,
        grad_parts,
        x,
        ctx,
        vec,
        at,
        mix_weight,
        up_weight,
        down_weight,
        reps,
    )
    down_got = swap(down_sent, "grp", group, 0)
    mixed_far = far(mixed, group)
    mixed_near = spread(mixed, group)
    down = Reduction(*halve(rep_bit, (down_keep, down_got)), reps, group, rep)
    down.along_first()
    gh, dctx, up_sent, up_keep, mix_sent, mix_keep, small = feed_back(
        me,
        tables,
        valid_count,
        core,
        grad_parts,
        x,
        after(branch, down.send, *mixed_near[1:]),
        slope,
        second,
        ctx,
        vec,
        at,
        mix_weight,
        up_weight,
        down_weight,
        reps,
    )
    up_got = swap(up_sent, "grp", group, 0)
    mix_got = swap(mix_sent, "grp", group, 0)
    down.keep = after(down.keep, dctx)
    down.along_rest()
    up = Reduction(
        *halve(rep_bit, (up_keep, up_got), (mix_keep, mix_got), (small,)), reps, group, rep
    )
    up.along_first()
    mixed_parts = mixed_near + spread(after(mixed_far, dctx), group)
    tokens_grad, attn_sent, attn_keep, attn_small = attention_back(
        core,
        qkv,
        ctx,
        after(dctx, down.parts[0], up.send, mixed_parts[-1]),
        probs,
        normed,
        attn_weight,
        vec,
        at,
        x,
        gh,
        reps,
    )
    home_far = far(tokens_grad, group)
    home_near = spread(tokens_grad, group)
    attn_got = swap(attn_sent, "grp", group, 0)
    up.keep = after(up.keep, tokens_grad)
    up.along_rest()
    attn = Reduction(
        *halve(rep_bit, (after(attn_keep, up.parts[0]), attn_got), (attn_small,)), reps, group, rep
    )
    attn.along_first()
    mixed_home = collect(me, after(destination, attn.send), mixed_parts)
    attn.keep = after(attn.keep, mixed_home)
    attn.along_rest()
    home_far = after(home_far, attn.parts[0])
    home_parts = home_near + spread(home_far, group)
    up.parts[0] = after(up.parts[0], home_far)
    down.parts[0] = after(down.parts[0], home_far)
    early = across(jnp.concatenate([add(*down.parts), add(*up.parts)]), group)
    tokens_home = collect(me, after(destination, early), home_parts)
    early_halves = both_cores(early, group)
    attn.parts[0] = after(attn.parts[0], early)
    attn_halves = both_cores(across(add(*attn.parts), group), group)
    down_halves = [h[:ffs] for h in early_halves]
    up_halves = [h[ffs:] for h in early_halves]

    def ordered(halves):
        own, other = (h.astype(F32) * scale for h in halves)
        return jnp.where(core[0] == 0, own, other), jnp.where(core[0] == 0, other, own)

    low, high = ordered(down_halves)
    g_down = jnp.concatenate([low, high], axis=1)
    low, high = ordered(up_halves)
    n_up = ff // 2 // CW
    cut = lambda h, j: h[j * size : (j + 1) * size]
    g_up = jnp.concatenate([cut(h, j) for h in (low, high) for j in range(n_up)], axis=1)
    g_mix = jnp.concatenate([cut(low, n_up), cut(high, n_up)], axis=1)
    tail = (low + high)[(n_up + 1) * size :]
    g_up_bias = take_small(tail[0], ff, reps, rep)
    g_down_bias, g_gain_two, g_bias_two, g_mix_bias = (
        take_small(tail[j], width, reps, rep) for j in range(1, 5)
    )
    low, high = ordered(attn_halves)
    n_pair = width // LANES // 2
    pieces = [cut(h, j) for j in range(n_pair) for h in (low, high)]
    g_attn = jnp.concatenate(
        [p[:, i * LANES : (i + 1) * LANES] for i in range(3) for p in pieces], axis=1
    )
    tail = (low + high)[n_pair * size :]
    g_gain_one = take_small(tail[0], width, reps, rep)
    g_bias_one = take_small(tail[1], width, reps, rep)
    g_attn_bias = take_small(tail[2], 2 * width, reps, rep)
    return (
        mixed_home,
        tokens_home,
        g_gain_one,
        g_bias_one,
        g_attn,
        g_attn_bias,
        g_mix,
        g_mix_bias,
        g_gain_two,
        g_bias_two,
        g_up,
        g_up_bias,
        g_down,
        g_down_bias,
    )


def solution(mesh):
    tokens = P(("grp", "rep"), None)
    blocks = P(("grp", "rep"))
    return jax.shard_map(
        per_device,
        mesh=mesh,
        in_specs=(tokens, tokens, blocks, blocks, blocks) + (P(),) * 12,
        out_specs=(
            tokens,
            tokens,
            P("rep"),
            P("rep"),
            P("rep", None),
            P("rep"),
            P("rep", None),
            P("rep"),
            P("rep"),
            P("rep"),
            P("rep", None),
            P("rep"),
            P("rep", None),
            P("rep"),
        ),
        check_vma=False,
    )
```

```python
import functools

import jax
import jax.numpy as jnp
from jax import lax
from jax.experimental import pallas as pl
from jax.experimental.pallas import tpu as pltpu
from jax.sharding import PartitionSpec as P

F32 = jnp.float32
BF = jnp.bfloat16
HEAD_DIM = 64
NB = 8
BL = 128
LANES = 128
CW = 384
EXTRA = 16
DOWN_STEPS = 4
EPSILON = 1e-05
C0 = 0.7978845608028654
C1 = 0.044715
NEG = -1e30
VMEM = 63 * 2**20
NT = (((1,), (1,)), ((), ()))
TN = (((0,), (0,)), ((), ()))


def dot(a, b):
    return jnp.dot(a, b, preferred_element_type=F32)


def dot_nt(a, b):
    return lax.dot_general(a, b, NT, preferred_element_type=F32)


def dot_tn(a, b):
    return lax.dot_general(a, b, TN, preferred_element_type=F32)


def normalise(rows):
    width = rows.shape[1]
    centered = rows - jnp.sum(rows, axis=1, keepdims=True) * (1.0 / width)
    rstd = lax.rsqrt(
        jnp.sum(centered * centered, axis=1, keepdims=True) * (1.0 / width) + EPSILON
    )
    return centered * rstd, rstd


def norm_back(grad, gain, xhat, rstd):
    width = grad.shape[1]
    dx = grad * gain
    mean_one = jnp.sum(dx, axis=1, keepdims=True) * (1.0 / width)
    mean_two = jnp.sum(dx * xhat, axis=1, keepdims=True) * (1.0 / width)
    return rstd * (dx - mean_one - xhat * mean_two)


def colsum(rows):
    return jnp.sum(rows, axis=0, keepdims=True)


def params(**more):
    return pltpu.CompilerParams(vmem_limit_bytes=VMEM, **more)


def cost(us):
    return pl.CostEstimate(flops=int(us * 2e10), bytes_accessed=int(us * 1e6), transcendentals=0)


def whole(array):
    return pl.BlockSpec(
        array.shape, lambda *_: (0,) * array.ndim, pipeline_mode=pl.Buffered(buffer_count=1)
    )


def swap(value, axis, size, bit):
    return lax.ppermute(value, axis, [(i, i ^ (1 << bit)) for i in range(size)])


def top_bit(size):
    return size.bit_length() - 2


def spread(value, size):
    found = [value]
    for bit in range(top_bit(size)):
        found = found + [swap(v, "grp", size, bit) for v in found]
    return found


def far(value, size):
    return swap(value, "grp", size, top_bit(size))


def share(value, size):
    return spread(value, size) + spread(far(value, size), size)


def after(value, *earlier):
    return lax.optimization_barrier((value,) + earlier)[0]


def start_gather(me, tables, sources, target, sems):
    for table, source in zip(tables, sources):
        for b in range(NB):
            slot = table[b] - me[0] * NB

            @pl.when((slot >= 0) & (slot < NB))
            def _(b=b, source=source, slot=slot):
                begin = pl.multiple_of(slot * BL, BL)
                pltpu.make_async_copy(
                    source.at[pl.ds(b * BL, BL)], target.at[pl.ds(begin, BL)], sems.at[slot]
                ).start()


def wait_gather(c, sources, target, sems):
    pltpu.make_async_copy(
        sources[0].at[pl.ds(0, BL)], target.at[pl.ds(c * BL, BL)], sems.at[c]
    ).wait()


def collect_kernel(me, destination, *refs, n):
    sources, out, sems = refs[:n], refs[n], refs[n + 1]
    for b in range(NB):
        peer = lax.div(destination[b], NB) ^ me[0]
        begin = pl.multiple_of(lax.rem(destination[b], NB) * BL, BL)
        for k, source in enumerate(sources):

            @pl.when(peer == k)
            def _(b=b, source=source, begin=begin):
                pltpu.make_async_copy(
                    source.at[pl.ds(begin, BL)], out.at[pl.ds(b * BL, BL)], sems.at[b]
                ).start()

    for b in range(NB):
        wait_gather(b, sources, out, sems)


def collect(me, destination, sources, us=0.001):
    n = len(sources)
    rows, width = sources[0].shape
    return pl.pallas_call(
        functools.partial(collect_kernel, n=n),
        grid_spec=pltpu.PrefetchScalarGridSpec(
            num_scalar_prefetch=2,
            grid=(1,),
            in_specs=[pl.BlockSpec(memory_space=pl.ANY)] * n,
            out_specs=pl.BlockSpec((rows, width), lambda i, *_: (0, 0)),
            scratch_shapes=[pltpu.SemaphoreType.DMA((NB,))],
        ),
        out_shape=jax.ShapeDtypeStruct((rows, width), sources[0].dtype),
        compiler_params=params(),
        cost_estimate=cost(us),
        name="collect",
    )(me, destination, *sources)


def project_kernel(me, *refs, n, tile, at):
    tables, sources, refs = refs[:n], refs[n : 2 * n], refs[2 * n :]
    vec, weight, x_out, normed_out, qkv_out, x_buf, sems = refs
    step = pl.program_id(0)
    per = tile // BL

    @pl.when(step == 0)
    def _():
        start_gather(me, tables, sources, x_buf, sems)

    for c in range(NB):

        @pl.when(step == c // per)
        def _(c=c):
            wait_gather(c, sources, x_buf, sems)

    x = x_buf[pl.ds(pl.multiple_of(step * tile, tile), tile), :]
    x_out[...] = x
    xhat, _ = normalise(x.astype(F32))
    width = x.shape[1]
    line = lambda name: vec[at[name] : at[name] + 1, :width]
    normed = xhat * line("first_gain") + line("first_bias")
    normed_out[...] = normed.T.astype(BF)
    normed = normed.astype(BF)
    for i, name in enumerate(("query_bias", None, "value_bias")):
        cols = slice(i * width, (i + 1) * width)
        part = dot(normed, weight[:, cols])
        qkv_out[:, cols] = (part + line(name) if name else part).astype(BF)


def project(me, tables, sources, vec, at, weight, tile=256):
    n = len(sources)
    rows, width = sources[0].shape
    row = lambda w: pl.BlockSpec((tile, w), lambda i, *_: (i, 0))
    return pl.pallas_call(
        functools.partial(project_kernel, n=n, tile=tile, at=at),
        grid_spec=pltpu.PrefetchScalarGridSpec(
            num_scalar_prefetch=1 + n,
            grid=(rows // tile,),
            in_specs=[pl.BlockSpec(memory_space=pl.ANY)] * n + [whole(vec), whole(weight)],
            out_specs=[
                row(width),
                pl.BlockSpec((width, tile), lambda i, *_: (0, i)),
                row(3 * width),
            ],
            scratch_shapes=[pltpu.VMEM((rows, width), BF), pltpu.SemaphoreType.DMA((NB,))],
        ),
        out_shape=[
            jax.ShapeDtypeStruct((rows, width), BF),
            jax.ShapeDtypeStruct((width, rows), BF),
            jax.ShapeDtypeStruct((rows, 3 * width), BF),
        ],
        compiler_params=params(),
        cost_estimate=cost(9),
        name="project",
    )(me, *tables, *sources, vec, weight)


def head_masks(rows):
    lane = lax.broadcasted_iota(jnp.int32, (rows, LANES), 1)
    return [lane < HEAD_DIM, lane >= HEAD_DIM]


def attention_kernel(first, count, q_ref, k_ref, v_ref, ctx_ref, p_ref, *, rows, tile):
    q = q_ref[...]
    k = k_ref[...]
    v = v_ref[...]
    masks = head_masks(rows)
    zero = jnp.zeros((), BF)
    scale = jnp.asarray(HEAD_DIM**-0.5, BF)
    key_pos = lax.broadcasted_iota(jnp.int32, (BL, BL), 1)
    causal = key_pos <= lax.broadcasted_iota(jnp.int32, (BL, BL), 0)
    value_mean = colsum(v.astype(F32)) * (1.0 / rows)
    queries = [jnp.where(m, q, zero) * scale for m in masks]
    values = [jnp.where(m, v, zero) for m in masks]
    for i in range(rows // tile):
        keys = k[: (i + 1) * tile]
        scores = [dot_nt(query[i * tile : (i + 1) * tile], keys) for query in queries]
        for c in range(i * tile // BL, (i + 1) * tile // BL):
            begin = c * BL - i * tile
            allowed = causal & (key_pos < count[c])
            total = None
            for h in range(2):
                strip = scores[h][begin : begin + BL]
                parts = []
                for j in range(c):
                    other = jnp.where(j >= first[c], jnp.float32(0), jnp.float32(NEG))
                    parts.append(strip[:, j * BL : (j + 1) * BL] + other)
                parts.append(jnp.where(allowed, strip[:, c * BL : (c + 1) * BL], NEG))
                top = functools.reduce(jnp.maximum, parts)
                top = jnp.max(top, axis=1, keepdims=True)
                parts = [jnp.exp(part - top) for part in parts]
                inverse = 1.0 / jnp.sum(
                    functools.reduce(jnp.add, parts), axis=1, keepdims=True
                )
                parts = [(part * inverse).astype(BF) for part in parts]
                for j, part in enumerate(parts):
                    p_ref[h, c * BL : (c + 1) * BL, j * BL : (j + 1) * BL] = part
                probs = jnp.concatenate(parts, axis=1) if c else parts[0]
                out = dot(probs, values[h][: (c + 1) * BL])
                total = out if total is None else total + out
            total = jnp.where(count[c] == 0, jnp.broadcast_to(value_mean, total.shape), total)
            ctx_ref[c * BL : (c + 1) * BL, :] = total.astype(BF)


def attention(first, count, qkv, tile=512):
    rows = qkv.shape[0]
    width = qkv.shape[1] // 3
    pairs = width // LANES
    col = lambda off: pl.BlockSpec((rows, LANES), lambda i, *_: (0, i + off))
    return pl.pallas_call(
        functools.partial(attention_kernel, rows=rows, tile=tile),
        grid_spec=pltpu.PrefetchScalarGridSpec(
            num_scalar_prefetch=2,
            grid=(pairs,),
            in_specs=[col(0), col(pairs), col(2 * pairs)],
            out_specs=[col(0), pl.BlockSpec((2, rows, rows), lambda i, *_: (i, 0, 0))],
        ),
        out_shape=[
            jax.ShapeDtypeStruct((rows, width), BF),
            jax.ShapeDtypeStruct((2 * pairs, rows, rows), BF),
        ],
        compiler_params=params(),
        cost_estimate=cost(0.001),
        name="attention",
    )(first, count, qkv, qkv, qkv)


def split_by(bit, value, keep_ref, send_ref, where):
    for i in range(value.shape[0] // 2):
        even, odd = value[2 * i], value[2 * i + 1]
        keep_ref[(i,) + where] = jnp.where(bit == 0, even, odd).astype(BF)
        send_ref[(i,) + where] = jnp.where(bit == 0, odd, even).astype(BF)


def window(total, share_size, r):
    return min(r * share_size // LANES * LANES, max(total - 2 * LANES, 0))


def extra_rows(rows):
    return EXTRA + -(rows + EXTRA) % 32


def small_shares(vectors, parts, rows=EXTRA):
    lines = []
    for v in vectors:
        w = v.shape[1]
        size = w // parts
        if size % LANES == 0:
            pieces = [v[:, r * size : (r + 1) * size] for r in range(parts)]
        else:
            pieces = [v[:, window(w, size, r) :][:, : 2 * LANES] for r in range(parts)]
        lines.append([jnp.pad(p, ((0, 0), (0, CW - p.shape[1]))) for p in pieces])
    blank = jnp.zeros((rows - len(lines), CW), F32)
    return [jnp.concatenate([line[r] for line in lines] + [blank], axis=0) for r in range(parts)]


def take_small(line, total, parts, rep):
    size = total // parts
    if size % LANES == 0:
        return line[:size]
    begin = jnp.minimum(rep * size // LANES * LANES, max(total - 2 * LANES, 0))
    return lax.dynamic_slice(line, (rep * size - begin,), (size,))


def feed_kernel(me, count, core, *refs, n, tile, ftile, at, parts):
    tables, sources, refs = refs[:n], refs[n : 2 * n], refs[2 * n :]
    x_ref, ctx_ref, ctx_all, vec, mixw, upw, downw = refs[:7]
    (
        mixed_ref,
        gh_ref,
        dctx_ref,
        down_sent,
        down_keep,
        up_sent,
        up_keep,
        mix_sent,
        mix_keep,
        small_ref,
        og_buf,
        act_buf,
        gu_buf,
        second_buf,
        pre_buf,
        sums,
        sems,
    ) = refs[7:]
    step = pl.program_id(0)
    per = tile // BL
    rows, width = og_buf.shape
    ff = upw.shape[1]
    tiles = rows // tile
    size = width // parts
    up_steps = ff // (2 * CW)
    line = lambda name, w: vec[at[name] : at[name] + 1, :w]

    @pl.when(step == 0)
    def _():
        start_gather(me, tables, sources, og_buf, sems)
        sums[...] = jnp.zeros_like(sums)

    for c in range(NB):

        @pl.when(step == c // per)
        def _(c=c):
            wait_gather(c, sources, og_buf, sems)

    @pl.when(step < tiles)
    def _():
        begin = pl.multiple_of(step * tile, tile)
        own = pl.ds(begin, tile)
        row = lax.broadcasted_iota(jnp.int32, (tile, 1), 0)
        live = jnp.zeros((tile, 1), F32)
        for b in range(per):
            filled = count[step * per + b]
            live = jnp.where((row >= b * BL) & (row < b * BL + filled), 1.0, live)
        branch = ((dot(ctx_ref[...], mixw[...]) + line("mix_bias", width)) * live).astype(BF)
        hidden = x_ref[...].astype(F32) + branch.astype(F32)
        xhat, rstd = normalise(hidden)
        second = xhat * line("second_gain", width) + line("second_bias", width)
        second_buf[:, own] = second.T.astype(BF)
        second = second.astype(BF)
        mixed = hidden + line("down_bias", width)
        og = og_buf[own, :]
        gs = jnp.zeros((tile, width), F32)
        for f in range(ff // ftile):
            cols = slice(f * ftile, (f + 1) * ftile)
            v = dot(second, upw[:, cols]) + vec[at["up_bias"] : at["up_bias"] + 1, cols]
            da = dot_nt(og, downw[cols, :])
            square = v * v
            half = 0.5 + 0.5 * jnp.tanh(v * (C0 + (C0 * C1) * square))
            act = (v * half).astype(BF)
            act_buf[own, cols] = act
            mixed = mixed + dot(act, downw[cols, :])
            slope = half + v * (half - half * half) * (2 * C0 + (6 * C0 * C1) * square)
            gu = (da * slope).astype(BF)
            gu_buf[own, cols] = gu
            sums[0:1, cols] += colsum(gu.astype(F32))
            gs = gs + dot_nt(gu, upw[:, cols])
        mixed_ref[...] = mixed.astype(BF)
        og = og.astype(F32)
        gh = og + norm_back(gs, line("second_gain", width), xhat, rstd)
        gh_ref[...] = gh
        pre = gh.astype(BF).astype(F32) * live
        sums[1:2, :width] += colsum(og)
        sums[2:3, :width] += colsum(gs * xhat)
        sums[3:4, :width] += colsum(gs)
        sums[4:5, :width] += colsum(pre)
        pre = pre.astype(BF)
        pre_buf[own, :] = pre
        dctx_ref[...] = dot_nt(pre, mixw[...]).astype(BF)

    @pl.when((step >= tiles) & (step < tiles + up_steps))
    def _():
        s = step - tiles
        half_steps = up_steps // 2
        turn = jnp.where(s < half_steps, 1 - core[0], core[0])
        block = turn * half_steps + lax.rem(s, half_steps)
        cols = pl.ds(pl.multiple_of(block * 2 * CW, 2 * CW), 2 * CW)
        product = dot(second_buf[...], gu_buf[:, cols])
        pieces = [product[:, j * CW : (j + 1) * CW].reshape(parts, size, CW) for j in range(2)]
        pieces = [p.astype(BF) for p in pieces]

        @pl.when(s < half_steps)
        def _():
            for j in range(2):
                up_sent[:, j * size : (j + 1) * size, :] = pieces[j]

        @pl.when(s >= half_steps)
        def _():
            for j in range(2):
                up_keep[:, j * size : (j + 1) * size, :] = pieces[j]

    @pl.when(step == tiles + up_steps)
    def _():
        product = dot_tn(ctx_all[...], pre_buf[...])
        low = product[:, :CW].reshape(mix_keep.shape)
        high = product[:, CW:].reshape(mix_keep.shape)
        mix_keep[...] = jnp.where(core[0] == 0, low, high).astype(BF)
        mix_sent[...] = jnp.where(core[0] == 0, high, low).astype(BF)
        vectors = [sums[0:1, :]] + [sums[j : j + 1, :width] for j in range(1, 5)]
        for r, value in enumerate(small_shares(vectors, parts, small_ref.shape[1])):
            small_ref[r] = value.astype(BF)

    @pl.when(step > tiles + up_steps)
    def _():
        block = ff // DOWN_STEPS
        begin = pl.multiple_of((step - tiles - up_steps - 1) * block, block)
        product = dot_tn(act_buf[:, pl.ds(begin, block)], og_buf[...])
        low = product[:, :CW].reshape(down_keep.shape)
        high = product[:, CW:].reshape(down_keep.shape)
        down_keep[...] = jnp.where(core[0] == 0, low, high).astype(BF)
        down_sent[...] = jnp.where(core[0] == 0, high, low).astype(BF)


def feed(me, tables, count, core, sources, x, ctx, vec, at, mixw, upw, downw, parts):
    tile, ftile = 256, 512
    n = len(sources)
    rows, width = x.shape
    ff = upw.shape[1]
    tiles = rows // tile
    size = width // parts
    up_steps = ff // (2 * CW)
    half = up_steps // 2
    extra = extra_rows(ff // 2 // CW * size + size)
    now = lambda i: jnp.minimum(i, tiles - 1)
    row = lambda w: pl.BlockSpec((tile, w), lambda i, *_: (now(i), 0))
    up_block = lambda begin: pl.BlockSpec(
        (parts, 2 * size, CW), lambda i, *_: (0, jnp.clip(i - tiles - begin, 0, half - 1), 0)
    )
    down_block = pl.BlockSpec(
        (parts // DOWN_STEPS, ff // parts, CW),
        lambda i, *_: (jnp.maximum(i - tiles - up_steps - 1, 0), 0, 0),
    )
    bf = lambda *shape: jax.ShapeDtypeStruct(shape, BF)
    once = lambda *shape: pl.BlockSpec(shape, lambda i, *_: (0,) * len(shape))
    up_rows = ff // 2 // CW * size
    return pl.pallas_call(
        functools.partial(feed_kernel, n=n, tile=tile, ftile=ftile, at=at, parts=parts),
        grid_spec=pltpu.PrefetchScalarGridSpec(
            num_scalar_prefetch=3 + n,
            grid=(tiles + up_steps + 1 + DOWN_STEPS,),
            in_specs=[pl.BlockSpec(memory_space=pl.ANY)] * n
            + [row(width), row(width)]
            + [whole(a) for a in (ctx, vec, mixw, upw, downw)],
            out_specs=[
                row(width),
                row(width),
                row(width),
                down_block,
                down_block,
                up_block(0),
                up_block(half),
                once(parts, size, CW),
                once(parts, size, CW),
                once(parts, extra, CW),
            ],
            scratch_shapes=[
                pltpu.VMEM((rows, width), BF),
                pltpu.VMEM((rows, ff), BF),
                pltpu.VMEM((rows, ff), BF),
                pltpu.VMEM((width, rows), BF),
                pltpu.VMEM((rows, width), BF),
                pltpu.VMEM((8, ff), F32),
                pltpu.SemaphoreType.DMA((NB,)),
            ],
        ),
        out_shape=[
            bf(rows, width),
            jax.ShapeDtypeStruct((rows, width), F32),
            bf(rows, width),
            bf(parts, ff // parts, CW),
            bf(parts, ff // parts, CW),
            bf(parts, up_rows, CW),
            bf(parts, up_rows, CW),
            bf(parts, size, CW),
            bf(parts, size, CW),
            bf(parts, extra, CW),
        ],
        compiler_params=params(),
        cost_estimate=cost(50),
        name="feed",
    )(me, count, core, *tables, *sources, x, ctx, ctx, vec, mixw, upw, downw)


def pair_back(q_ref, k_ref, v_ref, o_ref, g_ref, p_ref, ds_ref, out_ref, rows, tile):
    q = q_ref[...]
    k = k_ref[...]
    v = v_ref[...]
    grad = g_ref[...]
    masks = head_masks(rows)
    zero = jnp.zeros((), BF)
    scale = jnp.asarray(HEAD_DIM**-0.5, BF)
    product = grad.astype(F32) * o_ref[...].astype(F32)
    grads = [jnp.where(m, grad, zero) for m in masks]
    keys = [jnp.where(m, k, zero) * scale for m in masks]
    queries = [jnp.where(m, q, zero) * scale for m in masks]
    inner = [jnp.sum(jnp.where(m, product, 0.0), axis=1, keepdims=True) for m in masks]
    for i in range(rows // tile):
        cut = slice(i * tile, (i + 1) * tile)
        dprobs = [dot_nt(g[cut], v[: (i + 1) * tile]) for g in grads]
        for c in range(i * tile // BL, (i + 1) * tile // BL):
            begin = c * BL - i * tile
            own = slice(c * BL, (c + 1) * BL)
            width = (c + 1) * BL
            total = None
            for h in range(2):
                probs = p_ref[h, own, :width].astype(F32)
                ds = (probs * (dprobs[h][begin : begin + BL, :width] - inner[h][own])).astype(BF)
                ds_ref[h, own, :width] = ds
                out = dot(ds, keys[h][:width])
                total = out if total is None else total + out
            out_ref[own, :LANES] = total.astype(BF)
    for c in range(rows // BL):
        own = slice(c * BL, (c + 1) * BL)
        dk = dv = None
        for h in range(2):
            one = dot_tn(ds_ref[h, c * BL :, own], queries[h][c * BL :])
            two = dot_tn(p_ref[h, c * BL :, own], grads[h][c * BL :])
            dk = one if dk is None else dk + one
            dv = two if dv is None else dv + two
        out_ref[own, LANES : 2 * LANES] = dk.astype(BF)
        out_ref[own, 2 * LANES :] = dv.astype(BF)


def pairs_kernel(core, *refs, rows, tile, parts, at):
    ins = refs[:6]
    (
        normed,
        wq,
        wk,
        wv,
        vec,
        x_in,
        gh_in,
        tg_ref,
        sent_ref,
        keep_ref,
        small_ref,
        ds_ref,
        out_ref,
        grad,
        x_buf,
        gh_buf,
        bias,
        sems,
    ) = refs[6:]
    step = pl.program_id(0)
    steps = pl.num_programs(0)
    half = steps // 2
    width = x_buf.shape[1]
    copies = [
        pltpu.make_async_copy(a, b, sems.at[i])
        for i, (a, b) in enumerate(((x_in, x_buf), (gh_in, gh_buf)))
    ]

    @pl.when(step == 0)
    def _():
        for copy in copies:
            copy.start()
        grad[...] = jnp.zeros_like(grad)

    pair_back(*ins, ds_ref, out_ref, rows, tile)
    out = out_ref[...]
    value = dot(normed[...], out).reshape(sent_ref.shape).astype(BF)

    @pl.when(step < half)
    def _():
        sent_ref[...] = value

    @pl.when(step >= half)
    def _():
        keep_ref[...] = value

    weight = jnp.concatenate([wq[...], wk[...], wv[...]], axis=1)
    grad[...] += dot_nt(out, weight)
    sums = colsum(out.astype(F32))
    lanes = pl.ds(pl.multiple_of(pair_of(step, core, half) * LANES, LANES), LANES)
    bias[0:1, lanes] = sums[:, :LANES]
    bias[1:2, lanes] = sums[:, 2 * LANES :]

    @pl.when(step == steps - 1)
    def _():
        for copy in copies:
            copy.wait()
        gain = vec[at["first_gain"] : at["first_gain"] + 1, :width]
        gain_sum = jnp.zeros((1, width), F32)
        bias_sum = jnp.zeros((1, width), F32)
        block = 256
        for i in range(rows // block):
            cut = slice(i * block, (i + 1) * block)
            xhat, rstd = normalise(x_buf[cut, :].astype(F32))
            g = grad[cut, :]
            back = norm_back(g, gain, xhat, rstd).astype(BF).astype(F32)
            tg_ref[cut, :] = (gh_buf[cut, :] + back).astype(BF)
            gain_sum += colsum(g * xhat)
            bias_sum += colsum(g)
        both = jnp.concatenate([bias[0:1, :], bias[1:2, :]], axis=1)
        for r, value in enumerate(small_shares([gain_sum, bias_sum, both], parts)):
            small_ref[r] = value.astype(BF)


def pair_of(step, core, half):
    return jnp.where(step < half, 2 * step + 1 - core[0], 2 * (step - half) + core[0])


def attention_back(core, qkv, ctx, grad, probs, normed, weight, vec, at, x, gh, parts, tile=512):
    rows = qkv.shape[0]
    width = qkv.shape[1] // 3
    pairs = width // LANES
    half = pairs // 2
    size = width // parts
    anywhere = pl.BlockSpec(memory_space=pl.ANY)
    col = lambda off, h=rows: pl.BlockSpec(
        (h, LANES), lambda i, core: (0, pair_of(i, core, half) + off)
    )
    share_block = lambda begin: pl.BlockSpec(
        (parts, size, CW), lambda i, core: (0, jnp.clip(i - begin, 0, half - 1), 0)
    )
    return pl.pallas_call(
        functools.partial(pairs_kernel, rows=rows, tile=tile, parts=parts, at=at),
        grid_spec=pltpu.PrefetchScalarGridSpec(
            num_scalar_prefetch=1,
            grid=(pairs,),
            in_specs=[
                col(0),
                col(pairs),
                col(2 * pairs),
                col(0),
                col(0),
                pl.BlockSpec((2, rows, rows), lambda i, core: (pair_of(i, core, half), 0, 0)),
                whole(normed),
                col(0, width),
                col(pairs, width),
                col(2 * pairs, width),
                whole(vec),
                anywhere,
                anywhere,
            ],
            out_specs=[
                pl.BlockSpec((rows, width), lambda i, core: (0, 0)),
                share_block(0),
                share_block(half),
                pl.BlockSpec((parts, EXTRA, CW), lambda i, core: (0, 0, 0)),
            ],
            scratch_shapes=[
                pltpu.VMEM((2, rows, rows), BF),
                pltpu.VMEM((rows, 3 * LANES), BF),
                pltpu.VMEM((rows, width), F32),
                pltpu.VMEM((rows, width), BF),
                pltpu.VMEM((rows, width), F32),
                pltpu.VMEM((8, width), F32),
                pltpu.SemaphoreType.DMA((2,)),
            ],
        ),
        out_shape=[
            jax.ShapeDtypeStruct((rows, width), BF),
            jax.ShapeDtypeStruct((parts, half * size, CW), BF),
            jax.ShapeDtypeStruct((parts, half * size, CW), BF),
            jax.ShapeDtypeStruct((parts, EXTRA, CW), BF),
        ],
        compiler_params=params(),
        cost_estimate=cost(40),
        name="attention_back",
    )(core, qkv, qkv, qkv, ctx, grad, probs, normed, weight, weight, weight, vec, x, gh)


def halve_kernel(bit, *refs, counts, cuts):
    outs = refs[-2 * len(cuts) :]
    begin = 0
    given = iter(refs[: -2 * len(cuts)])
    for number in counts:
        pairs = [(next(given), next(given)) for _ in range(number)]
        low, high = (
            functools.reduce(jnp.add, [pair[j][0].astype(F32) for pair in pairs]) for j in range(2)
        )
        keep = jnp.where(bit[0] == 0, low, high).astype(BF)
        send = jnp.where(bit[0] == 0, high, low).astype(BF)
        first = 0
        for j, rows in enumerate(cuts):
            lo, hi = max(begin, first), min(begin + low.shape[0], first + rows)
            if lo < hi:
                outs[2 * j][0, lo - first : hi - first, :] = keep[lo - begin : hi - begin]
                outs[2 * j + 1][0, lo - first : hi - first, :] = send[lo - begin : hi - begin]
            first += rows
        begin += low.shape[0]


def halve(bit, k, groups, cuts=None, us=0.001):
    arrays = [a for group in groups for a in group]
    m, _, c = arrays[0].shape
    cuts = cuts or [sum(group[0].shape[1] for group in groups)]

    def entry(a, value):
        def index(i, bit):
            low = i & ((1 << k) - 1)
            return (((i >> k) << (k + 1)) + (value << k) + low, 0, 0)

        return pl.BlockSpec((1,) + a.shape[1:], index)

    cuts_twice = [n for n in cuts for _ in range(2)]
    outs = pl.pallas_call(
        functools.partial(halve_kernel, counts=[len(group) for group in groups], cuts=cuts),
        grid_spec=pltpu.PrefetchScalarGridSpec(
            num_scalar_prefetch=1,
            grid=(m // 2,),
            in_specs=[entry(a, value) for a in arrays for value in range(2)],
            out_specs=[pl.BlockSpec((1, n, c), lambda i, bit: (i, 0, 0)) for n in cuts_twice],
        ),
        out_shape=[jax.ShapeDtypeStruct((m // 2, n, c), BF) for n in cuts_twice],
        compiler_params=params(),
        cost_estimate=cost(us),
        name="halve",
    )(bit, *[a for a in arrays for _ in range(2)])
    return list(outs[::2]), list(outs[1::2])


def halve_rows_kernel(bit, one_ref, two_ref, keep_ref, send_ref):
    value = one_ref[0].astype(F32) + two_ref[0].astype(F32)
    half = value.shape[0] // 2
    low, high = value[:half], value[half:]
    keep_ref[0] = jnp.where(bit[0] == 0, low, high).astype(BF)
    send_ref[0] = jnp.where(bit[0] == 0, high, low).astype(BF)


def halve_rows(bit, one, two, us=0.001):
    m, n, c = one.shape
    block = lambda n: pl.BlockSpec((1, n, c), lambda i, bit: (i, 0, 0))
    return pl.pallas_call(
        halve_rows_kernel,
        grid_spec=pltpu.PrefetchScalarGridSpec(
            num_scalar_prefetch=1,
            grid=(m,),
            in_specs=[block(n), block(n)],
            out_specs=[block(n // 2), block(n // 2)],
        ),
        out_shape=[jax.ShapeDtypeStruct((m, n // 2, c), BF)] * 2,
        compiler_params=params(),
        cost_estimate=cost(us),
        name="halve_rows",
    )(bit, one, two)


def add(*arrays):
    return functools.reduce(jnp.add, [a.astype(F32) for a in arrays]).astype(BF)


class Reduction:
    def __init__(self, bits, reps, rep, groups, cuts=None, us=0.001):
        self.reps, self.rep = reps, rep
        self.left = sorted(bits)
        self.bits = list(bits)
        self.cuts = cuts
        self.split(groups, us)

    def split(self, groups, us):
        self.bit = self.bits.pop(0)
        place = self.left.index(self.bit)
        self.left.remove(self.bit)
        mine = ((self.rep >> self.bit) & 1).astype(jnp.int32).reshape(1)
        self.keep, self.send = halve(mine, place, groups, self.cuts, us)

    def exchange(self):
        self.got = [swap(s, "rep", self.reps, self.bit) for s in self.send]

    def wait(self, *earlier):
        self.keep = [after(k, *earlier) for k in self.keep] if earlier else self.keep

    def next(self, *earlier, us=0.001):
        self.wait(*earlier)
        self.split(list(zip(self.keep, self.got)), us)
        self.exchange()

    def rows(self, bit, group, us=0.001):
        mine = ((lax.axis_index("grp") >> bit) & 1).astype(jnp.int32).reshape(1)
        keep, send = halve_rows(mine, self.keep[0], self.got[0], us)
        self.keep, self.send = [keep], [send]
        self.got = [swap(send, "grp", group, bit)]

    def last(self):
        return jnp.concatenate([add(k, g)[0] for k, g in zip(self.keep, self.got)])


def across(value, group):
    for b in range(1, group.bit_length() - 1):
        value = add(value, swap(value, "grp", group, b))
    return value


def both_cores(value, group):
    return value, swap(value, "grp", group, 0)


def per_device(
    tokens,
    out_grad,
    destination,
    seq_first,
    valid_count,
    first_gain,
    first_bias,
    attn_weight,
    attn_bias,
    mix_weight,
    mix_bias,
    second_gain,
    second_bias,
    up_weight,
    up_bias,
    down_weight,
    down_bias,
):
    rows, width = tokens.shape
    ff = up_weight.shape[1]
    group = lax.axis_size("grp")
    reps = lax.axis_size("rep")
    me = lax.axis_index("grp").astype(jnp.int32).reshape(1)
    rep = lax.axis_index("rep").astype(jnp.int32)
    core = me & 1
    size = width // reps
    ffs = ff // reps

    names = {
        "first_gain": first_gain,
        "first_bias": first_bias,
        "query_bias": attn_bias[:width],
        "value_bias": attn_bias[width:],
        "mix_bias": mix_bias,
        "second_gain": second_gain,
        "second_bias": second_bias,
        "up_bias": up_bias,
        "down_bias": down_bias,
    }
    at = {name: i for i, name in enumerate(names)}
    vec = jnp.stack([jnp.pad(v, (0, ff - v.shape[0])) for v in names.values()])

    tables = share(destination, group)
    count_far = far(valid_count, group)
    tokens_far = far(after(tokens, tables[group // 2], count_far), group)
    tokens_near = spread(tokens, group)
    grad_near = spread(after(out_grad, tables[group // 2]), group)
    total = jnp.sum(valid_count + count_far).reshape(1)
    for b in range(reps.bit_length() - 1):
        total = total + swap(total, "rep", reps, b)
    for b in range(top_bit(group)):
        total = total + swap(total, "grp", group, b)
    grad_far = far(after(out_grad, tokens_far), group)
    token_parts = tokens_near + spread(
        after(tokens_far, vec, total, *tables, *tokens_near[1:], *grad_near[1:]), group
    )
    scale = 1.0 / total[0].astype(F32)
    x, normed, qkv = project(me, tables, token_parts, vec, at, attn_weight)
    ctx, probs = attention(seq_first, valid_count, qkv)
    grad_parts = grad_near + spread(after(grad_far, ctx), group)
    mixed, gh, dctx, down_sent, down_keep, up_sent, up_keep, mix_sent, mix_keep, small = feed(
        me,
        tables,
        valid_count,
        core,
        grad_parts,
        x,
        ctx,
        vec,
        at,
        mix_weight,
        up_weight,
        down_weight,
        reps,
    )
    mixed_far = far(mixed, group)
    up_got = swap(up_sent, "grp", group, 0)
    mix_got = swap(mix_sent, "grp", group, 0)
    down_got = swap(after(down_sent, up_got, mix_got), "grp", group, 0)
    bits = list(range(reps.bit_length() - 1))
    up = Reduction(bits, reps, rep, [(up_keep, up_got), (mix_keep, mix_got), (small,)])
    up.exchange()
    down = Reduction(
        bits[1:2] + bits[:1] + bits[2:], reps, rep, [(after(down_keep, *up.send), down_got)]
    )
    down.exchange()
    mixed_near = spread(after(mixed, *down.send), group)
    tokens_grad, attn_sent, attn_keep, attn_small = attention_back(
        core,
        qkv,
        ctx,
        after(dctx, *up.send, *down.send),
        probs,
        normed,
        attn_weight,
        vec,
        at,
        x,
        gh,
        reps,
    )
    top = top_bit(group)
    home_far = far(tokens_grad, group)
    home_near = spread(tokens_grad, group)
    attn_got = swap(attn_sent, "grp", group, 0)
    mixed_parts = mixed_near + spread(after(mixed_far, tokens_grad), group)
    up.next(tokens_grad, mixed_far, *mixed_near[1:], us=4)
    down.next(*up.send)
    attn_rows = attn_keep.shape[1] + EXTRA
    part = (attn_rows // 2 + 15) // 16 * 16
    attn = Reduction(
        bits,
        reps,
        rep,
        [(after(attn_keep, *down.send, *home_near[1:], mixed_parts[-1]), attn_got), (attn_small,)],
        [part, attn_rows - part],
    )
    attn.exchange()
    down.next(*attn.send)
    up.wait(*down.send)
    up.rows(top, group)
    attn.next(*up.send, home_far)
    while up.bits:
        up.next(*attn.send)
    while down.bits:
        down.next(*up.send)
    while len(attn.bits) > 1:
        attn.next(*down.send)
    attn.next(*up.send, *down.send)
    down.wait(*attn.send)
    up.wait(*attn.send)
    early = jnp.concatenate([down.last(), up.last()])
    early_own = early
    home_parts = home_near + spread(after(home_far, early), group)
    mixed_home = collect(me, after(destination, early), mixed_parts, us=4)
    tokens_home = collect(me, after(destination, mixed_home), home_parts)
    early_far = after(swap(early, "grp", group, top), tokens_home, *attn.got)
    high_row = (me[0] >> top) & 1
    early_down = add(early[:ffs], early_far[:ffs])
    early_up = [early[ffs:], early_far[ffs:]]
    for b in range(1, top):
        early_down = add(early_down, swap(early_down, "grp", group, b))
        early_up = [add(e, swap(e, "grp", group, b)) for e in early_up]
    early = jnp.concatenate(
        [early_down]
        + [jnp.where(high_row == j, early_up[1], early_up[0]) for j in (1, 0)]
    )
    attn.wait(early_own)
    attn_sum = attn.last()
    early_halves = both_cores(early, group)

    def ordered(halves):
        own, other = (h.astype(F32) * scale for h in halves)
        return jnp.where(core[0] == 0, own, other), jnp.where(core[0] == 0, other, own)

    low, high = ordered([h[:ffs] for h in early_halves])
    g_down = jnp.concatenate([low, high], axis=1)
    low, high = ordered([h[ffs:] for h in early_halves])
    n_up = ff // 2 // CW
    cut = lambda h, j: h[j * size : (j + 1) * size]
    g_up = jnp.concatenate([cut(h, j) for h in (low, high) for j in range(n_up)], axis=1)
    g_mix = jnp.concatenate([cut(low, n_up), cut(high, n_up)], axis=1)
    tail = (low + high)[(n_up + 1) * size :]
    g_up_bias = take_small(tail[0], ff, reps, rep)
    g_down_bias, g_gain_two, g_bias_two, g_mix_bias = (
        take_small(tail[j], width, reps, rep) for j in range(1, 5)
    )
    attn_sum = after(
        across(attn_sum, group),
        tokens_home,
        g_down,
        g_up,
        g_mix,
        g_up_bias,
        g_down_bias,
        g_gain_two,
        g_bias_two,
        g_mix_bias,
    )
    low, high = ordered(both_cores(attn_sum, group))
    n_pair = width // LANES // 2
    pieces = [cut(h, j) for j in range(n_pair) for h in (low, high)]
    g_attn = jnp.concatenate(
        [p[:, i * LANES : (i + 1) * LANES] for i in range(3) for p in pieces], axis=1
    )
    tail = (low + high)[n_pair * size :]
    g_gain_one = take_small(tail[0], width, reps, rep)
    g_bias_one = take_small(tail[1], width, reps, rep)
    g_attn_bias = take_small(tail[2], 2 * width, reps, rep)
    return (
        mixed_home,
        tokens_home,
        g_gain_one,
        g_bias_one,
        g_attn,
        g_attn_bias,
        g_mix,
        g_mix_bias,
        g_gain_two,
        g_bias_two,
        g_up,
        g_up_bias,
        g_down,
        g_down_bias,
    )


def solution(mesh):
    tokens = P(("grp", "rep"), None)
    blocks = P(("grp", "rep"))
    return jax.shard_map(
        per_device,
        mesh=mesh,
        in_specs=(tokens, tokens, blocks, blocks, blocks) + (P(),) * 12,
        out_specs=(
            tokens,
            tokens,
            P("rep"),
            P("rep"),
            P("rep", None),
            P("rep"),
            P("rep", None),
            P("rep"),
            P("rep"),
            P("rep"),
            P("rep", None),
            P("rep"),
            P("rep", None),
            P("rep"),
        ),
        check_vma=False,
    )
```

```python
import functools

import jax
import jax.numpy as jnp
from jax import lax
from jax.experimental import pallas as pl
from jax.experimental.pallas import tpu as pltpu
from jax.sharding import PartitionSpec as P

F32 = jnp.float32
BF = jnp.bfloat16
HEAD_DIM = 64
NB = 8
BL = 128
LANES = 128
CW = 384
EXTRA = 16
DOWN_STEPS = 4
EPSILON = 1e-05
C0 = 0.7978845608028654
C1 = 0.044715
NEG = -1e30
VMEM = 63 * 2**20
NT = (((1,), (1,)), ((), ()))
TN = (((0,), (0,)), ((), ()))


def dot(a, b):
    return jnp.dot(a, b, preferred_element_type=F32)


def dot_nt(a, b):
    return lax.dot_general(a, b, NT, preferred_element_type=F32)


def dot_tn(a, b):
    return lax.dot_general(a, b, TN, preferred_element_type=F32)


def normalise(rows):
    width = rows.shape[1]
    centered = rows - jnp.sum(rows, axis=1, keepdims=True) * (1.0 / width)
    rstd = lax.rsqrt(
        jnp.sum(centered * centered, axis=1, keepdims=True) * (1.0 / width) + EPSILON
    )
    return centered * rstd, rstd


def norm_back(grad, gain, xhat, rstd):
    width = grad.shape[1]
    dx = grad * gain
    mean_one = jnp.sum(dx, axis=1, keepdims=True) * (1.0 / width)
    mean_two = jnp.sum(dx * xhat, axis=1, keepdims=True) * (1.0 / width)
    return rstd * (dx - mean_one - xhat * mean_two)


def colsum(rows):
    return jnp.sum(rows, axis=0, keepdims=True)


def params(mib=None):
    return pltpu.CompilerParams(vmem_limit_bytes=mib * 2**20 if mib else VMEM)


def cost(us):
    return pl.CostEstimate(flops=int(us * 2e10), bytes_accessed=int(us * 1e6), transcendentals=0)


def whole(array):
    return pl.BlockSpec(
        array.shape, lambda *_: (0,) * array.ndim, pipeline_mode=pl.Buffered(buffer_count=1)
    )


def swap(value, axis, size, bit):
    return lax.ppermute(value, axis, [(i, i ^ (1 << bit)) for i in range(size)])


def top_bit(size):
    return size.bit_length() - 2


def spread(value, size):
    found = [value]
    for bit in range(top_bit(size)):
        found = found + [swap(v, "grp", size, bit) for v in found]
    return found


def far(value, size):
    return swap(value, "grp", size, top_bit(size))


def share(value, size):
    return spread(value, size) + spread(far(value, size), size)


def after(value, *earlier):
    return lax.optimization_barrier((value,) + earlier)[0]


def start_gather(me, tables, sources, target, sems):
    for table, source in zip(tables, sources):
        for b in range(NB):
            slot = table[b] - me[0] * NB

            @pl.when((slot >= 0) & (slot < NB))
            def _(b=b, source=source, slot=slot):
                begin = pl.multiple_of(slot * BL, BL)
                pltpu.make_async_copy(
                    source.at[pl.ds(b * BL, BL)], target.at[pl.ds(begin, BL)], sems.at[slot]
                ).start()


def wait_gather(c, sources, target, sems):
    pltpu.make_async_copy(
        sources[0].at[pl.ds(0, BL)], target.at[pl.ds(c * BL, BL)], sems.at[c]
    ).wait()


def collect_kernel(me, destination, *refs, n):
    sources, out, sems = refs[:n], refs[n], refs[n + 1]
    for b in range(NB):
        peer = lax.div(destination[b], NB) ^ me[0]
        begin = pl.multiple_of(lax.rem(destination[b], NB) * BL, BL)
        for k, source in enumerate(sources):

            @pl.when(peer == k)
            def _(b=b, source=source, begin=begin):
                pltpu.make_async_copy(
                    source.at[pl.ds(begin, BL)], out.at[pl.ds(b * BL, BL)], sems.at[b]
                ).start()

    for b in range(NB):
        wait_gather(b, sources, out, sems)


def collect(me, destination, sources, us=0.001):
    n = len(sources)
    rows, width = sources[0].shape
    return pl.pallas_call(
        functools.partial(collect_kernel, n=n),
        grid_spec=pltpu.PrefetchScalarGridSpec(
            num_scalar_prefetch=2,
            grid=(1,),
            in_specs=[pl.BlockSpec(memory_space=pl.ANY)] * n,
            out_specs=pl.BlockSpec((rows, width), lambda i, *_: (0, 0)),
            scratch_shapes=[pltpu.SemaphoreType.DMA((NB,))],
        ),
        out_shape=jax.ShapeDtypeStruct((rows, width), sources[0].dtype),
        compiler_params=params(),
        cost_estimate=cost(us),
        name="collect",
    )(me, destination, *sources)


def project_kernel(me, *refs, n, tile, at):
    tables, sources, refs = refs[:n], refs[n : 2 * n], refs[2 * n :]
    vec, weight, x_out, normed_out, qkv_out, x_buf, sems = refs
    step = pl.program_id(0)
    per = tile // BL

    @pl.when(step == 0)
    def _():
        start_gather(me, tables, sources, x_buf, sems)

    for c in range(NB):

        @pl.when(step == c // per)
        def _(c=c):
            wait_gather(c, sources, x_buf, sems)

    x = x_buf[pl.ds(pl.multiple_of(step * tile, tile), tile), :]
    x_out[...] = x
    xhat, _ = normalise(x.astype(F32))
    width = x.shape[1]
    line = lambda name: vec[at[name] : at[name] + 1, :width]
    normed = xhat * line("first_gain") + line("first_bias")
    normed_out[...] = normed.T.astype(BF)
    normed = normed.astype(BF)
    for i, name in enumerate(("query_bias", None, "value_bias")):
        cols = slice(i * width, (i + 1) * width)
        part = dot(normed, weight[:, cols])
        qkv_out[:, cols] = (part + line(name) if name else part).astype(BF)


def project(me, tables, sources, vec, at, weight, tile=256):
    n = len(sources)
    rows, width = sources[0].shape
    row = lambda w: pl.BlockSpec((tile, w), lambda i, *_: (i, 0))
    return pl.pallas_call(
        functools.partial(project_kernel, n=n, tile=tile, at=at),
        grid_spec=pltpu.PrefetchScalarGridSpec(
            num_scalar_prefetch=1 + n,
            grid=(rows // tile,),
            in_specs=[pl.BlockSpec(memory_space=pl.ANY)] * n + [whole(vec), whole(weight)],
            out_specs=[
                row(width),
                pl.BlockSpec((width, tile), lambda i, *_: (0, i)),
                row(3 * width),
            ],
            scratch_shapes=[pltpu.VMEM((rows, width), BF), pltpu.SemaphoreType.DMA((NB,))],
        ),
        out_shape=[
            jax.ShapeDtypeStruct((rows, width), BF),
            jax.ShapeDtypeStruct((width, rows), BF),
            jax.ShapeDtypeStruct((rows, 3 * width), BF),
        ],
        compiler_params=params(59),
        cost_estimate=cost(0.001),
        name="project",
    )(me, *tables, *sources, vec, weight)


def head_masks(rows):
    lane = lax.broadcasted_iota(jnp.int32, (rows, LANES), 1)
    return [lane < HEAD_DIM, lane >= HEAD_DIM]


def attention_kernel(first, count, q_ref, k_ref, v_ref, ctx_ref, p_ref, *, rows, tile):
    q = q_ref[...]
    k = k_ref[...]
    v = v_ref[...]
    masks = head_masks(rows)
    zero = jnp.zeros((), BF)
    scale = jnp.asarray(HEAD_DIM**-0.5, BF)
    key_pos = lax.broadcasted_iota(jnp.int32, (BL, BL), 1)
    causal = key_pos <= lax.broadcasted_iota(jnp.int32, (BL, BL), 0)
    value_mean = colsum(v.astype(F32)) * (1.0 / rows)
    queries = [jnp.where(m, q, zero) * scale for m in masks]
    values = [jnp.where(m, v, zero) for m in masks]
    for i in range(rows // tile):
        keys = k[: (i + 1) * tile]
        scores = [dot_nt(query[i * tile : (i + 1) * tile], keys) for query in queries]
        for c in range(i * tile // BL, (i + 1) * tile // BL):
            begin = c * BL - i * tile
            allowed = causal & (key_pos < count[c])
            total = None
            for h in range(2):
                strip = scores[h][begin : begin + BL]
                parts = []
                for j in range(c):
                    other = jnp.where(j >= first[c], jnp.float32(0), jnp.float32(NEG))
                    parts.append(strip[:, j * BL : (j + 1) * BL] + other)
                parts.append(jnp.where(allowed, strip[:, c * BL : (c + 1) * BL], NEG))
                top = functools.reduce(jnp.maximum, parts)
                top = jnp.max(top, axis=1, keepdims=True)
                parts = [jnp.exp(part - top) for part in parts]
                inverse = 1.0 / jnp.sum(
                    functools.reduce(jnp.add, parts), axis=1, keepdims=True
                )
                parts = [(part * inverse).astype(BF) for part in parts]
                for j, part in enumerate(parts):
                    p_ref[h, c * BL : (c + 1) * BL, j * BL : (j + 1) * BL] = part
                probs = jnp.concatenate(parts, axis=1) if c else parts[0]
                out = dot(probs, values[h][: (c + 1) * BL])
                total = out if total is None else total + out
            total = jnp.where(count[c] == 0, jnp.broadcast_to(value_mean, total.shape), total)
            ctx_ref[c * BL : (c + 1) * BL, :] = total.astype(BF)


def attention(first, count, qkv, tile=512):
    rows = qkv.shape[0]
    width = qkv.shape[1] // 3
    pairs = width // LANES
    col = lambda off: pl.BlockSpec((rows, LANES), lambda i, *_: (0, i + off))
    return pl.pallas_call(
        functools.partial(attention_kernel, rows=rows, tile=tile),
        grid_spec=pltpu.PrefetchScalarGridSpec(
            num_scalar_prefetch=2,
            grid=(pairs,),
            in_specs=[col(0), col(pairs), col(2 * pairs)],
            out_specs=[col(0), pl.BlockSpec((2, rows, rows), lambda i, *_: (i, 0, 0))],
        ),
        out_shape=[
            jax.ShapeDtypeStruct((rows, width), BF),
            jax.ShapeDtypeStruct((2 * pairs, rows, rows), BF),
        ],
        compiler_params=params(),
        cost_estimate=cost(0.001),
        name="attention",
    )(first, count, qkv, qkv, qkv)


def split_by(bit, value, keep_ref, send_ref, where):
    for i in range(value.shape[0] // 2):
        even, odd = value[2 * i], value[2 * i + 1]
        keep_ref[(i,) + where] = jnp.where(bit == 0, even, odd).astype(BF)
        send_ref[(i,) + where] = jnp.where(bit == 0, odd, even).astype(BF)


def window(total, share_size, r):
    return min(r * share_size // LANES * LANES, max(total - 2 * LANES, 0))


def small_shares(vectors, parts, rows=EXTRA):
    lines = []
    for v in vectors:
        w = v.shape[1]
        size = w // parts
        if size % LANES == 0:
            pieces = [v[:, r * size : (r + 1) * size] for r in range(parts)]
        else:
            pieces = [v[:, window(w, size, r) :][:, : 2 * LANES] for r in range(parts)]
        lines.append([jnp.pad(p, ((0, 0), (0, CW - p.shape[1]))) for p in pieces])
    blank = jnp.zeros((rows - len(lines), CW), F32)
    return [jnp.concatenate([line[r] for line in lines] + [blank], axis=0) for r in range(parts)]


def take_small(line, total, parts, rep):
    size = total // parts
    if size % LANES == 0:
        return line[:size]
    begin = jnp.minimum(rep * size // LANES * LANES, max(total - 2 * LANES, 0))
    return lax.dynamic_slice(line, (rep * size - begin,), (size,))


def feed_kernel(me, count, core, *refs, n, tile, ftile, at, parts):
    tables, sources, refs = refs[:n], refs[n : 2 * n], refs[2 * n :]
    x_ref, ctx_ref, ctx_all, vec, mixw, upw, downw = refs[:7]
    (
        mixed_ref,
        gh_ref,
        dctx_ref,
        down_sent,
        down_keep,
        up_sent,
        up_keep,
        mix_sent,
        mix_keep,
        small_ref,
        og_buf,
        act_buf,
        gu_buf,
        second_buf,
        pre_buf,
        sums,
        sems,
    ) = refs[7:]
    step = pl.program_id(0)
    per = tile // BL
    rows, width = og_buf.shape
    ff = upw.shape[1]
    tiles = rows // tile
    size = width // parts
    up_steps = ff // (2 * CW)
    line = lambda name, w: vec[at[name] : at[name] + 1, :w]

    @pl.when(step == 0)
    def _():
        start_gather(me, tables, sources, og_buf, sems)
        sums[...] = jnp.zeros_like(sums)

    for c in range(NB):

        @pl.when(step == c // per)
        def _(c=c):
            wait_gather(c, sources, og_buf, sems)

    @pl.when(step < tiles)
    def _():
        begin = pl.multiple_of(step * tile, tile)
        own = pl.ds(begin, tile)
        row = lax.broadcasted_iota(jnp.int32, (tile, 1), 0)
        live = jnp.zeros((tile, 1), F32)
        for b in range(per):
            filled = count[step * per + b]
            live = jnp.where((row >= b * BL) & (row < b * BL + filled), 1.0, live)
        branch = ((dot(ctx_ref[...], mixw[...]) + line("mix_bias", width)) * live).astype(BF)
        hidden = x_ref[...].astype(F32) + branch.astype(F32)
        xhat, rstd = normalise(hidden)
        second = xhat * line("second_gain", width) + line("second_bias", width)
        second_buf[:, own] = second.T.astype(BF)
        second = second.astype(BF)
        mixed = hidden + line("down_bias", width)
        og = og_buf[own, :]
        gs = jnp.zeros((tile, width), F32)
        for f in range(ff // ftile):
            cols = slice(f * ftile, (f + 1) * ftile)
            v = dot(second, upw[:, cols]) + vec[at["up_bias"] : at["up_bias"] + 1, cols]
            da = dot_nt(og, downw[cols, :])
            square = v * v
            half = 0.5 + 0.5 * jnp.tanh(v * (C0 + (C0 * C1) * square))
            act = (v * half).astype(BF)
            act_buf[own, cols] = act
            mixed = mixed + dot(act, downw[cols, :])
            slope = half + v * (half - half * half) * (2 * C0 + (6 * C0 * C1) * square)
            gu = (da * slope).astype(BF)
            gu_buf[own, cols] = gu
            sums[0:1, cols] += colsum(gu.astype(F32))
            gs = gs + dot_nt(gu, upw[:, cols])
        mixed_ref[...] = mixed.astype(BF)
        og = og.astype(F32)
        gh = og + norm_back(gs, line("second_gain", width), xhat, rstd)
        gh_ref[...] = gh
        pre = gh.astype(BF).astype(F32) * live
        sums[1:2, :width] += colsum(og)
        sums[2:3, :width] += colsum(gs * xhat)
        sums[3:4, :width] += colsum(gs)
        sums[4:5, :width] += colsum(pre)
        pre = pre.astype(BF)
        pre_buf[own, :] = pre
        dctx_ref[...] = dot_nt(pre, mixw[...]).astype(BF)

    @pl.when((step >= tiles) & (step < tiles + up_steps))
    def _():
        s = step - tiles
        half_steps = up_steps // 2
        turn = jnp.where(s < half_steps, 1 - core[0], core[0])
        block = turn * half_steps + lax.rem(s, half_steps)
        cols = pl.ds(pl.multiple_of(block * 2 * CW, 2 * CW), 2 * CW)
        product = dot(second_buf[...], gu_buf[:, cols])
        pieces = [product[:, j * CW : (j + 1) * CW].reshape(parts, size, CW) for j in range(2)]
        pieces = [p.astype(BF) for p in pieces]

        @pl.when(s < half_steps)
        def _():
            for j in range(2):
                up_sent[:, j * size : (j + 1) * size, :] = pieces[j]

        @pl.when(s >= half_steps)
        def _():
            for j in range(2):
                up_keep[:, j * size : (j + 1) * size, :] = pieces[j]

    @pl.when(step == tiles + up_steps)
    def _():
        product = dot_tn(ctx_all[...], pre_buf[...])
        low = product[:, :CW].reshape(mix_keep.shape)
        high = product[:, CW:].reshape(mix_keep.shape)
        mix_keep[...] = jnp.where(core[0] == 0, low, high).astype(BF)
        mix_sent[...] = jnp.where(core[0] == 0, high, low).astype(BF)
        vectors = [sums[0:1, :]] + [sums[j : j + 1, :width] for j in range(1, 5)]
        for r, value in enumerate(small_shares(vectors, parts, small_ref.shape[1])):
            small_ref[r] = value.astype(BF)

    @pl.when(step > tiles + up_steps)
    def _():
        block = ff // DOWN_STEPS
        begin = pl.multiple_of((step - tiles - up_steps - 1) * block, block)
        product = dot_tn(act_buf[:, pl.ds(begin, block)], og_buf[...])
        low = product[:, :CW].reshape(down_keep.shape)
        high = product[:, CW:].reshape(down_keep.shape)
        down_keep[...] = jnp.where(core[0] == 0, low, high).astype(BF)
        down_sent[...] = jnp.where(core[0] == 0, high, low).astype(BF)


def feed(me, tables, count, core, sources, x, ctx, vec, at, mixw, upw, downw, parts):
    tile, ftile = 256, 512
    n = len(sources)
    rows, width = x.shape
    ff = upw.shape[1]
    tiles = rows // tile
    size = width // parts
    up_steps = ff // (2 * CW)
    half = up_steps // 2
    extra = EXTRA
    now = lambda i: jnp.minimum(i, tiles - 1)
    row = lambda w: pl.BlockSpec((tile, w), lambda i, *_: (now(i), 0))
    up_block = lambda begin: pl.BlockSpec(
        (parts, 2 * size, CW), lambda i, *_: (0, jnp.clip(i - tiles - begin, 0, half - 1), 0)
    )
    down_block = pl.BlockSpec(
        (parts // DOWN_STEPS, ff // parts, CW),
        lambda i, *_: (jnp.maximum(i - tiles - up_steps - 1, 0), 0, 0),
    )
    bf = lambda *shape: jax.ShapeDtypeStruct(shape, BF)
    once = lambda *shape: pl.BlockSpec(shape, lambda i, *_: (0,) * len(shape))
    up_rows = ff // 2 // CW * size
    return pl.pallas_call(
        functools.partial(feed_kernel, n=n, tile=tile, ftile=ftile, at=at, parts=parts),
        grid_spec=pltpu.PrefetchScalarGridSpec(
            num_scalar_prefetch=3 + n,
            grid=(tiles + up_steps + 1 + DOWN_STEPS,),
            in_specs=[pl.BlockSpec(memory_space=pl.ANY)] * n
            + [row(width), row(width)]
            + [whole(a) for a in (ctx, vec, mixw, upw, downw)],
            out_specs=[
                row(width),
                row(width),
                row(width),
                down_block,
                down_block,
                up_block(0),
                up_block(half),
                once(parts, size, CW),
                once(parts, size, CW),
                once(parts, extra, CW),
            ],
            scratch_shapes=[
                pltpu.VMEM((rows, width), BF),
                pltpu.VMEM((rows, ff), BF),
                pltpu.VMEM((rows, ff), BF),
                pltpu.VMEM((width, rows), BF),
                pltpu.VMEM((rows, width), BF),
                pltpu.VMEM((8, ff), F32),
                pltpu.SemaphoreType.DMA((NB,)),
            ],
        ),
        out_shape=[
            bf(rows, width),
            jax.ShapeDtypeStruct((rows, width), F32),
            bf(rows, width),
            bf(parts, ff // parts, CW),
            bf(parts, ff // parts, CW),
            bf(parts, up_rows, CW),
            bf(parts, up_rows, CW),
            bf(parts, size, CW),
            bf(parts, size, CW),
            bf(parts, extra, CW),
        ],
        compiler_params=params(),
        cost_estimate=cost(50),
        name="feed",
    )(me, count, core, *tables, *sources, x, ctx, ctx, vec, mixw, upw, downw)


def pair_back(q_ref, k_ref, v_ref, o_ref, g_ref, p_ref, ds_ref, out_ref, rows, tile):
    q = q_ref[...]
    k = k_ref[...]
    v = v_ref[...]
    grad = g_ref[...]
    masks = head_masks(rows)
    zero = jnp.zeros((), BF)
    scale = jnp.asarray(HEAD_DIM**-0.5, BF)
    product = grad.astype(F32) * o_ref[...].astype(F32)
    grads = [jnp.where(m, grad, zero) for m in masks]
    keys = [jnp.where(m, k, zero) * scale for m in masks]
    queries = [jnp.where(m, q, zero) * scale for m in masks]
    inner = [jnp.sum(jnp.where(m, product, 0.0), axis=1, keepdims=True) for m in masks]
    for i in range(rows // tile):
        cut = slice(i * tile, (i + 1) * tile)
        dprobs = [dot_nt(g[cut], v[: (i + 1) * tile]) for g in grads]
        for c in range(i * tile // BL, (i + 1) * tile // BL):
            begin = c * BL - i * tile
            own = slice(c * BL, (c + 1) * BL)
            width = (c + 1) * BL
            total = None
            for h in range(2):
                probs = p_ref[h, own, :width].astype(F32)
                ds = (probs * (dprobs[h][begin : begin + BL, :width] - inner[h][own])).astype(BF)
                ds_ref[h, own, :width] = ds
                out = dot(ds, keys[h][:width])
                total = out if total is None else total + out
            out_ref[own, :LANES] = total.astype(BF)
    for c in range(rows // BL):
        own = slice(c * BL, (c + 1) * BL)
        dk = dv = None
        for h in range(2):
            one = dot_tn(ds_ref[h, c * BL :, own], queries[h][c * BL :])
            two = dot_tn(p_ref[h, c * BL :, own], grads[h][c * BL :])
            dk = one if dk is None else dk + one
            dv = two if dv is None else dv + two
        out_ref[own, LANES : 2 * LANES] = dk.astype(BF)
        out_ref[own, 2 * LANES :] = dv.astype(BF)


def first_pairs_kernel(core, *refs, rows, tile, parts):
    ins = refs[:6]
    normed_in, wq, wk, wv, grad_ref, sent_ref, bias_ref, ds_ref, out_ref, normed, sem = refs[6:]
    step = pl.program_id(0)
    copy = pltpu.make_async_copy(normed_in, normed, sem)

    @pl.when(step == 0)
    def _():
        copy.start()

    pair_back(*ins, ds_ref, out_ref, rows, tile)

    @pl.when(step == 0)
    def _():
        copy.wait()

    out = out_ref[...]
    sent_ref[...] = dot(normed[...], out).reshape(sent_ref.shape).astype(BF)
    weight = jnp.concatenate([wq[...], wk[...], wv[...]], axis=1)
    grad = dot_nt(out, weight)

    @pl.when(step == 0)
    def _():
        grad_ref[...] = grad

    @pl.when(step > 0)
    def _():
        grad_ref[...] += grad

    sums = colsum(out.astype(F32))
    bias_ref[0:1, :] = sums[:, :LANES]
    bias_ref[1:2, :] = sums[:, 2 * LANES :]


def last_pairs_kernel(sel, *refs, rows, tile, parts, at):
    ins = refs[:6]
    (
        normed_in,
        wq,
        wk,
        wv,
        got,
        bias_in,
        vec,
        grad_in,
        x_in,
        gh_in,
        tg_ref,
        keep_ref,
        send_ref,
        ds_ref,
        out_ref,
        grad,
        x_buf,
        gh_buf,
        bias,
        normed,
        sems,
    ) = refs[6:]
    step = pl.program_id(0)
    steps = pl.num_programs(0)
    width = x_buf.shape[1]
    size = width // parts
    last = width // LANES // 2 * size
    copies = [
        pltpu.make_async_copy(a, b, sems.at[i])
        for i, (a, b) in enumerate(
            ((normed_in, normed), (grad_in, grad), (x_in, x_buf), (gh_in, gh_buf))
        )
    ]

    @pl.when(step == 0)
    def _():
        for copy in copies:
            copy.start()
        bias[...] = bias_in[...]

    pair_back(*ins, ds_ref, out_ref, rows, tile)

    @pl.when(step == 0)
    def _():
        copies[0].wait()
        copies[1].wait()

    out = out_ref[...]
    value = dot(normed[...], out).reshape(got.shape) + got[...].astype(F32)
    where = (pl.ds(pl.multiple_of(step * size, 8), size), slice(None))
    split_by(sel[1], value, keep_ref, send_ref, where)
    weight = jnp.concatenate([wq[...], wk[...], wv[...]], axis=1)
    grad[...] += dot_nt(out, weight)
    sums = colsum(out.astype(F32))
    lanes = pl.ds(pl.multiple_of((2 * step + sel[0]) * LANES, LANES), LANES)
    bias[0:1, lanes] = sums[:, :LANES]
    bias[1:2, lanes] = sums[:, 2 * LANES :]

    @pl.when(step == steps - 1)
    def _():
        copies[2].wait()
        copies[3].wait()
        gain = vec[at["first_gain"] : at["first_gain"] + 1, :width]
        gain_sum = jnp.zeros((1, width), F32)
        bias_sum = jnp.zeros((1, width), F32)
        block = 256
        for i in range(rows // block):
            cut = slice(i * block, (i + 1) * block)
            xhat, rstd = normalise(x_buf[cut, :].astype(F32))
            g = grad[cut, :]
            back = norm_back(g, gain, xhat, rstd).astype(BF).astype(F32)
            tg_ref[cut, :] = (gh_buf[cut, :] + back).astype(BF)
            gain_sum += colsum(g * xhat)
            bias_sum += colsum(g)
        both = jnp.concatenate([bias[0:1, :], bias[1:2, :]], axis=1)
        shares = jnp.stack(small_shares([gain_sum, bias_sum, both], parts))
        where = (slice(last, last + EXTRA), slice(None))
        split_by(sel[1], shares, keep_ref, send_ref, where)


def pairs_specs(rows, width, side):
    pairs = width // LANES
    pair = lambda i, sel: 2 * i + side(sel)
    col = lambda off, h=rows: pl.BlockSpec((h, LANES), lambda i, sel: (0, pair(i, sel) + off))
    return [
        col(0),
        col(pairs),
        col(2 * pairs),
        col(0),
        col(0),
        pl.BlockSpec((2, rows, rows), lambda i, sel: (pair(i, sel), 0, 0)),
        pl.BlockSpec(memory_space=pl.ANY),
        col(0, width),
        col(pairs, width),
        col(2 * pairs, width),
    ]


def first_pairs(sel, qkv, ctx, grad, probs, normed, weight, parts, tile=512):
    rows = qkv.shape[0]
    width = qkv.shape[1] // 3
    half = width // LANES // 2
    size = width // parts
    return pl.pallas_call(
        functools.partial(first_pairs_kernel, rows=rows, tile=tile, parts=parts),
        grid_spec=pltpu.PrefetchScalarGridSpec(
            num_scalar_prefetch=1,
            grid=(half,),
            in_specs=pairs_specs(rows, width, lambda sel: 1 - sel[0]),
            out_specs=[
                pl.BlockSpec((rows, width), lambda i, sel: (0, 0)),
                pl.BlockSpec((parts, size, CW), lambda i, sel: (0, i, 0)),
                pl.BlockSpec((8, LANES), lambda i, sel: (0, 2 * i + 1 - sel[0])),
            ],
            scratch_shapes=[
                pltpu.VMEM((2, rows, rows), BF),
                pltpu.VMEM((rows, 3 * LANES), BF),
                pltpu.VMEM((width, rows), BF),
                pltpu.SemaphoreType.DMA,
            ],
        ),
        out_shape=[
            jax.ShapeDtypeStruct((rows, width), F32),
            jax.ShapeDtypeStruct((parts, half * size, CW), BF),
            jax.ShapeDtypeStruct((8, width), F32),
        ],
        compiler_params=params(),
        cost_estimate=cost(20),
        name="first_pairs",
    )(sel, qkv, qkv, qkv, ctx, grad, probs, normed, weight, weight, weight)


def last_pairs(
    sel, qkv, ctx, grad, probs, normed, weight, got, bias, vec, at, partial, x, gh, parts, tile=512
):
    rows = qkv.shape[0]
    width = qkv.shape[1] // 3
    half = width // LANES // 2
    size = width // parts
    total = half * size + EXTRA
    anywhere = pl.BlockSpec(memory_space=pl.ANY)
    share_out = pl.BlockSpec((parts // 2, total, CW), lambda i, sel: (0, 0, 0))
    return pl.pallas_call(
        functools.partial(last_pairs_kernel, rows=rows, tile=tile, parts=parts, at=at),
        grid_spec=pltpu.PrefetchScalarGridSpec(
            num_scalar_prefetch=1,
            grid=(half,),
            in_specs=pairs_specs(rows, width, lambda sel: sel[0])
            + [
                pl.BlockSpec((parts, size, CW), lambda i, sel: (0, i, 0)),
                whole(bias),
                whole(vec),
                anywhere,
                anywhere,
                anywhere,
            ],
            out_specs=[
                pl.BlockSpec((rows, width), lambda i, sel: (0, 0)),
                share_out,
                share_out,
            ],
            scratch_shapes=[
                pltpu.VMEM((2, rows, rows), BF),
                pltpu.VMEM((rows, 3 * LANES), BF),
                pltpu.VMEM((rows, width), F32),
                pltpu.VMEM((rows, width), BF),
                pltpu.VMEM((rows, width), F32),
                pltpu.VMEM((8, width), F32),
                pltpu.VMEM((width, rows), BF),
                pltpu.SemaphoreType.DMA((4,)),
            ],
        ),
        out_shape=[
            jax.ShapeDtypeStruct((rows, width), BF),
            jax.ShapeDtypeStruct((parts // 2, total, CW), BF),
            jax.ShapeDtypeStruct((parts // 2, total, CW), BF),
        ],
        compiler_params=params(),
        cost_estimate=cost(20),
        name="last_pairs",
    )(
        sel, qkv, qkv, qkv, ctx, grad, probs, normed, weight, weight, weight, got, bias, vec, partial, x, gh
    )


def halve_kernel(bit, *refs, counts, cuts):
    outs = refs[-2 * len(cuts) :]
    begin = 0
    given = iter(refs[: -2 * len(cuts)])
    for number in counts:
        pairs = [(next(given), next(given)) for _ in range(number)]
        low, high = (
            functools.reduce(jnp.add, [pair[j][0].astype(F32) for pair in pairs]) for j in range(2)
        )
        keep = jnp.where(bit[0] == 0, low, high).astype(BF)
        send = jnp.where(bit[0] == 0, high, low).astype(BF)
        first = 0
        for j, rows in enumerate(cuts):
            lo, hi = max(begin, first), min(begin + low.shape[0], first + rows)
            if lo < hi:
                outs[2 * j][0, lo - first : hi - first, :] = keep[lo - begin : hi - begin]
                outs[2 * j + 1][0, lo - first : hi - first, :] = send[lo - begin : hi - begin]
            first += rows
        begin += low.shape[0]


def halve(bit, k, groups, cuts=None, us=0.001):
    arrays = [a for group in groups for a in group]
    m, _, c = arrays[0].shape
    cuts = cuts or [sum(group[0].shape[1] for group in groups)]

    def entry(a, value):
        def index(i, bit):
            low = i & ((1 << k) - 1)
            return (((i >> k) << (k + 1)) + (value << k) + low, 0, 0)

        return pl.BlockSpec((1,) + a.shape[1:], index)

    cuts_twice = [n for n in cuts for _ in range(2)]
    outs = pl.pallas_call(
        functools.partial(halve_kernel, counts=[len(group) for group in groups], cuts=cuts),
        grid_spec=pltpu.PrefetchScalarGridSpec(
            num_scalar_prefetch=1,
            grid=(m // 2,),
            in_specs=[entry(a, value) for a in arrays for value in range(2)],
            out_specs=[pl.BlockSpec((1, n, c), lambda i, bit: (i, 0, 0)) for n in cuts_twice],
        ),
        out_shape=[jax.ShapeDtypeStruct((m // 2, n, c), BF) for n in cuts_twice],
        compiler_params=params(),
        cost_estimate=cost(us),
        name="halve",
    )(bit, *[a for a in arrays for _ in range(2)])
    return list(outs[::2]), list(outs[1::2])


def halve_rows_kernel(bit, one_ref, two_ref, keep_ref, send_ref):
    value = one_ref[0].astype(F32) + two_ref[0].astype(F32)
    half = value.shape[0] // 2
    low, high = value[:half], value[half:]
    keep_ref[0] = jnp.where(bit[0] == 0, low, high).astype(BF)
    send_ref[0] = jnp.where(bit[0] == 0, high, low).astype(BF)


def halve_rows(bit, one, two, us=0.001):
    m, n, c = one.shape
    block = lambda n: pl.BlockSpec((1, n, c), lambda i, bit: (i, 0, 0))
    return pl.pallas_call(
        halve_rows_kernel,
        grid_spec=pltpu.PrefetchScalarGridSpec(
            num_scalar_prefetch=1,
            grid=(m,),
            in_specs=[block(n), block(n)],
            out_specs=[block(n // 2), block(n // 2)],
        ),
        out_shape=[jax.ShapeDtypeStruct((m, n // 2, c), BF)] * 2,
        compiler_params=params(),
        cost_estimate=cost(us),
        name="halve_rows",
    )(bit, one, two)


def add(*arrays):
    return functools.reduce(jnp.add, [a.astype(F32) for a in arrays]).astype(BF)


class Reduction:
    def __init__(self, bits, reps, rep, groups=None, cuts=None, us=0.001, halves=None):
        self.reps, self.rep = reps, rep
        self.left = sorted(bits)
        self.bits = list(bits)
        self.cuts = cuts
        if halves is None:
            self.split(groups, us)
        else:
            self.bit = self.bits.pop(0)
            self.left.remove(self.bit)
            self.keep, self.send = [halves[0]], [halves[1]]

    def split(self, groups, us):
        self.bit = self.bits.pop(0)
        place = self.left.index(self.bit)
        self.left.remove(self.bit)
        mine = ((self.rep >> self.bit) & 1).astype(jnp.int32).reshape(1)
        self.keep, self.send = halve(mine, place, groups, self.cuts, us)

    def exchange(self):
        self.got = [swap(s, "rep", self.reps, self.bit) for s in self.send]

    def wait(self, *earlier):
        self.keep = [after(k, *earlier) for k in self.keep] if earlier else self.keep

    def next(self, *earlier, us=0.001):
        self.wait(*earlier)
        self.split(list(zip(self.keep, self.got)), us)
        self.exchange()

    def rows(self, bit, group, us=0.001):
        mine = ((lax.axis_index("grp") >> bit) & 1).astype(jnp.int32).reshape(1)
        keep, send = halve_rows(mine, self.keep[0], self.got[0], us)
        self.keep, self.send = [keep], [send]
        self.got = [swap(send, "grp", group, bit)]

    def last(self):
        return jnp.concatenate([add(k, g)[0] for k, g in zip(self.keep, self.got)])


def across(value, group):
    for b in range(1, group.bit_length() - 1):
        value = add(value, swap(value, "grp", group, b))
    return value


def both_cores(value, group):
    return value, swap(value, "grp", group, 0)


def per_device(
    tokens,
    out_grad,
    destination,
    seq_first,
    valid_count,
    first_gain,
    first_bias,
    attn_weight,
    attn_bias,
    mix_weight,
    mix_bias,
    second_gain,
    second_bias,
    up_weight,
    up_bias,
    down_weight,
    down_bias,
):
    rows, width = tokens.shape
    ff = up_weight.shape[1]
    group = lax.axis_size("grp")
    reps = lax.axis_size("rep")
    me = lax.axis_index("grp").astype(jnp.int32).reshape(1)
    rep = lax.axis_index("rep").astype(jnp.int32)
    core = me & 1
    size = width // reps
    ffs = ff // reps

    names = {
        "first_gain": first_gain,
        "first_bias": first_bias,
        "query_bias": attn_bias[:width],
        "value_bias": attn_bias[width:],
        "mix_bias": mix_bias,
        "second_gain": second_gain,
        "second_bias": second_bias,
        "up_bias": up_bias,
        "down_bias": down_bias,
    }
    at = {name: i for i, name in enumerate(names)}
    vec = jnp.stack([jnp.pad(v, (0, ff - v.shape[0])) for v in names.values()])

    tables = share(destination, group)
    count_far = far(valid_count, group)
    tokens_far = far(after(tokens, tables[group // 2], count_far), group)
    tokens_near = spread(tokens, group)
    grad_near = spread(after(out_grad, tables[group // 2]), group)
    total = jnp.sum(valid_count + count_far).reshape(1)
    for b in range(reps.bit_length() - 1):
        total = total + swap(total, "rep", reps, b)
    for b in range(top_bit(group)):
        total = total + swap(total, "grp", group, b)
    grad_far = far(after(jnp.pad(out_grad, ((0, EXTRA), (0, 0))), vec), group)
    token_parts = tokens_near + spread(
        after(tokens_far, vec, total, *tables, *tokens_near[1:], *grad_near[1:]), group
    )
    scale = 1.0 / total[0].astype(F32)
    x, normed, qkv = project(me, tables, token_parts, vec, at, attn_weight)
    ctx, probs = attention(seq_first, valid_count, qkv)
    grad_parts = grad_near + spread(after(grad_far, ctx), group)
    mixed, gh, dctx, down_sent, down_keep, up_sent, up_keep, mix_sent, mix_keep, small = feed(
        me,
        tables,
        valid_count,
        core,
        grad_parts,
        x,
        ctx,
        vec,
        at,
        mix_weight,
        up_weight,
        down_weight,
        reps,
    )
    mixed_far = far(mixed, group)
    up_got = swap(up_sent, "grp", group, 0)
    mix_got = swap(mix_sent, "grp", group, 0)
    down_got = swap(after(down_sent, up_got, mix_got), "grp", group, 0)
    bits = list(range(reps.bit_length() - 1))
    up = Reduction(bits, reps, rep, [(up_keep, up_got), (mix_keep, mix_got), (small,)])
    up.exchange()
    down = Reduction(
        bits[1:2] + bits[:1] + bits[2:], reps, rep, [(after(down_keep, *up.send), down_got)]
    )
    down.exchange()
    mixed_near = spread(after(mixed, *down.send), group)
    sel = jnp.concatenate([core, (rep & 1).reshape(1)])
    partial, attn_sent, bias_sums = first_pairs(
        sel, qkv, ctx, after(dctx, *up.send, *down.send), probs, normed, attn_weight, reps
    )
    attn_got = swap(attn_sent, "grp", group, 0)
    mixed_parts = mixed_near + spread(after(mixed_far, partial), group)
    top = top_bit(group)
    down.wait(partial, *mixed_near[1:])
    down.rows(top, group, us=4)
    up.next(*down.send)
    tokens_grad, attn_keep, attn_next = last_pairs(
        sel,
        qkv,
        ctx,
        after(dctx, *up.send, *down.send),
        probs,
        normed,
        attn_weight,
        attn_got,
        bias_sums,
        vec,
        at,
        partial,
        x,
        gh,
        reps,
    )
    top = top_bit(group)
    home_far = far(tokens_grad, group)
    home_near = spread(tokens_grad, group)
    attn = Reduction(bits, reps, rep, halves=(attn_keep, attn_next))
    attn.exchange()
    up.wait(tokens_grad, mixed_parts[-1])
    up.next(us=4)
    down.next(*up.send)
    attn.next(*down.send, *home_near[1:])
    while down.bits:
        down.next(*attn.send)
    while up.bits:
        up.next(*down.send)
    up.wait(*down.send)
    up_sum = up.last()
    home_parts = home_near + spread(after(home_far, up_sum), group)
    mixed_home = collect(me, after(destination, up_sum), mixed_parts, us=4)
    attn.wait(up_sum)
    while attn.bits:
        attn.next()
    tokens_home = collect(me, after(destination, mixed_home, *attn.send), home_parts, us=4)
    up_sum = add(up_sum, after(swap(up_sum, "grp", group, top), tokens_home))
    for b in range(1, top):
        up_sum = add(up_sum, swap(up_sum, "grp", group, b))
    down.wait(tokens_home)
    down_sum = down.last()
    down_far = after(swap(down_sum, "grp", group, top), tokens_home, up_sum)
    high_row = (me[0] >> top) & 1
    down_rows = [down_sum, down_far]
    for b in range(1, top):
        down_rows = [add(d, swap(d, "grp", group, b)) for d in down_rows]
    early = jnp.concatenate(
        [jnp.where(high_row == j, down_rows[1], down_rows[0]) for j in (1, 0)] + [up_sum]
    )
    early_halves = both_cores(early, group)
    attn_sum = attn.last()

    def ordered(halves):
        own, other = (h.astype(F32) * scale for h in halves)
        return jnp.where(core[0] == 0, own, other), jnp.where(core[0] == 0, other, own)

    low, high = ordered([h[:ffs] for h in early_halves])
    g_down = jnp.concatenate([low, high], axis=1)
    low, high = ordered([h[ffs:] for h in early_halves])
    n_up = ff // 2 // CW
    cut = lambda h, j: h[j * size : (j + 1) * size]
    g_up = jnp.concatenate([cut(h, j) for h in (low, high) for j in range(n_up)], axis=1)
    g_mix = jnp.concatenate([cut(low, n_up), cut(high, n_up)], axis=1)
    tail = (low + high)[(n_up + 1) * size :]
    g_up_bias = take_small(tail[0], ff, reps, rep)
    g_down_bias, g_gain_two, g_bias_two, g_mix_bias = (
        take_small(tail[j], width, reps, rep) for j in range(1, 5)
    )
    attn_sum = after(
        across(attn_sum, group),
        tokens_home,
        g_down,
        g_up,
        g_mix,
        g_up_bias,
        g_down_bias,
        g_gain_two,
        g_bias_two,
        g_mix_bias,
    )
    low, high = ordered(both_cores(attn_sum, group))
    n_pair = width // LANES // 2
    pieces = [cut(h, j) for j in range(n_pair) for h in (low, high)]
    g_attn = jnp.concatenate(
        [p[:, i * LANES : (i + 1) * LANES] for i in range(3) for p in pieces], axis=1
    )
    tail = (low + high)[n_pair * size :]
    g_gain_one = take_small(tail[0], width, reps, rep)
    g_bias_one = take_small(tail[1], width, reps, rep)
    g_attn_bias = take_small(tail[2], 2 * width, reps, rep)
    return (
        mixed_home,
        tokens_home,
        g_gain_one,
        g_bias_one,
        g_attn,
        g_attn_bias,
        g_mix,
        g_mix_bias,
        g_gain_two,
        g_bias_two,
        g_up,
        g_up_bias,
        g_down,
        g_down_bias,
    )


def solution(mesh):
    tokens = P(("grp", "rep"), None)
    blocks = P(("grp", "rep"))
    return jax.shard_map(
        per_device,
        mesh=mesh,
        in_specs=(tokens, tokens, blocks, blocks, blocks) + (P(),) * 12,
        out_specs=(
            tokens,
            tokens,
            P("rep"),
            P("rep"),
            P("rep", None),
            P("rep"),
            P("rep", None),
            P("rep"),
            P("rep"),
            P("rep"),
            P("rep", None),
            P("rep"),
            P("rep", None),
            P("rep"),
        ),
        check_vma=False,
    )
```

```python
import functools

import jax
import jax.numpy as jnp
from jax import lax
from jax.experimental import pallas as pl
from jax.experimental.pallas import tpu as pltpu
from jax.sharding import PartitionSpec as P

F32 = jnp.float32
BF = jnp.bfloat16
HEAD_DIM = 64
NB = 8
BL = 128
LANES = 128
CW = 384
EXTRA = 16
DOWN_STEPS = 4
EPSILON = 1e-05
C0 = 0.7978845608028654
C1 = 0.044715
NEG = -1e30
VMEM = 63 * 2**20
NT = (((1,), (1,)), ((), ()))
TN = (((0,), (0,)), ((), ()))


def dot(a, b):
    return jnp.dot(a, b, preferred_element_type=F32)


def dot_nt(a, b):
    return lax.dot_general(a, b, NT, preferred_element_type=F32)


def dot_tn(a, b):
    return lax.dot_general(a, b, TN, preferred_element_type=F32)


def normalise(rows):
    width = rows.shape[1]
    centered = rows - jnp.sum(rows, axis=1, keepdims=True) * (1.0 / width)
    rstd = lax.rsqrt(
        jnp.sum(centered * centered, axis=1, keepdims=True) * (1.0 / width) + EPSILON
    )
    return centered * rstd, rstd


def norm_back(grad, gain, xhat, rstd):
    width = grad.shape[1]
    dx = grad * gain
    mean_one = jnp.sum(dx, axis=1, keepdims=True) * (1.0 / width)
    mean_two = jnp.sum(dx * xhat, axis=1, keepdims=True) * (1.0 / width)
    return rstd * (dx - mean_one - xhat * mean_two)


def colsum(rows):
    return jnp.sum(rows, axis=0, keepdims=True)


def params(mib=None):
    return pltpu.CompilerParams(vmem_limit_bytes=mib * 2**20 if mib else VMEM)


def cost(us):
    return pl.CostEstimate(flops=int(us * 2e10), bytes_accessed=int(us * 1e6), transcendentals=0)


def whole(array):
    return pl.BlockSpec(
        array.shape, lambda *_: (0,) * array.ndim, pipeline_mode=pl.Buffered(buffer_count=1)
    )


def swap(value, axis, size, bit):
    return lax.ppermute(value, axis, [(i, i ^ (1 << bit)) for i in range(size)])


def top_bit(size):
    return size.bit_length() - 2


def spread(value, size):
    found = [value]
    for bit in range(top_bit(size)):
        found = found + [swap(v, "grp", size, bit) for v in found]
    return found


def far(value, size):
    return swap(value, "grp", size, top_bit(size))


def share(value, size):
    return spread(value, size) + spread(far(value, size), size)


def after(value, *earlier):
    return lax.optimization_barrier((value,) + earlier)[0]


def start_gather(me, tables, sources, target, sems):
    for table, source in zip(tables, sources):
        for b in range(NB):
            slot = table[b] - me[0] * NB

            @pl.when((slot >= 0) & (slot < NB))
            def _(b=b, source=source, slot=slot):
                begin = pl.multiple_of(slot * BL, BL)
                pltpu.make_async_copy(
                    source.at[pl.ds(b * BL, BL)], target.at[pl.ds(begin, BL)], sems.at[slot]
                ).start()


def wait_gather(c, sources, target, sems):
    pltpu.make_async_copy(
        sources[0].at[pl.ds(0, BL)], target.at[pl.ds(c * BL, BL)], sems.at[c]
    ).wait()


def collect_kernel(me, destination, *refs, n):
    sources, out, sems = refs[:n], refs[n], refs[n + 1]
    for b in range(NB):
        peer = lax.div(destination[b], NB) ^ me[0]
        begin = pl.multiple_of(lax.rem(destination[b], NB) * BL, BL)
        for k, source in enumerate(sources):

            @pl.when(peer == k)
            def _(b=b, source=source, begin=begin):
                pltpu.make_async_copy(
                    source.at[pl.ds(begin, BL)], out.at[pl.ds(b * BL, BL)], sems.at[b]
                ).start()

    for b in range(NB):
        wait_gather(b, sources, out, sems)


def collect(me, destination, sources, us=0.001):
    n = len(sources)
    rows, width = sources[0].shape
    return pl.pallas_call(
        functools.partial(collect_kernel, n=n),
        grid_spec=pltpu.PrefetchScalarGridSpec(
            num_scalar_prefetch=2,
            grid=(1,),
            in_specs=[pl.BlockSpec(memory_space=pl.ANY)] * n,
            out_specs=pl.BlockSpec((rows, width), lambda i, *_: (0, 0)),
            scratch_shapes=[pltpu.SemaphoreType.DMA((NB,))],
        ),
        out_shape=jax.ShapeDtypeStruct((rows, width), sources[0].dtype),
        compiler_params=params(),
        cost_estimate=cost(us),
        name="collect",
    )(me, destination, *sources)


def project_kernel(me, *refs, n, tile, at):
    tables, sources, refs = refs[:n], refs[n : 2 * n], refs[2 * n :]
    vec, weight, x_out, normed_out, qkv_out, x_buf, sems = refs
    step = pl.program_id(0)
    per = tile // BL

    @pl.when(step == 0)
    def _():
        start_gather(me, tables, sources, x_buf, sems)

    for c in range(NB):

        @pl.when(step == c // per)
        def _(c=c):
            wait_gather(c, sources, x_buf, sems)

    x = x_buf[pl.ds(pl.multiple_of(step * tile, tile), tile), :]
    x_out[...] = x
    xhat, _ = normalise(x.astype(F32))
    width = x.shape[1]
    line = lambda name: vec[at[name] : at[name] + 1, :width]
    normed = xhat * line("first_gain") + line("first_bias")
    normed_out[...] = normed.T.astype(BF)
    normed = normed.astype(BF)
    for i, name in enumerate(("query_bias", None, "value_bias")):
        cols = slice(i * width, (i + 1) * width)
        part = dot(normed, weight[:, cols])
        qkv_out[:, cols] = (part + line(name) if name else part).astype(BF)


def project(me, tables, sources, vec, at, weight, tile=256):
    n = len(sources)
    rows, width = sources[0].shape
    row = lambda w: pl.BlockSpec((tile, w), lambda i, *_: (i, 0))
    return pl.pallas_call(
        functools.partial(project_kernel, n=n, tile=tile, at=at),
        grid_spec=pltpu.PrefetchScalarGridSpec(
            num_scalar_prefetch=1 + n,
            grid=(rows // tile,),
            in_specs=[pl.BlockSpec(memory_space=pl.ANY)] * n + [whole(vec), whole(weight)],
            out_specs=[
                row(width),
                pl.BlockSpec((width, tile), lambda i, *_: (0, i)),
                row(3 * width),
            ],
            scratch_shapes=[pltpu.VMEM((rows, width), BF), pltpu.SemaphoreType.DMA((NB,))],
        ),
        out_shape=[
            jax.ShapeDtypeStruct((rows, width), BF),
            jax.ShapeDtypeStruct((width, rows), BF),
            jax.ShapeDtypeStruct((rows, 3 * width), BF),
        ],
        compiler_params=params(59),
        cost_estimate=cost(0.001),
        name="project",
    )(me, *tables, *sources, vec, weight)


def head_masks(rows):
    lane = lax.broadcasted_iota(jnp.int32, (rows, LANES), 1)
    return [lane < HEAD_DIM, lane >= HEAD_DIM]


def attention_kernel(first, count, q_ref, k_ref, v_ref, ctx_ref, p_ref, *, rows, tile):
    q = q_ref[...]
    k = k_ref[...]
    v = v_ref[...]
    masks = head_masks(rows)
    zero = jnp.zeros((), BF)
    scale = jnp.asarray(HEAD_DIM**-0.5, BF)
    key_pos = lax.broadcasted_iota(jnp.int32, (BL, BL), 1)
    causal = key_pos <= lax.broadcasted_iota(jnp.int32, (BL, BL), 0)
    value_mean = colsum(v.astype(F32)) * (1.0 / rows)
    queries = [jnp.where(m, q, zero) * scale for m in masks]
    values = [jnp.where(m, v, zero) for m in masks]
    for i in range(rows // tile):
        keys = k[: (i + 1) * tile]
        scores = [dot_nt(query[i * tile : (i + 1) * tile], keys) for query in queries]
        for c in range(i * tile // BL, (i + 1) * tile // BL):
            begin = c * BL - i * tile
            allowed = causal & (key_pos < count[c])
            total = None
            for h in range(2):
                strip = scores[h][begin : begin + BL]
                parts = []
                for j in range(c):
                    other = jnp.where(j >= first[c], jnp.float32(0), jnp.float32(NEG))
                    parts.append(strip[:, j * BL : (j + 1) * BL] + other)
                parts.append(jnp.where(allowed, strip[:, c * BL : (c + 1) * BL], NEG))
                top = functools.reduce(jnp.maximum, parts)
                top = jnp.max(top, axis=1, keepdims=True)
                parts = [jnp.exp(part - top) for part in parts]
                inverse = 1.0 / jnp.sum(
                    functools.reduce(jnp.add, parts), axis=1, keepdims=True
                )
                parts = [(part * inverse).astype(BF) for part in parts]
                for j, part in enumerate(parts):
                    p_ref[h, c * BL : (c + 1) * BL, j * BL : (j + 1) * BL] = part
                probs = jnp.concatenate(parts, axis=1) if c else parts[0]
                out = dot(probs, values[h][: (c + 1) * BL])
                total = out if total is None else total + out
            total = jnp.where(count[c] == 0, jnp.broadcast_to(value_mean, total.shape), total)
            ctx_ref[c * BL : (c + 1) * BL, :] = total.astype(BF)


def attention(first, count, qkv, tile=512):
    rows = qkv.shape[0]
    width = qkv.shape[1] // 3
    pairs = width // LANES
    col = lambda off: pl.BlockSpec((rows, LANES), lambda i, *_: (0, i + off))
    return pl.pallas_call(
        functools.partial(attention_kernel, rows=rows, tile=tile),
        grid_spec=pltpu.PrefetchScalarGridSpec(
            num_scalar_prefetch=2,
            grid=(pairs,),
            in_specs=[col(0), col(pairs), col(2 * pairs)],
            out_specs=[col(0), pl.BlockSpec((2, rows, rows), lambda i, *_: (i, 0, 0))],
        ),
        out_shape=[
            jax.ShapeDtypeStruct((rows, width), BF),
            jax.ShapeDtypeStruct((2 * pairs, rows, rows), BF),
        ],
        compiler_params=params(),
        cost_estimate=cost(0.001),
        name="attention",
    )(first, count, qkv, qkv, qkv)


def split_by(bit, value, keep_ref, send_ref, where):
    for i in range(value.shape[0] // 2):
        even, odd = value[2 * i], value[2 * i + 1]
        keep_ref[(i,) + where] = jnp.where(bit == 0, even, odd).astype(BF)
        send_ref[(i,) + where] = jnp.where(bit == 0, odd, even).astype(BF)


def window(total, share_size, r):
    return min(r * share_size // LANES * LANES, max(total - 2 * LANES, 0))


def small_shares(vectors, parts, rows=EXTRA):
    lines = []
    for v in vectors:
        w = v.shape[1]
        size = w // parts
        if size % LANES == 0:
            pieces = [v[:, r * size : (r + 1) * size] for r in range(parts)]
        else:
            pieces = [v[:, window(w, size, r) :][:, : 2 * LANES] for r in range(parts)]
        lines.append([jnp.pad(p, ((0, 0), (0, CW - p.shape[1]))) for p in pieces])
    blank = jnp.zeros((rows - len(lines), CW), F32)
    return [jnp.concatenate([line[r] for line in lines] + [blank], axis=0) for r in range(parts)]


def take_small(line, total, parts, rep):
    size = total // parts
    if size % LANES == 0:
        return line[:size]
    begin = jnp.minimum(rep * size // LANES * LANES, max(total - 2 * LANES, 0))
    return lax.dynamic_slice(line, (rep * size - begin,), (size,))


def feed_kernel(me, count, core, *refs, n, tile, ftile, at, parts):
    tables, sources, refs = refs[:n], refs[n : 2 * n], refs[2 * n :]
    x_ref, ctx_ref, ctx_all, vec, mixw, upw, downw = refs[:7]
    (
        mixed_ref,
        gh_ref,
        dctx_ref,
        down_sent,
        down_keep,
        up_sent,
        up_keep,
        mix_sent,
        mix_keep,
        small_ref,
        og_buf,
        act_buf,
        gu_buf,
        second_buf,
        pre_buf,
        sums,
        sems,
    ) = refs[7:]
    step = pl.program_id(0)
    per = tile // BL
    rows, width = og_buf.shape
    ff = upw.shape[1]
    tiles = rows // tile
    size = width // parts
    up_steps = ff // (2 * CW)
    line = lambda name, w: vec[at[name] : at[name] + 1, :w]

    @pl.when(step == 0)
    def _():
        start_gather(me, tables, sources, og_buf, sems)
        sums[...] = jnp.zeros_like(sums)

    for c in range(NB):

        @pl.when(step == c // per)
        def _(c=c):
            wait_gather(c, sources, og_buf, sems)

    @pl.when(step < tiles)
    def _():
        begin = pl.multiple_of(step * tile, tile)
        own = pl.ds(begin, tile)
        row = lax.broadcasted_iota(jnp.int32, (tile, 1), 0)
        live = jnp.zeros((tile, 1), F32)
        for b in range(per):
            filled = count[step * per + b]
            live = jnp.where((row >= b * BL) & (row < b * BL + filled), 1.0, live)
        branch = ((dot(ctx_ref[...], mixw[...]) + line("mix_bias", width)) * live).astype(BF)
        hidden = x_ref[...].astype(F32) + branch.astype(F32)
        xhat, rstd = normalise(hidden)
        second = xhat * line("second_gain", width) + line("second_bias", width)
        second_buf[:, own] = second.T.astype(BF)
        second = second.astype(BF)
        mixed = hidden + line("down_bias", width)
        og = og_buf[own, :]
        gs = jnp.zeros((tile, width), F32)
        for f in range(ff // ftile):
            cols = slice(f * ftile, (f + 1) * ftile)
            v = dot(second, upw[:, cols]) + vec[at["up_bias"] : at["up_bias"] + 1, cols]
            da = dot_nt(og, downw[cols, :])
            square = v * v
            half = 0.5 + 0.5 * jnp.tanh(v * (C0 + (C0 * C1) * square))
            act = (v * half).astype(BF)
            act_buf[own, cols] = act
            mixed = mixed + dot(act, downw[cols, :])
            slope = half + v * (half - half * half) * (2 * C0 + (6 * C0 * C1) * square)
            gu = (da * slope).astype(BF)
            gu_buf[own, cols] = gu
            sums[0:1, cols] += colsum(gu.astype(F32))
            gs = gs + dot_nt(gu, upw[:, cols])
        mixed_ref[...] = mixed.astype(BF)
        og = og.astype(F32)
        gh = og + norm_back(gs, line("second_gain", width), xhat, rstd)
        gh_ref[...] = gh
        pre = gh.astype(BF).astype(F32) * live
        sums[1:2, :width] += colsum(og)
        sums[2:3, :width] += colsum(gs * xhat)
        sums[3:4, :width] += colsum(gs)
        sums[4:5, :width] += colsum(pre)
        pre = pre.astype(BF)
        pre_buf[own, :] = pre
        dctx_ref[...] = dot_nt(pre, mixw[...]).astype(BF)

    @pl.when((step >= tiles) & (step < tiles + up_steps))
    def _():
        s = step - tiles
        half_steps = up_steps // 2
        turn = jnp.where(s < half_steps, 1 - core[0], core[0])
        block = turn * half_steps + lax.rem(s, half_steps)
        cols = pl.ds(pl.multiple_of(block * 2 * CW, 2 * CW), 2 * CW)
        product = dot(second_buf[...], gu_buf[:, cols])
        pieces = [product[:, j * CW : (j + 1) * CW].reshape(parts, size, CW) for j in range(2)]
        pieces = [p.astype(BF) for p in pieces]

        @pl.when(s < half_steps)
        def _():
            for j in range(2):
                up_sent[:, j * size : (j + 1) * size, :] = pieces[j]

        @pl.when(s >= half_steps)
        def _():
            for j in range(2):
                up_keep[:, j * size : (j + 1) * size, :] = pieces[j]

    @pl.when(step == tiles + up_steps)
    def _():
        product = dot_tn(ctx_all[...], pre_buf[...])
        low = product[:, :CW].reshape(mix_keep.shape)
        high = product[:, CW:].reshape(mix_keep.shape)
        mix_keep[...] = jnp.where(core[0] == 0, low, high).astype(BF)
        mix_sent[...] = jnp.where(core[0] == 0, high, low).astype(BF)
        vectors = [sums[0:1, :]] + [sums[j : j + 1, :width] for j in range(1, 5)]
        for r, value in enumerate(small_shares(vectors, parts, small_ref.shape[1])):
            small_ref[r] = value.astype(BF)

    @pl.when(step > tiles + up_steps)
    def _():
        block = ff // DOWN_STEPS
        begin = pl.multiple_of((step - tiles - up_steps - 1) * block, block)
        product = dot_tn(act_buf[:, pl.ds(begin, block)], og_buf[...])
        low = product[:, :CW].reshape(down_keep.shape)
        high = product[:, CW:].reshape(down_keep.shape)
        down_keep[...] = jnp.where(core[0] == 0, low, high).astype(BF)
        down_sent[...] = jnp.where(core[0] == 0, high, low).astype(BF)


def feed(me, tables, count, core, sources, x, ctx, vec, at, mixw, upw, downw, parts):
    tile, ftile = 256, 512
    n = len(sources)
    rows, width = x.shape
    ff = upw.shape[1]
    tiles = rows // tile
    size = width // parts
    up_steps = ff // (2 * CW)
    half = up_steps // 2
    extra = EXTRA
    now = lambda i: jnp.minimum(i, tiles - 1)
    row = lambda w: pl.BlockSpec((tile, w), lambda i, *_: (now(i), 0))
    up_block = lambda begin: pl.BlockSpec(
        (parts, 2 * size, CW), lambda i, *_: (0, jnp.clip(i - tiles - begin, 0, half - 1), 0)
    )
    down_block = pl.BlockSpec(
        (parts // DOWN_STEPS, ff // parts, CW),
        lambda i, *_: (jnp.maximum(i - tiles - up_steps - 1, 0), 0, 0),
    )
    bf = lambda *shape: jax.ShapeDtypeStruct(shape, BF)
    once = lambda *shape: pl.BlockSpec(shape, lambda i, *_: (0,) * len(shape))
    up_rows = ff // 2 // CW * size
    return pl.pallas_call(
        functools.partial(feed_kernel, n=n, tile=tile, ftile=ftile, at=at, parts=parts),
        grid_spec=pltpu.PrefetchScalarGridSpec(
            num_scalar_prefetch=3 + n,
            grid=(tiles + up_steps + 1 + DOWN_STEPS,),
            in_specs=[pl.BlockSpec(memory_space=pl.ANY)] * n
            + [row(width), row(width)]
            + [whole(a) for a in (ctx, vec, mixw, upw, downw)],
            out_specs=[
                row(width),
                row(width),
                row(width),
                down_block,
                down_block,
                up_block(0),
                up_block(half),
                once(parts, size, CW),
                once(parts, size, CW),
                once(parts, extra, CW),
            ],
            scratch_shapes=[
                pltpu.VMEM((rows, width), BF),
                pltpu.VMEM((rows, ff), BF),
                pltpu.VMEM((rows, ff), BF),
                pltpu.VMEM((width, rows), BF),
                pltpu.VMEM((rows, width), BF),
                pltpu.VMEM((8, ff), F32),
                pltpu.SemaphoreType.DMA((NB,)),
            ],
        ),
        out_shape=[
            bf(rows, width),
            jax.ShapeDtypeStruct((rows, width), F32),
            bf(rows, width),
            bf(parts, ff // parts, CW),
            bf(parts, ff // parts, CW),
            bf(parts, up_rows, CW),
            bf(parts, up_rows, CW),
            bf(parts, size, CW),
            bf(parts, size, CW),
            bf(parts, extra, CW),
        ],
        compiler_params=params(),
        cost_estimate=cost(50),
        name="feed",
    )(me, count, core, *tables, *sources, x, ctx, ctx, vec, mixw, upw, downw)


def pair_back(q_ref, k_ref, v_ref, o_ref, g_ref, p_ref, ds_ref, out_ref, rows, tile):
    q = q_ref[...]
    k = k_ref[...]
    v = v_ref[...]
    grad = g_ref[...]
    masks = head_masks(rows)
    zero = jnp.zeros((), BF)
    scale = jnp.asarray(HEAD_DIM**-0.5, BF)
    product = grad.astype(F32) * o_ref[...].astype(F32)
    grads = [jnp.where(m, grad, zero) for m in masks]
    keys = [jnp.where(m, k, zero) * scale for m in masks]
    queries = [jnp.where(m, q, zero) * scale for m in masks]
    inner = [jnp.sum(jnp.where(m, product, 0.0), axis=1, keepdims=True) for m in masks]
    for i in range(rows // tile):
        cut = slice(i * tile, (i + 1) * tile)
        dprobs = [dot_nt(g[cut], v[: (i + 1) * tile]) for g in grads]
        for c in range(i * tile // BL, (i + 1) * tile // BL):
            begin = c * BL - i * tile
            own = slice(c * BL, (c + 1) * BL)
            width = (c + 1) * BL
            total = None
            for h in range(2):
                probs = p_ref[h, own, :width].astype(F32)
                ds = (probs * (dprobs[h][begin : begin + BL, :width] - inner[h][own])).astype(BF)
                ds_ref[h, own, :width] = ds
                out = dot(ds, keys[h][:width])
                total = out if total is None else total + out
            out_ref[own, :LANES] = total.astype(BF)
    for c in range(rows // BL):
        own = slice(c * BL, (c + 1) * BL)
        dk = dv = None
        for h in range(2):
            one = dot_tn(ds_ref[h, c * BL :, own], queries[h][c * BL :])
            two = dot_tn(p_ref[h, c * BL :, own], grads[h][c * BL :])
            dk = one if dk is None else dk + one
            dv = two if dv is None else dv + two
        out_ref[own, LANES : 2 * LANES] = dk.astype(BF)
        out_ref[own, 2 * LANES :] = dv.astype(BF)


def first_pairs_kernel(core, *refs, rows, tile, parts):
    ins = refs[:6]
    normed_in, wq, wk, wv, grad_ref, sent_ref, bias_ref, ds_ref, out_ref, normed, sem = refs[6:]
    step = pl.program_id(0)
    copy = pltpu.make_async_copy(normed_in, normed, sem)

    @pl.when(step == 0)
    def _():
        copy.start()

    pair_back(*ins, ds_ref, out_ref, rows, tile)

    @pl.when(step == 0)
    def _():
        copy.wait()

    out = out_ref[...]
    sent_ref[...] = dot(normed[...], out).reshape(sent_ref.shape).astype(BF)
    weight = jnp.concatenate([wq[...], wk[...], wv[...]], axis=1)
    grad = dot_nt(out, weight)

    @pl.when(step == 0)
    def _():
        grad_ref[...] = grad

    @pl.when(step > 0)
    def _():
        grad_ref[...] += grad

    sums = colsum(out.astype(F32))
    bias_ref[0:1, :] = sums[:, :LANES]
    bias_ref[1:2, :] = sums[:, 2 * LANES :]


def last_pairs_kernel(sel, *refs, rows, tile, parts, at):
    ins = refs[:6]
    (
        normed_in,
        wq,
        wk,
        wv,
        got,
        bias_in,
        vec,
        grad_in,
        x_in,
        gh_in,
        tg_ref,
        keep_ref,
        send_ref,
        ds_ref,
        out_ref,
        grad,
        x_buf,
        gh_buf,
        bias,
        normed,
        sems,
    ) = refs[6:]
    step = pl.program_id(0)
    steps = pl.num_programs(0)
    width = x_buf.shape[1]
    size = width // parts
    last = width // LANES // 2 * size
    copies = [
        pltpu.make_async_copy(a, b, sems.at[i])
        for i, (a, b) in enumerate(
            ((normed_in, normed), (grad_in, grad), (x_in, x_buf), (gh_in, gh_buf))
        )
    ]

    @pl.when(step == 0)
    def _():
        for copy in copies:
            copy.start()
        bias[...] = bias_in[...]

    pair_back(*ins, ds_ref, out_ref, rows, tile)

    @pl.when(step == 0)
    def _():
        copies[0].wait()
        copies[1].wait()

    out = out_ref[...]
    value = dot(normed[...], out).reshape(got.shape) + got[...].astype(F32)
    where = (pl.ds(pl.multiple_of(step * size, 8), size), slice(None))
    split_by(sel[1], value, keep_ref, send_ref, where)
    weight = jnp.concatenate([wq[...], wk[...], wv[...]], axis=1)
    grad[...] += dot_nt(out, weight)
    sums = colsum(out.astype(F32))
    lanes = pl.ds(pl.multiple_of((2 * step + sel[0]) * LANES, LANES), LANES)
    bias[0:1, lanes] = sums[:, :LANES]
    bias[1:2, lanes] = sums[:, 2 * LANES :]

    @pl.when(step == steps - 1)
    def _():
        copies[2].wait()
        copies[3].wait()
        gain = vec[at["first_gain"] : at["first_gain"] + 1, :width]
        gain_sum = jnp.zeros((1, width), F32)
        bias_sum = jnp.zeros((1, width), F32)
        block = 256
        for i in range(rows // block):
            cut = slice(i * block, (i + 1) * block)
            xhat, rstd = normalise(x_buf[cut, :].astype(F32))
            g = grad[cut, :]
            back = norm_back(g, gain, xhat, rstd).astype(BF).astype(F32)
            tg_ref[cut, :] = (gh_buf[cut, :] + back).astype(BF)
            gain_sum += colsum(g * xhat)
            bias_sum += colsum(g)
        both = jnp.concatenate([bias[0:1, :], bias[1:2, :]], axis=1)
        shares = jnp.stack(small_shares([gain_sum, bias_sum, both], parts))
        where = (slice(last, last + EXTRA), slice(None))
        split_by(sel[1], shares, keep_ref, send_ref, where)


def pairs_specs(rows, width, side):
    pairs = width // LANES
    pair = lambda i, sel: 2 * i + side(sel)
    col = lambda off, h=rows: pl.BlockSpec((h, LANES), lambda i, sel: (0, pair(i, sel) + off))
    return [
        col(0),
        col(pairs),
        col(2 * pairs),
        col(0),
        col(0),
        pl.BlockSpec((2, rows, rows), lambda i, sel: (pair(i, sel), 0, 0)),
        pl.BlockSpec(memory_space=pl.ANY),
        col(0, width),
        col(pairs, width),
        col(2 * pairs, width),
    ]


def first_pairs(sel, qkv, ctx, grad, probs, normed, weight, parts, tile=512):
    rows = qkv.shape[0]
    width = qkv.shape[1] // 3
    half = width // LANES // 2
    size = width // parts
    return pl.pallas_call(
        functools.partial(first_pairs_kernel, rows=rows, tile=tile, parts=parts),
        grid_spec=pltpu.PrefetchScalarGridSpec(
            num_scalar_prefetch=1,
            grid=(half,),
            in_specs=pairs_specs(rows, width, lambda sel: 1 - sel[0]),
            out_specs=[
                pl.BlockSpec((rows, width), lambda i, sel: (0, 0)),
                pl.BlockSpec((parts, size, CW), lambda i, sel: (0, i, 0)),
                pl.BlockSpec((8, LANES), lambda i, sel: (0, 2 * i + 1 - sel[0])),
            ],
            scratch_shapes=[
                pltpu.VMEM((2, rows, rows), BF),
                pltpu.VMEM((rows, 3 * LANES), BF),
                pltpu.VMEM((width, rows), BF),
                pltpu.SemaphoreType.DMA,
            ],
        ),
        out_shape=[
            jax.ShapeDtypeStruct((rows, width), F32),
            jax.ShapeDtypeStruct((parts, half * size, CW), BF),
            jax.ShapeDtypeStruct((8, width), F32),
        ],
        compiler_params=params(),
        cost_estimate=cost(20),
        name="first_pairs",
    )(sel, qkv, qkv, qkv, ctx, grad, probs, normed, weight, weight, weight)


def last_pairs(
    sel, qkv, ctx, grad, probs, normed, weight, got, bias, vec, at, partial, x, gh, parts, tile=512
):
    rows = qkv.shape[0]
    width = qkv.shape[1] // 3
    half = width // LANES // 2
    size = width // parts
    total = half * size + EXTRA
    anywhere = pl.BlockSpec(memory_space=pl.ANY)
    share_out = pl.BlockSpec((parts // 2, total, CW), lambda i, sel: (0, 0, 0))
    return pl.pallas_call(
        functools.partial(last_pairs_kernel, rows=rows, tile=tile, parts=parts, at=at),
        grid_spec=pltpu.PrefetchScalarGridSpec(
            num_scalar_prefetch=1,
            grid=(half,),
            in_specs=pairs_specs(rows, width, lambda sel: sel[0])
            + [
                pl.BlockSpec((parts, size, CW), lambda i, sel: (0, i, 0)),
                whole(bias),
                whole(vec),
                anywhere,
                anywhere,
                anywhere,
            ],
            out_specs=[
                pl.BlockSpec((rows, width), lambda i, sel: (0, 0)),
                share_out,
                share_out,
            ],
            scratch_shapes=[
                pltpu.VMEM((2, rows, rows), BF),
                pltpu.VMEM((rows, 3 * LANES), BF),
                pltpu.VMEM((rows, width), F32),
                pltpu.VMEM((rows, width), BF),
                pltpu.VMEM((rows, width), F32),
                pltpu.VMEM((8, width), F32),
                pltpu.VMEM((width, rows), BF),
                pltpu.SemaphoreType.DMA((4,)),
            ],
        ),
        out_shape=[
            jax.ShapeDtypeStruct((rows, width), BF),
            jax.ShapeDtypeStruct((parts // 2, total, CW), BF),
            jax.ShapeDtypeStruct((parts // 2, total, CW), BF),
        ],
        compiler_params=params(),
        cost_estimate=cost(20),
        name="last_pairs",
    )(
        sel, qkv, qkv, qkv, ctx, grad, probs, normed, weight, weight, weight, got, bias, vec, partial, x, gh
    )


def halve_kernel(bit, *refs, counts, cuts):
    outs = refs[-2 * len(cuts) :]
    begin = 0
    given = iter(refs[: -2 * len(cuts)])
    for number in counts:
        pairs = [(next(given), next(given)) for _ in range(number)]
        low, high = (
            functools.reduce(jnp.add, [pair[j][0].astype(F32) for pair in pairs]) for j in range(2)
        )
        keep = jnp.where(bit[0] == 0, low, high).astype(BF)
        send = jnp.where(bit[0] == 0, high, low).astype(BF)
        first = 0
        for j, rows in enumerate(cuts):
            lo, hi = max(begin, first), min(begin + low.shape[0], first + rows)
            if lo < hi:
                outs[2 * j][0, lo - first : hi - first, :] = keep[lo - begin : hi - begin]
                outs[2 * j + 1][0, lo - first : hi - first, :] = send[lo - begin : hi - begin]
            first += rows
        begin += low.shape[0]


def halve(bit, k, groups, cuts=None, us=0.001):
    arrays = [a for group in groups for a in group]
    m, _, c = arrays[0].shape
    cuts = cuts or [sum(group[0].shape[1] for group in groups)]

    def entry(a, value):
        def index(i, bit):
            low = i & ((1 << k) - 1)
            return (((i >> k) << (k + 1)) + (value << k) + low, 0, 0)

        return pl.BlockSpec((1,) + a.shape[1:], index)

    cuts_twice = [n for n in cuts for _ in range(2)]
    outs = pl.pallas_call(
        functools.partial(halve_kernel, counts=[len(group) for group in groups], cuts=cuts),
        grid_spec=pltpu.PrefetchScalarGridSpec(
            num_scalar_prefetch=1,
            grid=(m // 2,),
            in_specs=[entry(a, value) for a in arrays for value in range(2)],
            out_specs=[pl.BlockSpec((1, n, c), lambda i, bit: (i, 0, 0)) for n in cuts_twice],
        ),
        out_shape=[jax.ShapeDtypeStruct((m // 2, n, c), BF) for n in cuts_twice],
        compiler_params=params(),
        cost_estimate=cost(us),
        name="halve",
    )(bit, *[a for a in arrays for _ in range(2)])
    return list(outs[::2]), list(outs[1::2])


def halve_rows_kernel(bit, one_ref, two_ref, keep_ref, send_ref):
    value = one_ref[0].astype(F32) + two_ref[0].astype(F32)
    half = value.shape[0] // 2
    low, high = value[:half], value[half:]
    keep_ref[0] = jnp.where(bit[0] == 0, low, high).astype(BF)
    send_ref[0] = jnp.where(bit[0] == 0, high, low).astype(BF)


def halve_rows(bit, one, two, us=0.001):
    m, n, c = one.shape
    block = lambda n: pl.BlockSpec((1, n, c), lambda i, bit: (i, 0, 0))
    return pl.pallas_call(
        halve_rows_kernel,
        grid_spec=pltpu.PrefetchScalarGridSpec(
            num_scalar_prefetch=1,
            grid=(m,),
            in_specs=[block(n), block(n)],
            out_specs=[block(n // 2), block(n // 2)],
        ),
        out_shape=[jax.ShapeDtypeStruct((m, n // 2, c), BF)] * 2,
        compiler_params=params(),
        cost_estimate=cost(us),
        name="halve_rows",
    )(bit, one, two)


def add(*arrays):
    return functools.reduce(jnp.add, [a.astype(F32) for a in arrays]).astype(BF)


class Reduction:
    def __init__(self, bits, reps, rep, groups=None, cuts=None, us=0.001, halves=None):
        self.reps, self.rep = reps, rep
        self.left = sorted(bits)
        self.bits = list(bits)
        self.cuts = cuts
        if halves is None:
            self.split(groups, us)
        else:
            self.bit = self.bits.pop(0)
            self.left.remove(self.bit)
            self.keep, self.send = [halves[0]], [halves[1]]

    def split(self, groups, us):
        self.bit = self.bits.pop(0)
        place = self.left.index(self.bit)
        self.left.remove(self.bit)
        mine = ((self.rep >> self.bit) & 1).astype(jnp.int32).reshape(1)
        self.keep, self.send = halve(mine, place, groups, self.cuts, us)

    def exchange(self):
        self.got = [swap(s, "rep", self.reps, self.bit) for s in self.send]

    def wait(self, *earlier):
        self.keep = [after(k, *earlier) for k in self.keep] if earlier else self.keep

    def next(self, *earlier, us=0.001):
        self.wait(*earlier)
        self.split(list(zip(self.keep, self.got)), us)
        self.exchange()

    def rows(self, bit, group, us=0.001):
        mine = ((lax.axis_index("grp") >> bit) & 1).astype(jnp.int32).reshape(1)
        keep, send = halve_rows(mine, self.keep[0], self.got[0], us)
        self.keep, self.send = [keep], [send]
        self.got = [swap(send, "grp", group, bit)]

    def last(self):
        return jnp.concatenate([add(k, g)[0] for k, g in zip(self.keep, self.got)])


def across(value, group):
    for b in range(1, group.bit_length() - 1):
        value = add(value, swap(value, "grp", group, b))
    return value


def both_cores(value, group):
    return value, swap(value, "grp", group, 0)


def per_device(
    tokens,
    out_grad,
    destination,
    seq_first,
    valid_count,
    first_gain,
    first_bias,
    attn_weight,
    attn_bias,
    mix_weight,
    mix_bias,
    second_gain,
    second_bias,
    up_weight,
    up_bias,
    down_weight,
    down_bias,
):
    rows, width = tokens.shape
    ff = up_weight.shape[1]
    group = lax.axis_size("grp")
    reps = lax.axis_size("rep")
    me = lax.axis_index("grp").astype(jnp.int32).reshape(1)
    rep = lax.axis_index("rep").astype(jnp.int32)
    core = me & 1
    size = width // reps
    ffs = ff // reps

    names = {
        "first_gain": first_gain,
        "first_bias": first_bias,
        "query_bias": attn_bias[:width],
        "value_bias": attn_bias[width:],
        "mix_bias": mix_bias,
        "second_gain": second_gain,
        "second_bias": second_bias,
        "up_bias": up_bias,
        "down_bias": down_bias,
    }
    at = {name: i for i, name in enumerate(names)}
    vec = jnp.stack([jnp.pad(v, (0, ff - v.shape[0])) for v in names.values()])

    tables = share(destination, group)
    count_far = far(valid_count, group)
    tokens_far = far(after(tokens, tables[group // 2], count_far), group)
    tokens_near = spread(tokens, group)
    grad_near = spread(after(out_grad, tables[group // 2]), group)
    total = jnp.sum(valid_count + count_far).reshape(1)
    for b in range(reps.bit_length() - 1):
        total = total + swap(total, "rep", reps, b)
    for b in range(top_bit(group)):
        total = total + swap(total, "grp", group, b)
    grad_far = far(after(jnp.pad(out_grad, ((0, EXTRA), (0, 0))), vec), group)
    token_parts = tokens_near + spread(
        after(tokens_far, vec, total, *tables, *tokens_near[1:], *grad_near[1:]), group
    )
    scale = 1.0 / total[0].astype(F32)
    x, normed, qkv = project(me, tables, token_parts, vec, at, attn_weight)
    ctx, probs = attention(seq_first, valid_count, qkv)
    grad_parts = grad_near + spread(after(grad_far, ctx), group)
    mixed, gh, dctx, down_sent, down_keep, up_sent, up_keep, mix_sent, mix_keep, small = feed(
        me,
        tables,
        valid_count,
        core,
        grad_parts,
        x,
        ctx,
        vec,
        at,
        mix_weight,
        up_weight,
        down_weight,
        reps,
    )
    mixed_far = far(mixed, group)
    up_got = swap(up_sent, "grp", group, 0)
    mix_got = swap(mix_sent, "grp", group, 0)
    down_got = swap(after(down_sent, up_got, mix_got), "grp", group, 0)
    bits = list(range(reps.bit_length() - 1))
    up = Reduction(bits, reps, rep, [(up_keep, up_got), (mix_keep, mix_got), (small,)])
    up.exchange()
    down = Reduction(
        bits[1:2] + bits[:1] + bits[2:], reps, rep, [(after(down_keep, *up.send), down_got)]
    )
    down.exchange()
    mixed_near = spread(after(mixed, *down.send), group)
    sel = jnp.concatenate([core, (rep & 1).reshape(1)])
    partial, attn_sent, bias_sums = first_pairs(
        sel, qkv, ctx, after(dctx, *up.send, *down.send), probs, normed, attn_weight, reps
    )
    attn_got = swap(attn_sent, "grp", group, 0)
    mixed_parts = mixed_near + spread(after(mixed_far, partial), group)
    top = top_bit(group)
    down.wait(partial, *mixed_near[1:])
    down.rows(top, group, us=4)
    up.next(*down.send)
    tokens_grad, attn_keep, attn_next = last_pairs(
        sel,
        qkv,
        ctx,
        after(dctx, *up.send, *down.send),
        probs,
        normed,
        attn_weight,
        attn_got,
        bias_sums,
        vec,
        at,
        partial,
        x,
        gh,
        reps,
    )
    top = top_bit(group)
    home_far = far(tokens_grad, group)
    home_near = spread(tokens_grad, group)
    attn = Reduction(bits, reps, rep, halves=(attn_keep, attn_next))
    attn.exchange()
    up.wait(tokens_grad, mixed_parts[-1])
    up.next(us=4)
    down.next(*up.send)
    attn.next(*down.send, *home_near[1:])
    while down.bits:
        down.next(*attn.send)
    while up.bits:
        up.next(*down.send)
    up.wait(*down.send)
    up_sum = up.last()
    home_parts = home_near + spread(after(home_far, up_sum), group)
    mixed_home = collect(me, after(destination, up_sum), mixed_parts, us=4)
    attn.wait(up_sum)
    while attn.bits:
        attn.next()
    tokens_home = collect(me, after(destination, mixed_home, *attn.send), home_parts, us=4)
    up_sum = add(up_sum, after(swap(up_sum, "grp", group, top), tokens_home))
    for b in range(1, top):
        up_sum = add(up_sum, swap(up_sum, "grp", group, b))
    down.wait(tokens_home)
    down_sum = down.last()
    down_far = after(swap(down_sum, "grp", group, top), tokens_home, up_sum)
    high_row = (me[0] >> top) & 1
    down_rows = [down_sum, down_far]
    for b in range(1, top):
        down_rows = [add(d, swap(d, "grp", group, b)) for d in down_rows]
    early = jnp.concatenate(
        [jnp.where(high_row == j, down_rows[1], down_rows[0]) for j in (1, 0)] + [up_sum]
    )
    early_halves = both_cores(early, group)
    attn_sum = attn.last()

    def ordered(halves):
        own, other = (h.astype(F32) * scale for h in halves)
        return jnp.where(core[0] == 0, own, other), jnp.where(core[0] == 0, other, own)

    low, high = ordered([h[:ffs] for h in early_halves])
    g_down = jnp.concatenate([low, high], axis=1)
    low, high = ordered([h[ffs:] for h in early_halves])
    n_up = ff // 2 // CW
    cut = lambda h, j: h[j * size : (j + 1) * size]
    g_up = jnp.concatenate([cut(h, j) for h in (low, high) for j in range(n_up)], axis=1)
    g_mix = jnp.concatenate([cut(low, n_up), cut(high, n_up)], axis=1)
    tail = (low + high)[(n_up + 1) * size :]
    g_up_bias = take_small(tail[0], ff, reps, rep)
    g_down_bias, g_gain_two, g_bias_two, g_mix_bias = (
        take_small(tail[j], width, reps, rep) for j in range(1, 5)
    )
    attn_sum = after(across(attn_sum, group), early_halves[1])
    low, high = ordered(both_cores(attn_sum, group))
    n_pair = width // LANES // 2
    pieces = [cut(h, j) for j in range(n_pair) for h in (low, high)]
    g_attn = jnp.concatenate(
        [p[:, i * LANES : (i + 1) * LANES] for i in range(3) for p in pieces], axis=1
    )
    tail = (low + high)[n_pair * size :]
    g_gain_one = take_small(tail[0], width, reps, rep)
    g_bias_one = take_small(tail[1], width, reps, rep)
    g_attn_bias = take_small(tail[2], 2 * width, reps, rep)
    return (
        mixed_home,
        tokens_home,
        g_gain_one,
        g_bias_one,
        g_attn,
        g_attn_bias,
        g_mix,
        g_mix_bias,
        g_gain_two,
        g_bias_two,
        g_up,
        g_up_bias,
        g_down,
        g_down_bias,
    )


def solution(mesh):
    tokens = P(("grp", "rep"), None)
    blocks = P(("grp", "rep"))
    return jax.shard_map(
        per_device,
        mesh=mesh,
        in_specs=(tokens, tokens, blocks, blocks, blocks) + (P(),) * 12,
        out_specs=(
            tokens,
            tokens,
            P("rep"),
            P("rep"),
            P("rep", None),
            P("rep"),
            P("rep", None),
            P("rep"),
            P("rep"),
            P("rep"),
            P("rep", None),
            P("rep"),
            P("rep", None),
            P("rep"),
        ),
        check_vma=False,
    )
```
